32 devices in a mesh: elem: 8 (over z, y), pts: 4 (over x, core).
Axes of the slice: x: 2, y: 2, z: 4, core: 2. Of those that a mesh axis runs over, the one named last changes fastest.
Arguments:
- basis: float32 [32, 2048, 256], P('elem', 'pts'), may hold values from -6 to 6
- applied: float32 [32, 2048, 256], P('elem', 'pts'), may hold values from -6 to 6
- quad: float32 [32, 2048], P('elem', 'pts'), may hold values from 0.00034526698 to 0.0013810679
- face_index: int32 [32, 4, 256], P('elem', None, 'pts'), may hold values from 0 to 511
- face_pairing: int32 [32, 256], P('elem', 'pts'), may hold values from 0 to 63, as said below
- orbitals: float32 [8192, 2048], P('elem', 'pts'), may hold values from -6 to 6
Outputs:
- filtered: float32 [8192, 2048], P('elem', 'pts')
The draws below stay inside these ranges and needn't reach their ends.
Inputs may be any that keep to these rules, and one draw needn't show every extreme that they name: `face_pairing`: each aligned block of 64 entries of a row is a permutation of 0 to 63.
All inputs are finite; a program needn't handle non-finite values.
Results may differ from the reference program's by a relative error of at most 0.0003.
Values sent between devices are 32-bit elements; how exact they have to be, the bound alone decides.
No kernel may reach another device: no remote copies, remote signals or barrier semaphores. Data moves between devices by JAX's collectives and lax.ppermute only.
A program may use at most 64 MiB of HBM per device.

```python
import math
import jax
import jax.numpy as jnp
from jax import lax

NB = 256
NORB = 2048
DEG = 4
PTS_DEV = 512
FACE_DEV = 64
NELEM = 32
NPTS = 2048
FACES = 256


def draw_face_pairing(key, part):
    blocks = FACES // FACE_DEV
    keys = jax.random.split(jax.random.fold_in(key, 7), NELEM * blocks)
    perms = jax.vmap(lambda single: jax.random.permutation(single, FACE_DEV))(keys)
    return perms.reshape(NELEM, FACES).astype(jnp.int32)


def set_ends(values, key, least, top_value):
    shape = values.shape
    index_at = [jax.random.randint(jax.random.fold_in(key, axis), (), 0, shape[axis]) for axis in range(len(shape))]
    values = values.at[tuple(index_at)].set(least)
    longest = shape.index(max(shape))
    index_at[longest] = (index_at[longest] + 1) % shape[longest]
    return values.at[tuple(index_at)].set(top_value)


def block_levels(own_key, shape, shards, least, largest):
    loudness, own = 1.0, jax.random.fold_in(own_key, 6)
    for axis_at, blocks in shards:
        draws = jnp.exp(jax.random.uniform(jax.random.fold_in(own, axis_at), (blocks,), jnp.float32, least / len(shards), largest / len(shards)))
        loudness = loudness * jnp.repeat(draws, shape[axis_at] // blocks).reshape([-1 if axis == axis_at else 1 for axis in range(len(shape))])
    return loudness


def gaussian(own_key, dims, width, reach, cuts=(), held_as=jnp.bfloat16):
    values = width * jax.random.normal(own_key, dims, jnp.float32)
    if cuts:
        values = values * block_levels(own_key, dims, cuts, -0.22, 0.18)
    return jnp.clip(values, -reach, reach).astype(held_as)


def setup_inputs(seed: int = 0) -> dict:
    arg_keys = jax.random.split(jax.random.key(seed), 7)
    basis = gaussian(arg_keys[0], (NELEM, NPTS, NB), 1.0, 6.0, ((0, 8), (1, 4)), jnp.float32)
    applied = gaussian(arg_keys[1], (NELEM, NPTS, NB), 1.0, 6.0, ((0, 8), (1, 4)), jnp.float32)
    quad = jnp.clip(jnp.exp(math.log(0.0013810679) - 1.3862944 * jax.random.uniform(arg_keys[2], (NELEM, NPTS), jnp.float32) ** block_levels(arg_keys[2], (NELEM, NPTS), ((0, 8), (1, 4)), -0.2, 0.2)), 0.00034526698, 0.0013810679)
    face_index = set_ends(jax.random.randint(arg_keys[3], (NELEM, 4, FACES), 0, PTS_DEV), jax.random.fold_in(arg_keys[3], 1), 0, PTS_DEV - 1).astype(jnp.int32)
    face_pairing = draw_face_pairing(jax.random.fold_in(arg_keys[6], 71), 0)
    orbitals = gaussian(arg_keys[5], (NELEM * NB, NORB), 1.0, 6.0, ((0, 8), (1, 4)), jnp.float32)
    return dict(basis=basis, applied=applied, quad=quad, face_index=face_index, face_pairing=face_pairing, orbitals=orbitals)


highest = lax.Precision.HIGHEST
penalty = 3.0
center = 4.0
half_width = 12.0


def inner(first, second):
    return jnp.dot(first.T, second, precision=highest)


def reference(basis, applied, quad, face_index, face_pairing, orbitals):
    shard_start = (jnp.arange(FACES) // FACE_DEV * PTS_DEV).astype(jnp.int32)
    pair_start = (jnp.arange(FACES) // FACE_DEV * FACE_DEV).astype(jnp.int32)
    faces_total = float(FACES)

    def element_blocks(index):
        following = (index + 1) % NELEM
        basis_own = basis[index]
        points = (face_index[index] + shard_start[None, :]).astype(jnp.int32)
        traces = basis_own[points]
        next_points = (face_index[following, 0:2] + shard_start[None, :]).astype(jnp.int32)
        next_traces = basis[following][next_points]
        order = (face_pairing[index] + pair_start).astype(jnp.int32)
        next_face = next_traces[0][order]
        next_deriv = (next_traces[0] - next_traces[1])[order]
        left_face = traces[0]
        left_deriv = traces[0] - traces[1]
        right_face = traces[2]
        right_deriv = traces[2] - traces[3]
        gram = jnp.dot((basis_own * quad[index][:, None]).T, applied[index], precision=highest)
        mixed = inner(left_deriv, left_face) + inner(right_deriv, right_face)
        own_block = penalty * (inner(left_face, left_face) + inner(right_face, right_face)) - 0.5 * (mixed + mixed.T)
        coupling = 0.5 * inner(right_deriv, next_face) - 0.5 * inner(right_face, next_deriv) - penalty * inner(right_face, next_face)
        return 0.5 * (gram + gram.T) + own_block / faces_total, coupling / faces_total

    volume, coupling = lax.map(element_blocks, jnp.arange(NELEM, dtype=jnp.int32))
    earlier = jnp.roll(coupling, 1, axis=0)

    def operate(field):
        above = jnp.roll(field, -1, axis=0)
        below = jnp.roll(field, 1, axis=0)
        result = jnp.einsum("eab,ebo->eao", volume, field, precision=highest)
        result = result + jnp.einsum("eab,ebo->eao", coupling, above, precision=highest)
        result = result + jnp.einsum("eba,ebo->eao", earlier, below, precision=highest)
        return (result - center * field) / half_width

    vector = orbitals.reshape(NELEM, NB, NORB)
    previous = vector
    current = operate(vector)
    for degree in range(1, DEG):
        upcoming = 2.0 * operate(current) - previous
        previous = current
        current = upcoming
    return current.reshape(NELEM * NB, NORB)
```

```python
import functools

import jax
import jax.numpy as jnp
from jax import lax
from jax.experimental import pallas as pl
from jax.experimental.pallas import tpu as pltpu
from jax.sharding import PartitionSpec as P

NB = 256
DEG = 4

penalty = 3.0
center = 4.0
half_width = 12.0

PARAMS = pltpu.CompilerParams(vmem_limit_bytes=40 * 1024 * 1024)
NN = (((1,), (0,)), ((), ()))
NT = (((1,), (1,)), ((), ()))


def split(value):
    high = value.astype(jnp.bfloat16)
    low = (value - high.astype(jnp.float32)).astype(jnp.bfloat16)
    return high, low


def dot(first, second, dims=NN):
    return lax.dot_general(first, second, dims, preferred_element_type=jnp.float32)


def dot3(first, second, dims=NN):
    first_high, first_low = first
    second_high, second_low = second
    return dot(first_high, second_high, dims) + (dot(first_high, second_low, dims) + dot(first_low, second_high, dims))


def picked(parts, chosen):
    return dot(parts[0], chosen) + dot(parts[1], chosen)


def one_hot(index_row, rows, offset=0):
    at = lax.broadcasted_iota(jnp.int32, (rows, index_row.shape[1]), 0) - offset
    return (at == index_row).astype(jnp.float32).astype(jnp.bfloat16)


def edge_kernel(index_ref, basis_ref, traces_ref):
    parts = split(basis_ref[0].T)
    traces_ref[...] = picked(parts, one_hot(index_ref[0], basis_ref.shape[1]))


def volume_kernel(faces_total, index_ref, quad_ref, basis_ref, applied_ref, traces_ref, volume_ref):
    flipped = basis_ref[0].T
    traces = picked(split(flipped), one_hot(index_ref[0], basis_ref.shape[1]))
    traces_ref[0] = traces
    width = traces.shape[1] // 2
    outer, layer = traces[:, :width], traces[:, width:]
    total = dot3(split(flipped * quad_ref[0]), split(applied_ref[0]))
    total = total + dot3(split((2.0 * outer + layer) * (1.0 / faces_total)), split(outer), NT)
    volume_ref[0] = 0.5 * (total + total.T)


def coupling_kernel(faces_total, count, pair_ref, own_ref, next_ref, lead_ref, coupling_ref):
    step = pl.program_id(0)
    own = own_ref[0]
    width = own.shape[1] // 2
    outer, layer = own[:, :width], own[:, width:]
    near = split((penalty * outer + 0.5 * layer) * (-1.0 / faces_total))
    far = split(outer * (0.5 / faces_total))

    def finish(face, inside):
        coupling_ref[0] = dot3(near, split(face), NT) + dot3(far, split(inside), NT)

    @pl.when(step < count - 1)
    def _():
        order = one_hot(pair_ref[0], width)
        following = next_ref[0]
        finish(picked(split(following[:, :width]), order), picked(split(following[:, width:]), order))

    @pl.when(step == count - 1)
    def _():
        lead = split(lead_ref[...])
        finish(picked(lead, one_hot(pair_ref[0], width)), picked(lead, one_hot(pair_ref[0], width, width // 2)))


def weights_kernel(volume_ref, coupling_ref, earlier_ref, before_ref, high_ref, low_ref):
    step = pl.program_id(0)
    size = volume_ref.shape[1]
    diagonal = lax.broadcasted_iota(jnp.int32, (size, size), 0) == lax.broadcasted_iota(jnp.int32, (size, size), 1)
    own = (volume_ref[0] - jnp.where(diagonal, center, 0.0)) * (1.0 / half_width)
    earlier = jnp.where(step == 0, before_ref[0], earlier_ref[0])
    for at, value in enumerate((earlier.T, own, coupling_ref[0])):
        high, low = split(value * (1.0 / half_width) if at != 1 else value)
        high_ref[0, :, at * size : (at + 1) * size] = high
        low_ref[0, :, at * size : (at + 1) * size] = low


def apply_row(high, low, below, middle, above):
    total = None
    size = middle.shape[0]
    for at, value in enumerate((below, middle, above)):
        value_high, value_low = split(value)
        part_high, part_low = high[:, at * size : (at + 1) * size], low[:, at * size : (at + 1) * size]
        term = dot3((part_high, part_low), (value_high, value_low))
        total = term if total is None else total + term
    return total


def advance(first, result, before):
    return result if first else 2.0 * result - before


def ends_kernel(first, count, high0, low0, high1, low1, ends, inner, below, above, before, out):
    row = apply_row(high0[0], low0[0], below[0], ends[0], inner[0])
    out[0] = advance(first, row, None if first else before[0])
    row = apply_row(high1[0], low1[0], inner[count - 3], ends[1], above[0])
    out[1] = advance(first, row, None if first else before[1])


def inner_kernel(first, count, high, low, ends, inner, before, out):
    for at in range(1, count - 1):
        lower = ends[0] if at == 1 else inner[at - 2]
        upper = ends[1] if at == count - 2 else inner[at]
        row = apply_row(high[at], low[at], lower, inner[at - 1], upper)
        out[at - 1] = advance(first, row, None if first else before[at - 1])


def whole(shape):
    return pl.BlockSpec(shape, lambda *steps: (0,) * len(shape))


def edge_traces(index, basis):
    points, size = basis.shape[1:]
    return pl.pallas_call(
        edge_kernel,
        grid=(1,),
        in_specs=[pl.BlockSpec((1, 1, index.shape[2]), lambda s: (0, 0, 0)), pl.BlockSpec((1, points, size), lambda s: (0, 0, 0))],
        out_specs=whole((size, index.shape[2])),
        out_shape=jax.ShapeDtypeStruct((size, index.shape[2]), jnp.float32),
        compiler_params=PARAMS,
    )(index, basis)


def volumes(index, quad, basis, applied, faces_total):
    count, points, size = basis.shape
    spots = index.shape[2]
    per = lambda *shape: pl.BlockSpec((1, *shape), lambda s: (s, 0, 0))
    return pl.pallas_call(
        functools.partial(volume_kernel, faces_total),
        grid=(count,),
        in_specs=[per(1, spots), per(1, points), per(points, size), per(points, size)],
        out_specs=[per(size, spots), per(size, size)],
        out_shape=[
            jax.ShapeDtypeStruct((count, size, spots), jnp.float32),
            jax.ShapeDtypeStruct((count, size, size), jnp.float32),
        ],
        compiler_params=PARAMS,
    )(index, quad, basis, applied)


def couplings(pairs, traces, lead, faces_total):
    count, size, spots = traces.shape
    per = lambda *shape: pl.BlockSpec((1, *shape), lambda s: (s, 0, 0))
    return pl.pallas_call(
        functools.partial(coupling_kernel, faces_total, count),
        grid=(count,),
        in_specs=[
            per(1, pairs.shape[2]),
            per(size, spots),
            pl.BlockSpec((1, size, spots), lambda s: (jnp.minimum(s + 1, count - 1), 0, 0)),
            whole(lead.shape),
        ],
        out_specs=per(size, size),
        out_shape=jax.ShapeDtypeStruct((count, size, size), jnp.float32),
        compiler_params=PARAMS,
    )(pairs, traces, traces, lead)


def weights(volume, coupling, before):
    count, size, _ = volume.shape
    per = lambda *shape: pl.BlockSpec((1, *shape), lambda s: (s, 0, 0))
    return pl.pallas_call(
        weights_kernel,
        grid=(count,),
        in_specs=[
            per(size, size),
            per(size, size),
            pl.BlockSpec((1, size, size), lambda s: (jnp.maximum(s - 1, 0), 0, 0)),
            whole(before.shape),
        ],
        out_specs=[per(size, 3 * size), per(size, 3 * size)],
        out_shape=[jax.ShapeDtypeStruct((count, size, 3 * size), jnp.bfloat16)] * 2,
        compiler_params=PARAMS,
    )(volume, coupling, coupling, before)


def chunk_of(columns):
    return 256 if columns % 256 == 0 else columns


def apply_ends(first, high, low, ends, inner, below, above, before):
    count, size, depth = high.shape
    columns = ends.shape[2]
    chunk = chunk_of(columns)
    part = lambda n: pl.BlockSpec((n, size, chunk), lambda s: (0, 0, s))
    head = pl.BlockSpec((1, size, depth), lambda s: (0, 0, 0))
    tail = pl.BlockSpec((1, size, depth), lambda s: (count - 1, 0, 0))
    return pl.pallas_call(
        functools.partial(ends_kernel, first, count),
        grid=(columns // chunk,),
        in_specs=[head, head, tail, tail, part(2), part(count - 2), part(1), part(1), part(2)],
        out_specs=part(2),
        out_shape=jax.ShapeDtypeStruct((2, size, columns), jnp.float32),
        compiler_params=PARAMS,
    )(high, low, high, low, ends, inner, below, above, before)


def apply_inner(first, high, low, ends, inner, before):
    count, size, depth = high.shape
    columns = ends.shape[2]
    chunk = chunk_of(columns)
    part = lambda n: pl.BlockSpec((n, size, chunk), lambda s: (0, 0, s))
    return pl.pallas_call(
        functools.partial(inner_kernel, first, count),
        grid=(columns // chunk,),
        in_specs=[whole(high.shape), whole(low.shape), part(2), part(count - 2), part(count - 2)],
        out_specs=part(count - 2),
        out_shape=jax.ShapeDtypeStruct((count - 2, size, columns), jnp.float32),
        compiler_params=PARAMS,
    )(high, low, ends, inner, before)


def flipped(value, axis, bit):
    count = lax.axis_size(axis)
    return lax.ppermute(value, axis, [(i, i ^ bit) for i in range(count)])


def shifted(value, axis, steps):
    count = lax.axis_size(axis)
    return lax.ppermute(value, axis, [(i, (i + steps) % count) for i in range(count)])


def summed_half(value, core):
    half = value.shape[0] // 2
    send = lax.dynamic_slice_in_dim(value, (1 - core) * half, half)
    keep = lax.dynamic_slice_in_dim(value, core * half, half)
    keep = keep + flipped(send, "pts", 1)
    bit = 2
    while bit < lax.axis_size("pts"):
        keep = keep + flipped(keep, "pts", bit)
        bit *= 2
    return keep


def both_halves(value, core):
    other = flipped(value, "pts", 1)
    return jnp.where(core == 0, jnp.concatenate([value, other]), jnp.concatenate([other, value]))


def body(basis, applied, quad, face_index, face_pairing, orbitals):
    count, points, size = basis.shape
    spots = face_index.shape[2]
    columns = orbitals.shape[1]
    faces_total = float(spots * lax.axis_size("pts"))
    core = lax.axis_index("pts") % 2

    vector = orbitals.reshape(count, size, columns)
    ends = jnp.concatenate([vector[:1], vector[-1:]])
    inner = vector[1:-1]
    below = shifted(vector[-1:], "elem", 1)
    above = shifted(vector[:1], "elem", -1)

    lead_index = face_index[:1, 0:2].reshape(1, 1, 2 * spots)
    lead = shifted(edge_traces(lead_index, basis), "elem", -1)
    index = jnp.stack([face_index[:, 0], face_index[:, 2], face_index[:, 1], face_index[:, 3]], axis=1)
    index = index.reshape(count, 1, 4 * spots)
    pairs = jnp.concatenate([jnp.full_like(face_pairing, -points), face_pairing], axis=1).reshape(count, 1, 2 * spots)
    traces, volume = volumes(index, quad.reshape(count, 1, points), basis, applied, faces_total)
    coupling = couplings(pairs, traces, lead, faces_total)
    volume = both_halves(summed_half(volume, core), core)
    coupling = both_halves(summed_half(coupling, core), core)
    before = shifted(coupling[-1:], "elem", 1)
    high, low = weights(volume, coupling, before)

    old_ends, old_inner = ends, inner
    for degree in range(DEG):
        first = degree == 0
        new_inner = apply_inner(first, high, low, ends, inner, old_inner)
        new_ends = apply_ends(first, high, low, ends, inner, below, above, old_ends)
        old_ends, old_inner, ends, inner = ends, inner, new_ends, new_inner
        if degree < DEG - 1:
            below = shifted(ends[1:], "elem", 1)
            above = shifted(ends[:1], "elem", -1)
    result = jnp.concatenate([ends[:1], inner, ends[1:]])
    return result.reshape(count * size, columns)


def solution(mesh):
    return jax.shard_map(
        body,
        mesh=mesh,
        in_specs=(
            P("elem", "pts", None),
            P("elem", "pts", None),
            P("elem", "pts"),
            P("elem", None, "pts"),
            P("elem", "pts"),
            P("elem", "pts"),
        ),
        out_specs=P("elem", "pts"),
        check_vma=False,
    )
```

```python
import functools

import jax
import jax.numpy as jnp
from jax import lax
from jax.experimental import pallas as pl
from jax.experimental.pallas import tpu as pltpu
from jax.sharding import PartitionSpec as P

NB = 256
DEG = 4

penalty = 3.0
center = 4.0
half_width = 12.0

PARAMS = pltpu.CompilerParams(vmem_limit_bytes=40 * 1024 * 1024)
NN = (((1,), (0,)), ((), ()))
NT = (((1,), (1,)), ((), ()))


def split(value):
    high = value.astype(jnp.bfloat16)
    low = (value - high.astype(jnp.float32)).astype(jnp.bfloat16)
    return high, low


def dot(first, second, dims=NN):
    return lax.dot_general(first, second, dims, preferred_element_type=jnp.float32)


def dot3(first, second, dims=NN):
    first_high, first_low = first
    second_high, second_low = second
    return dot(first_high, second_high, dims) + (dot(first_high, second_low, dims) + dot(first_low, second_high, dims))


def picked(parts, chosen):
    return dot(parts[0], chosen) + dot(parts[1], chosen)


def one_hot(index_row, rows, offset=0):
    at = lax.broadcasted_iota(jnp.int32, (rows, index_row.shape[1]), 0) - offset
    return (at == index_row).astype(jnp.float32).astype(jnp.bfloat16)


def edge_kernel(index_ref, basis_ref, traces_ref):
    parts = split(basis_ref[0].T)
    traces_ref[...] = picked(parts, one_hot(index_ref[0], basis_ref.shape[1]))


def volume_kernel(faces_total, index_ref, quad_ref, basis_ref, applied_ref, traces_ref, volume_ref):
    flipped = basis_ref[0].T
    traces = picked(split(flipped), one_hot(index_ref[0], basis_ref.shape[1]))
    traces_ref[0] = traces
    width = traces.shape[1] // 2
    outer, layer = traces[:, :width], traces[:, width:]
    total = dot3(split(flipped * quad_ref[0]), split(applied_ref[0]))
    total = total + dot3(split((2.0 * outer + layer) * (1.0 / faces_total)), split(outer), NT)
    volume_ref[0] = 0.5 * (total + total.T)


def packed(volume):
    half = volume.shape[0] // 2
    row = lax.broadcasted_iota(jnp.int32, (half, half), 0)
    column = lax.broadcasted_iota(jnp.int32, (half, half), 1)
    corner = volume[half:, half:]
    mixed = jnp.where(column >= row, volume[:half, :half], corner)
    diagonal = jnp.sum(jnp.where(column == row, corner, 0.0), axis=0, keepdims=True)
    return mixed, volume[:half, half:], diagonal


def unpacked(mixed, side, diagonal):
    half = mixed.shape[0]
    row = lax.broadcasted_iota(jnp.int32, (half, half), 0)
    column = lax.broadcasted_iota(jnp.int32, (half, half), 1)
    turned = mixed.T
    first = jnp.where(column >= row, mixed, turned)
    corner = jnp.where(column < row, mixed, jnp.where(column == row, diagonal, turned))
    top = jnp.concatenate([first, side], axis=1)
    return jnp.concatenate([top, jnp.concatenate([side.T, corner], axis=1)], axis=0)


def coupling_kernel(faces_total, count, order_ref, pair_ref, own_ref, next_ref, lead_ref, volume_ref, send_ref, keep_ref):
    step = pl.program_id(0)
    element = order_ref[step]
    own = own_ref[0]
    size = own.shape[0]
    width = own.shape[1] // 2
    outer, layer = own[:, :width], own[:, width:]
    near = split((penalty * outer + 0.5 * layer) * (-1.0 / faces_total))
    far = split(outer * (0.5 / faces_total))
    mixed, side, diagonal = packed(volume_ref[0])
    half = size // 2

    def store(out_ref, coupling):
        out_ref[0, :size] = coupling
        out_ref[0, size : size + half, :half] = mixed
        out_ref[0, size : size + half, half:] = side
        out_ref[0, size + half :, :] = jnp.broadcast_to(jnp.concatenate([diagonal, diagonal], axis=1), (8, size))

    def finish(face, inside):
        coupling = dot3(near, split(face), NT) + dot3(far, split(inside), NT)

        @pl.when(step < count // 2)
        def _():
            store(send_ref, coupling)

        @pl.when(step >= count // 2)
        def _():
            store(keep_ref, coupling)

    @pl.when(element < count - 1)
    def _():
        order = one_hot(pair_ref[0], width)
        following = next_ref[0]
        finish(picked(split(following[:, :width]), order), picked(split(following[:, width:]), order))

    @pl.when(element == count - 1)
    def _():
        lead = split(lead_ref[...])
        finish(picked(lead, one_hot(pair_ref[0], width)), picked(lead, one_hot(pair_ref[0], width, width // 2)))


def weights_kernel(me_ref, own_ref, other_ref, before_own_ref, before_other_ref, high_ref, low_ref):
    step = pl.program_id(0)
    me = me_ref[0]
    size = own_ref.shape[2]
    half = size // 2
    away = ((step ^ me) >> 1) & 1
    block = jnp.where(away == 1, other_ref[0], own_ref[0])
    volume = unpacked(block[size : size + half, :half], block[size : size + half, half:], block[size + half : size + half + 1, :half])
    diagonal = lax.broadcasted_iota(jnp.int32, (size, size), 0) == lax.broadcasted_iota(jnp.int32, (size, size), 1)
    volume = (volume - jnp.where(diagonal, center, 0.0)) * (1.0 / half_width)
    away = (((step - 1) ^ me) >> 1) & 1
    earlier = jnp.where(away == 1, before_other_ref[0], before_own_ref[0]) * (1.0 / half_width)
    for at, value in enumerate((earlier.T, volume, block[:size] * (1.0 / half_width))):
        high, low = split(value)
        high_ref[0, :, at * size : (at + 1) * size] = high
        low_ref[0, :, at * size : (at + 1) * size] = low


def apply_row(weights, values):
    total = None
    for weight, value in zip(weights, values):
        term = dot3(weight, split(value))
        total = term if total is None else total + term
    return total


def row_weights(high, low):
    size = high.shape[0]
    return [(high[:, at * size : (at + 1) * size], low[:, at * size : (at + 1) * size]) for at in range(3)]


def advance(first, result, before):
    return result if first else 2.0 * result - before


def ends_kernel(first, count, before, high0, low0, high1, low1, head, tail, inner, below, above, old_head, old_tail, new_head, new_tail):
    rows = row_weights(high0[0], low0[0])
    rows[0] = split((before[...] * (1.0 / half_width)).T)
    row = apply_row(rows, (below[...], head[...], inner[0]))
    new_head[...] = advance(first, row, None if first else old_head[...])
    row = apply_row(row_weights(high1[0], low1[0]), (inner[count - 3], tail[...], above[...]))
    new_tail[...] = advance(first, row, None if first else old_tail[...])


def inner_kernel(first, count, high, low, head, tail, inner, old, out):
    for at in range(1, count - 1):
        lower = head[...] if at == 1 else inner[at - 2]
        upper = tail[...] if at == count - 2 else inner[at]
        row = apply_row(row_weights(high[at], low[at]), (lower, inner[at - 1], upper))
        out[at - 1] = advance(first, row, None if first else old[at - 1])


def arrange_kernel(count, side_ref, own_ref, got_ref, head_ref, tail_ref, inner_ref):
    step = pl.program_id(0)
    value = jnp.where(step // (count // 2) == side_ref[0], own_ref[0], got_ref[0])

    @pl.when(step == 0)
    def _():
        head_ref[...] = value

    @pl.when(step == count - 1)
    def _():
        tail_ref[...] = value

    @pl.when((step > 0) & (step < count - 1))
    def _():
        inner_ref[0] = value


def collect_kernel(count, side_ref, head_ref, tail_ref, inner_ref, got_end_ref, got_inner_ref, out_ref):
    step = pl.program_id(0)
    side = side_ref[0]
    end = jnp.where(side == 0, head_ref[...], tail_ref[...])
    at_end = step == side * (count - 1)
    mine = jnp.where(at_end, end, inner_ref[0])
    theirs = jnp.where(at_end, got_end_ref[...], got_inner_ref[0])
    columns = mine.shape[1]
    out_ref[0, :, :columns] = jnp.where(side == 0, mine, theirs)
    out_ref[0, :, columns:] = jnp.where(side == 0, theirs, mine)


def whole(shape):
    return pl.BlockSpec(shape, lambda *steps: (0,) * len(shape))


def edge_traces(index, basis):
    points, size = basis.shape[1:]
    return pl.pallas_call(
        edge_kernel,
        grid=(1,),
        in_specs=[pl.BlockSpec((1, 1, index.shape[2]), lambda s: (0, 0, 0)), pl.BlockSpec((1, points, size), lambda s: (0, 0, 0))],
        out_specs=whole((size, index.shape[2])),
        out_shape=jax.ShapeDtypeStruct((size, index.shape[2]), jnp.float32),
        compiler_params=PARAMS,
    )(index, basis)


def volumes(index, quad, basis, applied, faces_total):
    count, points, size = basis.shape
    spots = index.shape[2]
    per = lambda *shape: pl.BlockSpec((1, *shape), lambda s: (s, 0, 0))
    return pl.pallas_call(
        functools.partial(volume_kernel, faces_total),
        grid=(count,),
        in_specs=[per(1, spots), per(1, points), per(points, size), per(points, size)],
        out_specs=[per(size, spots), per(size, size)],
        out_shape=[
            jax.ShapeDtypeStruct((count, size, spots), jnp.float32),
            jax.ShapeDtypeStruct((count, size, size), jnp.float32),
        ],
        compiler_params=PARAMS,
    )(index, quad, basis, applied)


def couplings(order, pairs, traces, lead, volume, faces_total):
    count, size, spots = traces.shape
    rows = size + size // 2 + 8
    per = lambda *shape: pl.BlockSpec((1, *shape), lambda s, o: (o[s], 0, 0))
    half = count // 2
    return pl.pallas_call(
        functools.partial(coupling_kernel, faces_total, count),
        grid_spec=pltpu.PrefetchScalarGridSpec(
            num_scalar_prefetch=1,
            grid=(count,),
            in_specs=[
                per(1, pairs.shape[2]),
                per(size, spots),
                pl.BlockSpec((1, size, spots), lambda s, o: (jnp.minimum(o[s] + 1, count - 1), 0, 0)),
                whole(lead.shape),
                per(size, size),
            ],
            out_specs=[
                pl.BlockSpec((1, rows, size), lambda s, o: (jnp.minimum(s, half - 1), 0, 0)),
                pl.BlockSpec((1, rows, size), lambda s, o: (jnp.maximum(s - half, 0), 0, 0)),
            ],
        ),
        out_shape=[jax.ShapeDtypeStruct((half, rows, size), jnp.float32)] * 2,
        compiler_params=PARAMS,
    )(order, pairs, traces, traces, lead, volume)


def weights(me, own, other, size):
    count = 2 * own.shape[0]
    rows = own.shape[1]

    def spot(element, mine):
        away = element ^ mine
        return (away >> 2) * 2 + (away & 1)

    block = pl.BlockSpec((1, rows, size), lambda s, m: (spot(s, m[0]), 0, 0))
    prior = pl.BlockSpec((1, size, size), lambda s, m: (spot(jnp.maximum(s - 1, 0), m[0]), 0, 0))
    return pl.pallas_call(
        weights_kernel,
        grid_spec=pltpu.PrefetchScalarGridSpec(
            num_scalar_prefetch=1,
            grid=(count,),
            in_specs=[block, block, prior, prior],
            out_specs=[pl.BlockSpec((1, size, 3 * size), lambda s, m: (s, 0, 0))] * 2,
        ),
        out_shape=[jax.ShapeDtypeStruct((count, size, 3 * size), jnp.bfloat16)] * 2,
        compiler_params=PARAMS,
    )(me, own, other, own, other)


def apply_ends(first, before, high, low, head, tail, inner, below, above, old_head, old_tail):
    count, size, depth = high.shape
    columns = head.shape[1]
    flat = pl.BlockSpec((size, columns), lambda s: (0, 0))
    row = lambda at: pl.BlockSpec((1, size, depth), lambda s: (at, 0, 0))
    return pl.pallas_call(
        functools.partial(ends_kernel, first, count),
        grid=(1,),
        in_specs=[whole(before.shape), row(0), row(0), row(count - 1), row(count - 1), flat, flat, whole(inner.shape)] + [flat] * 4,
        out_specs=[flat, flat],
        out_shape=[jax.ShapeDtypeStruct((size, columns), jnp.float32)] * 2,
        compiler_params=PARAMS,
    )(before, high, low, high, low, head, tail, inner, below, above, old_head, old_tail)


def apply_inner(first, high, low, head, tail, inner, old):
    count, size, depth = high.shape
    return pl.pallas_call(
        functools.partial(inner_kernel, first, count),
        grid=(1,),
        in_specs=[whole(high.shape), whole(low.shape), whole(head.shape), whole(tail.shape), whole(inner.shape), whole(inner.shape)],
        out_specs=whole(inner.shape),
        out_shape=jax.ShapeDtypeStruct(inner.shape, jnp.float32),
        compiler_params=PARAMS,
    )(high, low, head, tail, inner, old)


def arranged(side, own, got):
    half, size, columns = own.shape
    count = 2 * half
    block = pl.BlockSpec((1, size, columns), lambda s, o: (s % half, 0, 0))
    flat = pl.BlockSpec((size, columns), lambda s, o: (0, 0))
    return pl.pallas_call(
        functools.partial(arrange_kernel, count),
        grid_spec=pltpu.PrefetchScalarGridSpec(
            num_scalar_prefetch=1,
            grid=(count,),
            in_specs=[block, block],
            out_specs=[flat, flat, pl.BlockSpec((1, size, columns), lambda s, o: (jnp.clip(s - 1, 0, count - 3), 0, 0))],
        ),
        out_shape=[jax.ShapeDtypeStruct((size, columns), jnp.float32)] * 2
        + [jax.ShapeDtypeStruct((count - 2, size, columns), jnp.float32)],
        compiler_params=PARAMS,
    )(side, own, got)


def collected(side, head, tail, inner, got_end, got_inner):
    size, columns = head.shape
    half = got_inner.shape[0] + 1
    spot = lambda s, o: jnp.where(o[0] == 0, jnp.maximum(s - 1, 0), jnp.minimum(s, half - 2))
    return pl.pallas_call(
        functools.partial(collect_kernel, half),
        grid_spec=pltpu.PrefetchScalarGridSpec(
            num_scalar_prefetch=1,
            grid=(half,),
            in_specs=[
                pl.BlockSpec((size, columns), lambda s, o: (0, 0)),
                pl.BlockSpec((size, columns), lambda s, o: (0, 0)),
                pl.BlockSpec((1, size, columns), lambda s, o: (o[0] * (half - 1) + spot(s, o), 0, 0)),
                pl.BlockSpec((size, columns), lambda s, o: (0, 0)),
                pl.BlockSpec((1, size, columns), lambda s, o: (spot(s, o), 0, 0)),
            ],
            out_specs=pl.BlockSpec((1, size, 2 * columns), lambda s, o: (s, 0, 0)),
        ),
        out_shape=jax.ShapeDtypeStruct((half, size, 2 * columns), jnp.float32),
        compiler_params=PARAMS,
    )(side, head, tail, inner, got_end, got_inner)


def flipped(value, axis, bit):
    count = lax.axis_size(axis)
    return lax.ppermute(value, axis, [(i, i ^ bit) for i in range(count)])


def shifted(value, axis, steps):
    count = lax.axis_size(axis)
    return lax.ppermute(value, axis, [(i, (i + steps) % count) for i in range(count)])


def body(basis, applied, quad, face_index, face_pairing, orbitals):
    count, points, size = basis.shape
    spots = face_index.shape[2]
    columns = orbitals.shape[1] // 2
    elems, width = lax.axis_size("elem"), lax.axis_size("pts")
    faces_total = float(spots * width)
    side = lax.axis_index("elem") % 2
    core = lax.axis_index("pts") % 2
    lane = lax.axis_index("pts") // 2 % 2
    side_at = side.reshape(1).astype(jnp.int32)

    vector = orbitals.reshape(count, size, 2 * columns)
    got = flipped(lax.dynamic_slice_in_dim(vector, (1 - side) * columns, columns, axis=2), "elem", 1)

    lead_index = face_index[:1, 0:2].reshape(1, 1, 2 * spots)
    lead = shifted(edge_traces(lead_index, basis), "elem", -1)
    index = jnp.stack([face_index[:, 0], face_index[:, 2], face_index[:, 1], face_index[:, 3]], axis=1)
    index = index.reshape(count, 1, 4 * spots)
    pairs = jnp.concatenate([jnp.full_like(face_pairing, -points), face_pairing], axis=1).reshape(count, 1, 2 * spots)
    traces, volume = volumes(index, quad.reshape(count, 1, points), basis, applied, faces_total)
    half = count // 2
    order = jnp.arange(count, dtype=jnp.int32) ^ ((1 - core).astype(jnp.int32) * half)
    send, keep = couplings(order, pairs, traces, lead, volume, faces_total)

    other = flipped(send, "pts", 1)
    quarter = half // 2
    pick = lambda value, at: lax.dynamic_slice_in_dim(value, at * quarter, quarter)
    send = pick(keep, 1 - lane) + pick(other, 1 - lane)
    mine = pick(keep, lane) + pick(other, lane) + flipped(send, "pts", 2)
    bit = 4
    while bit < width:
        mine = mine + flipped(mine, "pts", bit)
        bit *= 2
    beside = flipped(mine, "pts", 2)
    across = flipped(mine, "elem", 1)
    both = flipped(across, "pts", 2)
    own = jnp.concatenate([mine, beside, across, both])
    other = flipped(own, "pts", 1)

    last = lax.dynamic_slice(own, ((1 - side) * 2 + 1 - lane, 0, 0), (1, size, size))[0]
    flat = lambda e, p: e % elems * width + p
    odd = [(e, p) for e in range(elems) for p in range(1, width, 2)]
    before = lax.ppermute(last, ("elem", "pts"), [(flat(e, p), flat(e + 2, p)) for e, p in odd])
    before = before + lax.ppermute(before, ("elem", "pts"), [(flat(e, p), flat(e, p - 1)) for e, p in odd])

    own_half = lax.dynamic_slice_in_dim(vector, side * columns, columns, axis=2)
    head, tail, inner = arranged(side_at, own_half, got)
    below = shifted(tail, "elem", 2)
    above = shifted(head, "elem", -2)

    me = (side * 4 + core * 2 + lane).reshape(1).astype(jnp.int32)
    high, low = weights(me, own, other, size)

    old = head, tail, inner
    for degree in range(DEG):
        first = degree == 0
        new_head, new_tail = apply_ends(first, before, high, low, head, tail, inner, below, above, old[0], old[1])
        new_inner = apply_inner(first, high, low, head, tail, inner, old[2])
        old = head, tail, inner
        head, tail, inner = new_head, new_tail, new_inner
        if degree < DEG - 1:
            below = shifted(tail, "elem", 2)
            above = shifted(head, "elem", -2)

    got_inner = flipped(lax.dynamic_slice_in_dim(inner, (1 - side) * (count - 1), count - 1), "elem", 1)
    got_end = flipped(jnp.where(side == 0, tail, head), "elem", 1)
    result = collected(side_at, head, tail, inner, got_end, got_inner)
    return result.reshape(count * size, 2 * columns)


def solution(mesh):
    return jax.shard_map(
        body,
        mesh=mesh,
        in_specs=(
            P("elem", "pts", None),
            P("elem", "pts", None),
            P("elem", "pts"),
            P("elem", None, "pts"),
            P("elem", "pts"),
            P("elem", "pts"),
        ),
        out_specs=P("elem", "pts"),
        check_vma=False,
    )
```

```python
import functools

import jax
import jax.numpy as jnp
from jax import lax
from jax.experimental import pallas as pl
from jax.experimental.pallas import tpu as pltpu
from jax.sharding import PartitionSpec as P

NB = 256
DEG = 4

penalty = 3.0
center = 4.0
half_width = 12.0

LARGE = pltpu.CompilerParams(vmem_limit_bytes=48 * 1024 * 1024)
SMALL = pltpu.CompilerParams(vmem_limit_bytes=24 * 1024 * 1024)
VMEM = pl.BlockSpec(memory_space=pltpu.VMEM)
NN = (((1,), (0,)), ((), ()))
NT = (((1,), (1,)), ((), ()))


def split(value):
    high = value.astype(jnp.bfloat16)
    low = (value - high.astype(jnp.float32)).astype(jnp.bfloat16)
    return high, low


def dot(first, second, dims=NN):
    return lax.dot_general(first, second, dims, preferred_element_type=jnp.float32)


def dot3(first, second, dims=NN):
    first_high, first_low = first
    second_high, second_low = second
    return dot(first_high, second_high, dims) + (dot(first_high, second_low, dims) + dot(first_low, second_high, dims))


def picked(parts, chosen):
    return dot(parts[0], chosen) + dot(parts[1], chosen)


def one_hot(index_row, rows, offset=0):
    at = lax.broadcasted_iota(jnp.int32, (rows, index_row.shape[1]), 0) - offset
    return (at == index_row).astype(jnp.float32).astype(jnp.bfloat16)


def edge_kernel(index_ref, basis_ref, traces_ref):
    parts = split(basis_ref[0].T)
    traces_ref[...] = picked(parts, one_hot(index_ref[0], basis_ref.shape[1]))


def volume_kernel(faces_total, index_ref, quad_ref, basis_ref, applied_ref, traces_ref, volume_ref):
    flipped = basis_ref[0].T
    traces = picked(split(flipped), one_hot(index_ref[0], basis_ref.shape[1]))
    traces_ref[0] = traces
    width = traces.shape[1] // 2
    outer, layer = traces[:, :width], traces[:, width:]
    total = dot3(split(flipped * quad_ref[0]), split(applied_ref[0]))
    total = total + dot3(split((2.0 * outer + layer) * (1.0 / faces_total)), split(outer), NT)
    volume_ref[0] = 0.5 * (total + total.T)


def packed(volume):
    half = volume.shape[0] // 2
    row = lax.broadcasted_iota(jnp.int32, (half, half), 0)
    column = lax.broadcasted_iota(jnp.int32, (half, half), 1)
    corner = volume[half:, half:]
    mixed = jnp.where(column >= row, volume[:half, :half], corner)
    diagonal = jnp.sum(jnp.where(column == row, corner, 0.0), axis=0, keepdims=True)
    return mixed, volume[:half, half:], diagonal


def unpacked(mixed, side, diagonal):
    half = mixed.shape[0]
    row = lax.broadcasted_iota(jnp.int32, (half, half), 0)
    column = lax.broadcasted_iota(jnp.int32, (half, half), 1)
    turned = mixed.T
    first = jnp.where(column >= row, mixed, turned)
    corner = jnp.where(column < row, mixed, jnp.where(column == row, diagonal, turned))
    top = jnp.concatenate([first, side], axis=1)
    return jnp.concatenate([top, jnp.concatenate([side.T, corner], axis=1)], axis=0)


def coupling_kernel(faces_total, count, order_ref, pair_ref, own_ref, next_ref, lead_ref, volume_ref, send_ref, keep_ref):
    step = pl.program_id(0)
    element = order_ref[step]
    own = own_ref[0]
    size = own.shape[0]
    width = own.shape[1] // 2
    outer, layer = own[:, :width], own[:, width:]
    near = split((penalty * outer + 0.5 * layer) * (-1.0 / faces_total))
    far = split(outer * (0.5 / faces_total))
    mixed, side, diagonal = packed(volume_ref[0])
    half = size // 2

    def store(out_ref, coupling):
        out_ref[0, :size] = coupling
        out_ref[0, size : size + half, :half] = mixed
        out_ref[0, size : size + half, half:] = side
        out_ref[0, size + half :, :] = jnp.broadcast_to(jnp.concatenate([diagonal, diagonal], axis=1), (8, size))

    def finish(face, inside):
        coupling = dot3(near, split(face), NT) + dot3(far, split(inside), NT)

        @pl.when(step < count // 2)
        def _():
            store(send_ref, coupling)

        @pl.when(step >= count // 2)
        def _():
            store(keep_ref, coupling)

    @pl.when(element < count - 1)
    def _():
        order = one_hot(pair_ref[0], width)
        following = next_ref[0]
        finish(picked(split(following[:, :width]), order), picked(split(following[:, width:]), order))

    @pl.when(element == count - 1)
    def _():
        lead = split(lead_ref[...])
        finish(picked(lead, one_hot(pair_ref[0], width)), picked(lead, one_hot(pair_ref[0], width, width // 2)))


def weights_kernel(me_ref, mine, beside, across, both, near_ref, far_ref, high_ref, low_ref):
    me = me_ref[0]
    size = mine.shape[2]
    half = size // 2
    pieces = {0: (mine, 0), 1: (beside, 0), 4: (across, 0), 5: (both, 0), 2: (near_ref, 0), 3: (near_ref, 1), 6: (near_ref, 2), 7: (far_ref, 0)}
    row = lax.broadcasted_iota(jnp.int32, (size, size), 0)
    diagonal = row == lax.broadcasted_iota(jnp.int32, (size, size), 1)

    for away, (piece, at) in pieces.items():
        element = away ^ me
        volume = unpacked(
            piece[at, size : size + half, :half], piece[at, size : size + half, half:], piece[at, size + half : size + half + 1, :half]
        )
        volume = (volume - jnp.where(diagonal, center, 0.0)) * (1.0 / half_width)
        coupling = piece[at, :size] * (1.0 / half_width)
        following = lax.rem(element + 1, len(pieces))
        for place, at_column, value in ((following, 0, coupling.T), (element, 1, volume), (element, 2, coupling)):
            high, low = split(value)
            high_ref[place, :, at_column * size : (at_column + 1) * size] = high
            low_ref[place, :, at_column * size : (at_column + 1) * size] = low


def apply_row(weights, values):
    total = None
    for weight, value in zip(weights, values):
        term = dot3(weight, split(value))
        total = term if total is None else total + term
    return total


def row_weights(high, low):
    size = high.shape[0]
    return [(high[:, at * size : (at + 1) * size], low[:, at * size : (at + 1) * size]) for at in range(3)]


def advance(first, result, before):
    return result if first else 2.0 * result - before


def head_kernel(first, before, high, low, head, inner, below, old, out):
    rows = row_weights(high[0], low[0])
    rows[0] = split((before[...] * (1.0 / half_width)).T)
    out[...] = advance(first, apply_row(rows, (below[...], head[...], inner[0])), None if first else old[...])


def tail_kernel(first, high, low, tail, inner, above, old, out):
    rows = row_weights(high[high.shape[0] - 1], low[high.shape[0] - 1])
    values = (inner[inner.shape[0] - 1], tail[...], above[...])
    out[...] = advance(first, apply_row(rows, values), None if first else old[...])


def inner_kernel(first, high, low, head, tail, inner, old, out):
    count = inner.shape[0]

    @pl.loop(0, count)
    def _(at):
        lower = jnp.where(at == 0, head[...], inner[jnp.maximum(at - 1, 0)])
        upper = jnp.where(at == count - 1, tail[...], inner[jnp.minimum(at + 1, count - 1)])
        row = apply_row(row_weights(high[at + 1], low[at + 1]), (lower, inner[at], upper))
        out[at] = advance(first, row, None if first else old[at])


def cut_kernel(vector_ref, *out_refs):
    width = out_refs[0].shape[2]
    for at, out_ref in enumerate(out_refs):
        out_ref[...] = vector_ref[:, :, at * width : (at + 1) * width]


def arrange_kernel(count, side_ref, own_ref, got_ref, head_ref, tail_ref, inner_ref):
    step = pl.program_id(0)
    value = jnp.where(step // (count // 2) == side_ref[0], own_ref[0], got_ref[0])

    @pl.when(step == 0)
    def _():
        head_ref[...] = value

    @pl.when(step == count - 1)
    def _():
        tail_ref[...] = value

    @pl.when((step > 0) & (step < count - 1))
    def _():
        inner_ref[0] = value


def collect_kernel(count, chunks, side_ref, *refs):
    out_ref = refs[-1]
    step = pl.program_id(0)
    side = side_ref[0]
    at_end = step == side * (count - 1)
    for chunk in range(chunks):
        head_ref, tail_ref, inner_ref, got_end_ref, got_inner_ref = refs[5 * chunk : 5 * chunk + 5]
        end = jnp.where(side == 0, head_ref[...], tail_ref[...])
        mine = jnp.where(at_end, end, inner_ref[0])
        theirs = jnp.where(at_end, got_end_ref[...], got_inner_ref[0])
        width = mine.shape[1]
        first = chunk * width
        second = (chunks + chunk) * width
        out_ref[0, :, first : first + width] = jnp.where(side == 0, mine, theirs)
        out_ref[0, :, second : second + width] = jnp.where(side == 0, theirs, mine)


def whole(shape):
    return pl.BlockSpec(shape, lambda *steps: (0,) * len(shape))


def edge_traces(index, basis):
    points, size = basis.shape[1:]
    return pl.pallas_call(
        edge_kernel,
        grid=(1,),
        in_specs=[pl.BlockSpec((1, 1, index.shape[2]), lambda s: (0, 0, 0)), pl.BlockSpec((1, points, size), lambda s: (0, 0, 0))],
        out_specs=whole((size, index.shape[2])),
        out_shape=jax.ShapeDtypeStruct((size, index.shape[2]), jnp.float32),
        compiler_params=LARGE,
    )(index, basis)


def volumes(index, quad, basis, applied, faces_total):
    count, points, size = basis.shape
    spots = index.shape[2]
    per = lambda *shape: pl.BlockSpec((1, *shape), lambda s: (s, 0, 0))
    return pl.pallas_call(
        functools.partial(volume_kernel, faces_total),
        grid=(count,),
        in_specs=[per(1, spots), per(1, points), per(points, size), per(points, size)],
        out_specs=[per(size, spots), per(size, size)],
        out_shape=[
            jax.ShapeDtypeStruct((count, size, spots), jnp.float32),
            jax.ShapeDtypeStruct((count, size, size), jnp.float32),
        ],
        compiler_params=LARGE,
    )(index, quad, basis, applied)


def couplings(order, pairs, traces, lead, volume, faces_total):
    count, size, spots = traces.shape
    rows = size + size // 2 + 8
    per = lambda *shape: pl.BlockSpec((1, *shape), lambda s, o: (o[s], 0, 0))
    half = count // 2
    return pl.pallas_call(
        functools.partial(coupling_kernel, faces_total, count),
        grid_spec=pltpu.PrefetchScalarGridSpec(
            num_scalar_prefetch=1,
            grid=(count,),
            in_specs=[
                per(1, pairs.shape[2]),
                per(size, spots),
                pl.BlockSpec((1, size, spots), lambda s, o: (jnp.minimum(o[s] + 1, count - 1), 0, 0)),
                whole(lead.shape),
                per(size, size),
            ],
            out_specs=[
                pl.BlockSpec((1, rows, size), lambda s, o: (jnp.minimum(s, half - 1), 0, 0)),
                pl.BlockSpec((1, rows, size), lambda s, o: (jnp.maximum(s - half, 0), 0, 0)),
            ],
        ),
        out_shape=[jax.ShapeDtypeStruct((half, rows, size), jnp.float32)] * 2,
        compiler_params=LARGE,
    )(order, pairs, traces, traces, lead, volume)


def weights(me, mine, beside, across, both, near, far):
    size = mine.shape[2]
    return pl.pallas_call(
        weights_kernel,
        in_specs=[pl.BlockSpec(memory_space=pltpu.SMEM)] + [VMEM] * 6,
        out_specs=[VMEM] * 2,
        out_shape=[jax.ShapeDtypeStruct((8, size, 3 * size), jnp.bfloat16)] * 2,
        compiler_params=SMALL,
    )(me, mine, beside, across, both, near, far)


def apply_head(first, before, high, low, head, inner, below, old):
    return pl.pallas_call(
        functools.partial(head_kernel, first),
        in_specs=[VMEM] * 7,
        out_specs=VMEM,
        out_shape=jax.ShapeDtypeStruct(head.shape, jnp.float32),
        compiler_params=SMALL,
    )(before, high, low, head, inner, below, old)


def apply_tail(first, high, low, tail, inner, above, old):
    return pl.pallas_call(
        functools.partial(tail_kernel, first),
        in_specs=[VMEM] * 6,
        out_specs=VMEM,
        out_shape=jax.ShapeDtypeStruct(tail.shape, jnp.float32),
        compiler_params=SMALL,
    )(high, low, tail, inner, above, old)


def apply_inner(first, high, low, head, tail, inner, old):
    return pl.pallas_call(
        functools.partial(inner_kernel, first),
        in_specs=[VMEM] * 6,
        out_specs=VMEM,
        out_shape=jax.ShapeDtypeStruct(inner.shape, jnp.float32),
        compiler_params=SMALL,
    )(high, low, head, tail, inner, old)


def cut_columns(side, vector, chunks):
    count, size, columns = vector.shape
    half = columns // 2
    return pl.pallas_call(
        lambda side_ref, *refs: cut_kernel(*refs),
        grid_spec=pltpu.PrefetchScalarGridSpec(
            num_scalar_prefetch=1,
            grid=(count,),
            in_specs=[pl.BlockSpec((1, size, half), lambda s, o: (s, 0, o[0]))],
            out_specs=[pl.BlockSpec((1, size, half // chunks), lambda s, o: (s, 0, 0))] * chunks,
        ),
        out_shape=[jax.ShapeDtypeStruct((count, size, half // chunks), jnp.float32)] * chunks,
        compiler_params=LARGE,
    )(side, vector)


def arranged(side, vector, got, chunk):
    half, size, columns = got.shape
    count = 2 * half
    chunks = max(vector.shape[2] // 2 // columns, 1)
    block = pl.BlockSpec((1, size, columns), lambda s, o: (s % half, 0, 0))
    own = pl.BlockSpec((1, size, columns), lambda s, o: (s % half, 0, o[1] * chunks + chunk))
    flat = pl.BlockSpec((size, columns), lambda s, o: (0, 0))
    return pl.pallas_call(
        functools.partial(arrange_kernel, count),
        grid_spec=pltpu.PrefetchScalarGridSpec(
            num_scalar_prefetch=1,
            grid=(count,),
            in_specs=[own, block],
            out_specs=[flat, flat, pl.BlockSpec((1, size, columns), lambda s, o: (jnp.clip(s - 1, 0, count - 3), 0, 0))],
        ),
        out_shape=[jax.ShapeDtypeStruct((size, columns), jnp.float32)] * 2
        + [jax.ShapeDtypeStruct((count - 2, size, columns), jnp.float32)],
        compiler_params=LARGE,
    )(side, vector, got)


def collected(side, parts):
    size, width = parts[0][0].shape
    chunks = len(parts)
    half = parts[0][4].shape[0] + 1
    spot = lambda s, o: jnp.where(o[0] == 0, jnp.maximum(s - 1, 0), jnp.minimum(s, half - 2))
    flat = pl.BlockSpec((size, width), lambda s, o: (0, 0))
    return pl.pallas_call(
        functools.partial(collect_kernel, half, chunks),
        grid_spec=pltpu.PrefetchScalarGridSpec(
            num_scalar_prefetch=1,
            grid=(half,),
            in_specs=[
                flat,
                flat,
                pl.BlockSpec((1, size, width), lambda s, o: (o[0] * (half - 1) + spot(s, o), 0, 0)),
                flat,
                pl.BlockSpec((1, size, width), lambda s, o: (spot(s, o), 0, 0)),
            ]
            * chunks,
            out_specs=pl.BlockSpec((1, size, 2 * chunks * width), lambda s, o: (s, 0, 0)),
        ),
        out_shape=jax.ShapeDtypeStruct((half, size, 2 * chunks * width), jnp.float32),
        compiler_params=LARGE,
    )(side, *[value for part in parts for value in part])


def flipped(value, axis, bit):
    count = lax.axis_size(axis)
    return lax.ppermute(value, axis, [(i, i ^ bit) for i in range(count)])


def shifted(value, axis, steps):
    count = lax.axis_size(axis)
    return lax.ppermute(value, axis, [(i, (i + steps) % count) for i in range(count)])


def body(basis, applied, quad, face_index, face_pairing, orbitals):
    count, points, size = basis.shape
    spots = face_index.shape[2]
    columns = orbitals.shape[1]
    chunks = 2 if columns % 512 == 0 else 1
    elems, width = lax.axis_size("elem"), lax.axis_size("pts")
    faces_total = float(spots * width)
    side = lax.axis_index("elem") % 2
    core = lax.axis_index("pts") % 2
    lane = lax.axis_index("pts") // 2 % 2
    side_at = side.reshape(1).astype(jnp.int32)
    vector = orbitals.reshape(count, size, columns)

    if columns // 2 % 128 == 0:
        own, own_at = vector, side_at
        foreign = cut_columns(1 - side_at, vector, chunks)
    else:
        own, own_at = lax.dynamic_slice_in_dim(vector, side * (columns // 2), columns // 2, axis=2), jnp.zeros_like(side_at)
        foreign = [lax.dynamic_slice_in_dim(vector, (1 - side) * (columns // 2), columns // 2, axis=2)]
    got = [flipped(value, "elem", 1) for value in foreign]

    lead_index = face_index[:1, 0:2].reshape(1, 1, 2 * spots)
    lead = shifted(edge_traces(lead_index, basis), "elem", -1)
    index = jnp.stack([face_index[:, 0], face_index[:, 2], face_index[:, 1], face_index[:, 3]], axis=1)
    index = index.reshape(count, 1, 4 * spots)
    pairs = jnp.concatenate([jnp.full_like(face_pairing, -points), face_pairing], axis=1).reshape(count, 1, 2 * spots)
    traces, volume = volumes(index, quad.reshape(count, 1, points), basis, applied, faces_total)
    got[0], lead, traces, volume = lax.optimization_barrier((got[0], lead, traces, volume))
    half = count // 2
    order = jnp.arange(count, dtype=jnp.int32) ^ ((1 - core).astype(jnp.int32) * half)
    send, keep = couplings(order, pairs, traces, lead, volume, faces_total)

    state, belows, aboves = [], [], []

    def arrange(chunk, received):
        state.append(arranged(jnp.concatenate([side_at, own_at]), own, received, chunk))
        belows.append(shifted(state[chunk][1], "elem", 2))
        aboves.append(shifted(state[chunk][0], "elem", -2))

    arrange(0, got[0])

    other = flipped(send, "pts", 1)
    quarter = half // 2
    pick = lambda value, at: lax.dynamic_slice_in_dim(value, at * quarter, quarter)
    send = pick(keep, 1 - lane) + pick(other, 1 - lane)
    mine = pick(keep, lane) + pick(other, lane) + flipped(send, "pts", 2)
    bit = 4
    while bit < width:
        mine = mine + flipped(mine, "pts", bit)
        bit *= 2
    belows[0], aboves[0], got_last, mine = lax.optimization_barrier((belows[0], aboves[0], got[-1], mine))
    if chunks > 1:
        arrange(1, got_last)
    beside = flipped(mine, "pts", 2)
    across = flipped(mine, "elem", 1)
    both = flipped(across, "pts", 2)
    near = flipped(jnp.concatenate([mine, beside, across]), "pts", 1)
    belows[-1], aboves[-1], both = lax.optimization_barrier((belows[-1], aboves[-1], both))
    far = flipped(both, "pts", 1)

    last = jnp.where(
        side == 1, jnp.where(lane == 1, mine[0, :size], beside[0, :size]), jnp.where(lane == 1, across[0, :size], both[0, :size])
    )
    flat = lambda e, p: e % elems * width + p
    odd = [(e, p) for e in range(elems) for p in range(1, width, 2)]
    before = lax.ppermute(last, ("elem", "pts"), [(flat(e, p), flat(e + 2, p)) for e, p in odd])
    before = before + lax.ppermute(before, ("elem", "pts"), [(flat(e, p), flat(e, p - 1)) for e, p in odd])

    me = (side * 4 + core * 2 + lane).reshape(1).astype(jnp.int32)
    high, low = weights(me, mine, beside, across, both, near, far)

    old = list(state)
    parts = []
    for degree in range(DEG):
        first = degree == 0
        for c in range(chunks):
            head, tail, inner = state[c]
            new_tail = apply_tail(first, high, low, tail, inner, aboves[c], old[c][1])
            new_head = apply_head(first, before, high, low, head, inner, belows[c], old[c][0])
            new_inner = apply_inner(first, high, low, head, tail, inner, old[c][2])
            old[c] = state[c]
            state[c] = new_head, new_tail, new_inner
            if degree < DEG - 1:
                belows[c] = shifted(new_tail, "elem", 2)
                aboves[c] = shifted(new_head, "elem", -2)
            else:
                foreign = lax.dynamic_slice_in_dim(new_inner, (1 - side) * (count - 1), count - 1)
                got_inner = flipped(foreign, "elem", 1)
                got_end = flipped(jnp.where(side == 0, new_tail, new_head), "elem", 1)
                parts.append((new_head, new_tail, new_inner, got_end, got_inner))
    return collected(side_at, parts).reshape(count * size, columns)


def solution(mesh):
    return jax.shard_map(
        body,
        mesh=mesh,
        in_specs=(
            P("elem", "pts", None),
            P("elem", "pts", None),
            P("elem", "pts"),
            P("elem", None, "pts"),
            P("elem", "pts"),
            P("elem", "pts"),
        ),
        out_specs=P("elem", "pts"),
        check_vma=False,
    )
```

```python
import functools

import jax
import jax.numpy as jnp
from jax import lax
from jax.experimental import pallas as pl
from jax.experimental.pallas import tpu as pltpu
from jax.sharding import PartitionSpec as P

NB = 256
DEG = 4

penalty = 3.0
center = 4.0
half_width = 12.0

PARAMS = pltpu.CompilerParams(vmem_limit_bytes=12 * 1024 * 1024)
SCALARS = pl.BlockSpec(memory_space=pltpu.SMEM)
ANY = pl.BlockSpec(memory_space=pl.ANY)
VMEM = pl.BlockSpec(memory_space=pltpu.VMEM)
NN = (((1,), (0,)), ((), ()))
NT = (((1,), (1,)), ((), ()))


def split(value):
    high = value.astype(jnp.bfloat16)
    low = (value - high.astype(jnp.float32)).astype(jnp.bfloat16)
    return high, low


def dot(first, second, dims=NN):
    return lax.dot_general(first, second, dims, preferred_element_type=jnp.float32)


def dot3(first, second, dims=NN):
    first_high, first_low = first
    second_high, second_low = second
    return dot(first_high, second_high, dims) + (dot(first_high, second_low, dims) + dot(first_low, second_high, dims))


def picked(parts, chosen):
    return dot(parts[0], chosen) + dot(parts[1], chosen)


def one_hot(index_row, rows, offset=0):
    at = lax.broadcasted_iota(jnp.int32, (rows, index_row.shape[1]), 0) - offset
    return (at == index_row).astype(jnp.float32).astype(jnp.bfloat16)


def lead_kernel(side_ref, index_ref, basis_ref, vector_ref, traces_ref, *rest):
    cut_refs, (held, sems) = rest[:-2], rest[-2:]
    first = pltpu.make_async_copy(basis_ref.at[0], held, sems.at[0])
    first.start()
    width = cut_refs[0].shape[2]
    copies = []
    for at, out_ref in enumerate(cut_refs):
        source = vector_ref
        if vector_ref.shape[2] > width:
            start = pl.multiple_of((side_ref[0] * len(cut_refs) + at) * width, width)
            source = vector_ref.at[:, :, pl.ds(start, width)]
        copies.append(pltpu.make_async_copy(source, out_ref, sems.at[1 + at]))
        copies[-1].start()
    first.wait()
    traces_ref[...] = picked(split(held[...].T), one_hot(index_ref[0], held.shape[0]))
    for copy in copies:
        copy.wait()


def blocks_kernel(
    faces_total, core_ref, index_ref, quad_ref, pair_ref, basis_ref, applied_ref, send_ref, keep_ref, last_ref, held, acted, traces, sems
):
    count = basis_ref.shape[0]
    size = basis_ref.shape[2]
    half = size // 2
    core = core_ref[0]

    def copies(at):
        return (
            pltpu.make_async_copy(basis_ref.at[at], held.at[at], sems.at[2 * at]),
            pltpu.make_async_copy(applied_ref.at[at], acted.at[at], sems.at[2 * at + 1]),
        )

    for at in range(count):
        for copy in copies(at):
            copy.start()

    def store(element, rows, value):
        @pl.when(element // (count // 2) == core)
        def _():
            keep_ref[element % (count // 2), rows] = value

        @pl.when(element // (count // 2) != core)
        def _():
            send_ref[element % (count // 2), rows] = value

    @pl.loop(0, count)
    def _(at):
        for copy in copies(at):
            copy.wait()
        turned = held[at].T
        found = picked(split(turned), one_hot(index_ref[at], held.shape[1]))
        traces[at] = found
        width = found.shape[1] // 2
        outer, layer = found[:, :width], found[:, width:]
        total = dot3(split(turned * quad_ref[at]), split(acted[at]))
        total = total + dot3(split((2.0 * outer + layer) * (1.0 / faces_total)), split(outer), NT)
        mixed, side, diagonal = packed(0.5 * (total + total.T))
        store(at, slice(size, size + half), jnp.concatenate([mixed, side], axis=1))
        store(at, slice(size + half, None), jnp.broadcast_to(jnp.concatenate([diagonal, diagonal], axis=1), (8, size)))

    @pl.loop(0, count - 1)
    def _(at):
        following = traces[at + 1]
        width = following.shape[1] // 2
        order = one_hot(pair_ref[at], width)
        face, inside = picked(split(following[:, :width]), order), picked(split(following[:, width:]), order)
        store(at, slice(0, size), coupled(traces[at], face, inside, faces_total))

    last_ref[...] = traces[count - 1]


def coupled(own, face, inside, faces_total):
    width = own.shape[1] // 2
    outer, layer = own[:, :width], own[:, width:]
    near = split((penalty * outer + 0.5 * layer) * (-1.0 / faces_total))
    far = split(outer * (0.5 / faces_total))
    return dot3(near, split(face), NT) + dot3(far, split(inside), NT)


def last_kernel(faces_total, core_ref, pair_ref, own_ref, lead_ref, send_in, keep_in, send_ref, keep_ref, block, sem):
    width = own_ref.shape[1] // 2
    lead = split(lead_ref[...])
    face = picked(lead, one_hot(pair_ref[...], width))
    inside = picked(lead, one_hot(pair_ref[...], width, width // 2))
    block[...] = coupled(own_ref[...], face, inside, faces_total)
    at = send_ref.shape[0] - 1
    rows = pl.ds(0, block.shape[0])
    for core, ref in ((0, send_ref), (1, keep_ref)):

        @pl.when(core_ref[0] == core)
        def _():
            copy = pltpu.make_async_copy(block, ref.at[at, rows], sem)
            copy.start()
            copy.wait()


def packed(volume):
    half = volume.shape[0] // 2
    row = lax.broadcasted_iota(jnp.int32, (half, half), 0)
    column = lax.broadcasted_iota(jnp.int32, (half, half), 1)
    corner = volume[half:, half:]
    mixed = jnp.where(column >= row, volume[:half, :half], corner)
    diagonal = jnp.sum(jnp.where(column == row, corner, 0.0), axis=0, keepdims=True)
    return mixed, volume[:half, half:], diagonal


def unpacked(mixed, side, diagonal):
    half = mixed.shape[0]
    row = lax.broadcasted_iota(jnp.int32, (half, half), 0)
    column = lax.broadcasted_iota(jnp.int32, (half, half), 1)
    turned = mixed.T
    first = jnp.where(column >= row, mixed, turned)
    corner = jnp.where(column < row, mixed, jnp.where(column == row, diagonal, turned))
    top = jnp.concatenate([first, side], axis=1)
    return jnp.concatenate([top, jnp.concatenate([side.T, corner], axis=1)], axis=0)


def weights_kernel(me_ref, *refs):
    sources, (high_ref, low_ref), held, sems = refs[:6], refs[6:8], refs[8], refs[9]
    me = me_ref[0]
    size = held.shape[2]
    half = size // 2
    places = ((0, 0), (1, 0), (2, 0), (3, 0), (4, 0), (4, 1), (4, 2), (5, 0))
    away_at = (0, 1, 4, 5, 2, 3, 6, 7)
    copies = [pltpu.make_async_copy(sources[ref].at[at], held.at[n], sems.at[n]) for n, (ref, at) in enumerate(places)]
    for copy in copies:
        copy.start()
    row = lax.broadcasted_iota(jnp.int32, (size, size), 0)
    diagonal = row == lax.broadcasted_iota(jnp.int32, (size, size), 1)

    for n, away in enumerate(away_at):
        copies[n].wait()
        element = away ^ me
        volume = unpacked(held[n, size : size + half, :half], held[n, size : size + half, half:], held[n, size + half : size + half + 1, :half])
        volume = (volume - jnp.where(diagonal, center, 0.0)) * (1.0 / half_width)
        coupling = held[n, :size] * (1.0 / half_width)
        following = lax.rem(element + 1, len(away_at))
        for place, at_column, value in ((following, 0, coupling.T), (element, 1, volume), (element, 2, coupling)):
            high, low = split(value)
            high_ref[place, :, at_column * size : (at_column + 1) * size] = high
            low_ref[place, :, at_column * size : (at_column + 1) * size] = low


def held_shape(rows, columns):
    return (rows, 2 * columns) if columns % 128 == 0 else (2, rows, columns)


def hold(held, at, value):
    high, low = split(value)
    size, columns = value.shape
    rows = slice(at * size, (at + 1) * size)
    if len(held.shape) == 2:
        held[rows, :columns] = high
        held[rows, columns:] = low
    else:
        held[0, rows] = high
        held[1, rows] = low


def apply_row(high, low, held, start, columns):
    rows = pl.ds(start, high.shape[1])
    if len(held.shape) == 2:
        if columns == 128:
            both = dot(high, held[rows, :])
            total = both[:, :columns] + both[:, columns:]
        else:
            total = dot(high, held[rows, :columns]) + dot(high, held[rows, columns:])
        return total + dot(low, held[rows, :columns])
    return dot(high, held[0, rows]) + (dot(high, held[1, rows]) + dot(low, held[0, rows]))


def advance(first, result, before):
    return result if first else 2.0 * result - before


def head_kernel(first, before, high, low, head, inner, below, old, out, held):
    size, columns = head.shape
    for at, value in enumerate((below[...], head[...], inner[0])):
        hold(held, at, value)
    before_high, before_low = split((before[...] * (1.0 / half_width)).T)
    row = apply_row(
        jnp.concatenate([before_high, high[0, :, size:]], axis=1), jnp.concatenate([before_low, low[0, :, size:]], axis=1), held, 0, columns
    )
    out[...] = advance(first, row, None if first else old[...])


def tail_kernel(first, high, low, tail, inner, above, old, out, held):
    for at, value in enumerate((inner[inner.shape[0] - 1], tail[...], above[...])):
        hold(held, at, value)
    last = high.shape[0] - 1
    row = apply_row(high[last], low[last], held, 0, tail.shape[1])
    out[...] = advance(first, row, None if first else old[...])


def inner_kernel(first, high, low, head, tail, inner, old, out, held):
    count, size, columns = inner.shape
    hold(held, 0, head[...])
    for at in range(count):
        hold(held, at + 1, inner[at])
    hold(held, count + 1, tail[...])

    @pl.loop(0, count)
    def _(at):
        row = apply_row(high[at + 1], low[at + 1], held, pl.multiple_of(at * size, size), columns)
        out[at] = advance(first, row, None if first else old[at])


def arrange_kernel(chunk, chunks, at_ref, vector_ref, got_ref, head_ref, tail_ref, inner_ref, sems):
    half, _, width = got_ref.shape
    side = at_ref[0]
    targets = [head_ref] + [inner_ref.at[at] for at in range(2 * half - 2)] + [tail_ref]

    def moved(act):
        for element, target in enumerate(targets):
            own = vector_ref.at[element % half]
            if vector_ref.shape[2] > width:
                start = pl.multiple_of((at_ref[0] * chunks + chunk) * width, width)
                own = vector_ref.at[element % half, :, pl.ds(start, width)]
            for source, mine in ((own, True), (got_ref.at[element % half], False)):

                @pl.when((side == element // half) == mine)
                def _():
                    act(pltpu.make_async_copy(source, target, sems.at[element]))

    moved(lambda copy: copy.start())
    moved(lambda copy: copy.wait())


def collect_kernel(count, chunks, side_ref, *refs):
    out_ref = refs[-1]
    step = pl.program_id(0)
    side = side_ref[0]
    at_end = step == side * (count - 1)
    for chunk in range(chunks):
        head_ref, tail_ref, inner_ref, got_end_ref, got_inner_ref = refs[5 * chunk : 5 * chunk + 5]
        end = jnp.where(side == 0, head_ref[...], tail_ref[...])
        mine = jnp.where(at_end, end, inner_ref[0])
        theirs = jnp.where(at_end, got_end_ref[...], got_inner_ref[0])
        width = mine.shape[1]
        first = chunk * width
        second = (chunks + chunk) * width
        out_ref[0, :, first : first + width] = jnp.where(side == 0, mine, theirs)
        out_ref[0, :, second : second + width] = jnp.where(side == 0, theirs, mine)


def whole(shape):
    return pl.BlockSpec(shape, lambda *steps: (0,) * len(shape))


def lead_and_cut(side, index, basis, vector, chunks, width):
    points, size = basis.shape[1:]
    count = vector.shape[0]
    return pl.pallas_call(
        lead_kernel,
        in_specs=[SCALARS, VMEM, ANY, ANY],
        out_specs=[VMEM] + [VMEM] * chunks,
        out_shape=[jax.ShapeDtypeStruct((size, index.shape[2]), jnp.float32)]
        + [jax.ShapeDtypeStruct((count, size, width), jnp.float32)] * chunks,
        scratch_shapes=[pltpu.VMEM((points, size), jnp.float32), pltpu.SemaphoreType.DMA((1 + chunks,))],
        compiler_params=PARAMS,
    )(side, index, basis, vector)


def blocks(core, index, quad, pairs, basis, applied, faces_total):
    count, points, size = basis.shape
    spots = index.shape[2]
    part = jax.ShapeDtypeStruct((count // 2, size + size // 2 + 8, size), jnp.float32)
    return pl.pallas_call(
        functools.partial(blocks_kernel, faces_total),
        in_specs=[SCALARS, VMEM, VMEM, VMEM, ANY, ANY],
        out_specs=[VMEM] * 3,
        out_shape=[part, part, jax.ShapeDtypeStruct((size, spots), jnp.float32)],
        scratch_shapes=[
            pltpu.VMEM((count, points, size), jnp.float32),
            pltpu.VMEM((count, points, size), jnp.float32),
            pltpu.VMEM((count, size, spots), jnp.float32),
            pltpu.SemaphoreType.DMA((2 * count,)),
        ],
        compiler_params=PARAMS,
    )(core, index, quad, pairs, basis, applied)


def last_coupling(core, pair, own, lead, send, keep, faces_total):
    size = own.shape[0]
    return pl.pallas_call(
        functools.partial(last_kernel, faces_total),
        in_specs=[SCALARS, VMEM, VMEM, VMEM, ANY, ANY],
        out_specs=[ANY] * 2,
        out_shape=[jax.ShapeDtypeStruct(send.shape, jnp.float32)] * 2,
        input_output_aliases={4: 0, 5: 1},
        scratch_shapes=[pltpu.VMEM((size, size), jnp.float32), pltpu.SemaphoreType.DMA],
        compiler_params=PARAMS,
    )(core, pair, own, lead, send, keep)


def weights(me, *parts):
    rows, size = parts[0].shape[1:]
    return pl.pallas_call(
        weights_kernel,
        in_specs=[SCALARS] + [ANY] * 6,
        out_specs=[VMEM] * 2,
        out_shape=[jax.ShapeDtypeStruct((8, size, 3 * size), jnp.bfloat16)] * 2,
        scratch_shapes=[pltpu.VMEM((8, rows, size), jnp.float32), pltpu.SemaphoreType.DMA((8,))],
        compiler_params=PARAMS,
    )(me, *parts)


def apply_head(first, before, high, low, head, inner, below, old):
    return pl.pallas_call(
        functools.partial(head_kernel, first),
        in_specs=[VMEM] * 7,
        out_specs=VMEM,
        out_shape=jax.ShapeDtypeStruct(head.shape, jnp.float32),
        scratch_shapes=[pltpu.VMEM(held_shape(3 * head.shape[0], head.shape[1]), jnp.bfloat16)],
        compiler_params=PARAMS,
    )(before, high, low, head, inner, below, old)


def apply_tail(first, high, low, tail, inner, above, old):
    return pl.pallas_call(
        functools.partial(tail_kernel, first),
        in_specs=[VMEM] * 6,
        out_specs=VMEM,
        out_shape=jax.ShapeDtypeStruct(tail.shape, jnp.float32),
        scratch_shapes=[pltpu.VMEM(held_shape(3 * tail.shape[0], tail.shape[1]), jnp.bfloat16)],
        compiler_params=PARAMS,
    )(high, low, tail, inner, above, old)


def apply_inner(first, high, low, head, tail, inner, old):
    return pl.pallas_call(
        functools.partial(inner_kernel, first),
        in_specs=[VMEM] * 6,
        out_specs=VMEM,
        out_shape=jax.ShapeDtypeStruct(inner.shape, jnp.float32),
        scratch_shapes=[pltpu.VMEM(held_shape((inner.shape[0] + 2) * inner.shape[1], inner.shape[2]), jnp.bfloat16)],
        compiler_params=PARAMS,
    )(high, low, head, tail, inner, old)


def arranged(at, vector, got, chunk):
    half, size, columns = got.shape
    chunks = max(vector.shape[2] // 2 // columns, 1)
    return pl.pallas_call(
        functools.partial(arrange_kernel, chunk, chunks),
        in_specs=[SCALARS, ANY, ANY],
        out_specs=[VMEM] * 3,
        out_shape=[jax.ShapeDtypeStruct((size, columns), jnp.float32)] * 2
        + [jax.ShapeDtypeStruct((2 * half - 2, size, columns), jnp.float32)],
        scratch_shapes=[pltpu.SemaphoreType.DMA((2 * half,))],
        compiler_params=PARAMS,
    )(at, vector, got)


def collected(side, parts):
    size, width = parts[0][0].shape
    chunks = len(parts)
    half = parts[0][4].shape[0] + 1
    spot = lambda s, o: jnp.where(o[0] == 0, jnp.maximum(s - 1, 0), jnp.minimum(s, half - 2))
    flat = pl.BlockSpec((size, width), lambda s, o: (0, 0))
    return pl.pallas_call(
        functools.partial(collect_kernel, half, chunks),
        grid_spec=pltpu.PrefetchScalarGridSpec(
            num_scalar_prefetch=1,
            grid=(half,),
            in_specs=[
                flat,
                flat,
                pl.BlockSpec((1, size, width), lambda s, o: (o[0] * (half - 1) + spot(s, o), 0, 0)),
                flat,
                pl.BlockSpec((1, size, width), lambda s, o: (spot(s, o), 0, 0)),
            ]
            * chunks,
            out_specs=pl.BlockSpec((1, size, 2 * chunks * width), lambda s, o: (s, 0, 0)),
        ),
        out_shape=jax.ShapeDtypeStruct((half, size, 2 * chunks * width), jnp.float32),
        compiler_params=PARAMS,
    )(side, *[value for part in parts for value in part])


def flipped(value, axis, bit):
    count = lax.axis_size(axis)
    return lax.ppermute(value, axis, [(i, i ^ bit) for i in range(count)])


def shifted(value, axis, steps):
    count = lax.axis_size(axis)
    return lax.ppermute(value, axis, [(i, (i + steps) % count) for i in range(count)])


def body(basis, applied, quad, face_index, face_pairing, orbitals):
    count, points, size = basis.shape
    spots = face_index.shape[2]
    columns = orbitals.shape[1]
    chunks = 2 if columns % 512 == 0 else 1
    elems, width = lax.axis_size("elem"), lax.axis_size("pts")
    faces_total = float(spots * width)
    side = lax.axis_index("elem") % 2
    core = lax.axis_index("pts") % 2
    lane = lax.axis_index("pts") // 2 % 2
    side_at = side.reshape(1).astype(jnp.int32)
    vector = orbitals.reshape(count, size, columns)

    lead_index = face_index[:1, 0:2].reshape(1, 1, 2 * spots)
    part = columns // 2 // chunks
    own = foreign = vector
    if part % 128:
        own = lax.dynamic_slice_in_dim(vector, side * part, part, axis=2)
        foreign = lax.dynamic_slice_in_dim(vector, (1 - side) * part, part, axis=2)
    lead, *foreign = lead_and_cut(1 - side_at, lead_index, basis, foreign, chunks, part)
    lead = shifted(lead, "elem", -1)
    got = [flipped(value, "elem", 1) for value in foreign]

    index = jnp.stack([face_index[:, 0], face_index[:, 2], face_index[:, 1], face_index[:, 3]], axis=1)
    index = index.reshape(count, 1, 4 * spots)
    pairs = jnp.concatenate([jnp.full_like(face_pairing, -points), face_pairing], axis=1).reshape(count, 1, 2 * spots)
    core_at = core.reshape(1).astype(jnp.int32)
    send, keep, last = blocks(core_at, index, quad.reshape(count, 1, points), pairs, basis, applied, faces_total)
    send, keep = last_coupling(core_at, pairs[-1], last, lead, send, keep, faces_total)
    half = count // 2

    state, belows, aboves = [], [], []

    def arrange(chunk, received):
        state.append(arranged(side_at, own, received, chunk))
        belows.append(shifted(state[chunk][1], "elem", 2))
        aboves.append(shifted(state[chunk][0], "elem", -2))


    other = flipped(send, "pts", 1)
    quarter = half // 2
    pick = lambda value, at: lax.dynamic_slice_in_dim(value, at * quarter, quarter)
    send = pick(keep, 1 - lane) + pick(other, 1 - lane)
    mine = pick(keep, lane) + pick(other, lane) + flipped(send, "pts", 2)
    bit = 4
    while bit < width:
        mine = mine + flipped(mine, "pts", bit)
        bit *= 2
    got[0], mine = lax.optimization_barrier((got[0], mine))
    arrange(0, got[0])
    beside = flipped(mine, "pts", 2)
    across = flipped(mine, "elem", 1)
    belows[0], aboves[0], across = lax.optimization_barrier((belows[0], aboves[0], across))
    both = flipped(across, "pts", 2)
    near = flipped(jnp.concatenate([mine, beside, across]), "pts", 1)
    if chunks > 1:
        got[1], both = lax.optimization_barrier((got[1], both))
        arrange(1, got[1])
    far = flipped(both, "pts", 1)

    last = jnp.where(
        side == 1, jnp.where(lane == 1, mine[0, :size], beside[0, :size]), jnp.where(lane == 1, across[0, :size], both[0, :size])
    )
    flat = lambda e, p: e % elems * width + p
    odd = [(e, p) for e in range(elems) for p in range(1, width, 2)]
    before = lax.ppermute(last, ("elem", "pts"), [(flat(e, p), flat(e + 2, p)) for e, p in odd])
    before = before + lax.ppermute(before, ("elem", "pts"), [(flat(e, p), flat(e, p - 1)) for e, p in odd])

    me = (side * 4 + core * 2 + lane).reshape(1).astype(jnp.int32)
    high, low = weights(me, mine, beside, across, both, near, far)

    old = list(state)
    parts = []
    for degree in range(DEG):
        first = degree == 0
        for c in range(chunks):
            head, tail, inner = state[c]
            new_tail = apply_tail(first, high, low, tail, inner, aboves[c], old[c][1])
            new_head = apply_head(first, before, high, low, head, inner, belows[c], old[c][0])
            new_inner = apply_inner(first, high, low, head, tail, inner, old[c][2])
            old[c] = state[c]
            state[c] = new_head, new_tail, new_inner
            if degree < DEG - 1:
                belows[c] = shifted(new_tail, "elem", 2)
                aboves[c] = shifted(new_head, "elem", -2)
            else:
                foreign = lax.dynamic_slice_in_dim(new_inner, (1 - side) * (count - 1), count - 1)
                got_inner = flipped(foreign, "elem", 1)
                got_end = flipped(jnp.where(side == 0, new_tail, new_head), "elem", 1)
                parts.append((new_head, new_tail, new_inner, got_end, got_inner))
    return collected(side_at, parts).reshape(count * size, columns)


def solution(mesh):
    return jax.shard_map(
        body,
        mesh=mesh,
        in_specs=(
            P("elem", "pts", None),
            P("elem", "pts", None),
            P("elem", "pts"),
            P("elem", None, "pts"),
            P("elem", "pts"),
            P("elem", "pts"),
        ),
        out_specs=P("elem", "pts"),
        check_vma=False,
    )
```

```python
import functools

import jax
import jax.numpy as jnp
from jax import lax
from jax.experimental import pallas as pl
from jax.experimental.pallas import tpu as pltpu
from jax.sharding import PartitionSpec as P

NB = 256
DEG = 4

penalty = 3.0
center = 4.0
half_width = 12.0

PARAMS = pltpu.CompilerParams(vmem_limit_bytes=12 * 1024 * 1024)
SCALARS = pl.BlockSpec(memory_space=pltpu.SMEM)
ANY = pl.BlockSpec(memory_space=pl.ANY)


def near_core(shape, dtype=jnp.float32):
    return pltpu.VMEM(shape, dtype)


def far_off(value):
    return pltpu.with_memory_space_constraint(value, pltpu.MemorySpace.HBM)


def close_by(value):
    return pltpu.with_memory_space_constraint(value, pltpu.MemorySpace.VMEM)
VMEM = pl.BlockSpec(memory_space=pltpu.VMEM)
NN = (((1,), (0,)), ((), ()))
NT = (((1,), (1,)), ((), ()))


def split(value):
    high = value.astype(jnp.bfloat16)
    low = (value - high.astype(jnp.float32)).astype(jnp.bfloat16)
    return high, low


def dot(first, second, dims=NN):
    return lax.dot_general(first, second, dims, preferred_element_type=jnp.float32)


def dot3(first, second, dims=NN):
    first_high, first_low = first
    second_high, second_low = second
    return dot(first_high, second_high, dims) + (dot(first_high, second_low, dims) + dot(first_low, second_high, dims))


def picked(parts, chosen):
    return dot(parts[0], chosen) + dot(parts[1], chosen)


def one_hot(index_row, rows, offset=0):
    at = lax.broadcasted_iota(jnp.int32, (rows, index_row.shape[1]), 0) - offset
    return (at == index_row).astype(jnp.float32).astype(jnp.bfloat16)


def lead_kernel(side_ref, index_ref, basis_ref, vector_ref, traces_ref, *rest):
    cut_refs, (held, sems) = rest[:-2], rest[-2:]
    first = pltpu.make_async_copy(basis_ref.at[0], held, sems.at[0])
    first.start()
    width = cut_refs[0].shape[2]
    copies = []
    for at, out_ref in enumerate(cut_refs):
        source = vector_ref
        if vector_ref.shape[2] > width:
            start = pl.multiple_of((side_ref[0] * len(cut_refs) + at) * width, width)
            source = vector_ref.at[:, :, pl.ds(start, width)]
        copies.append(pltpu.make_async_copy(source, out_ref, sems.at[1 + at]))
        copies[-1].start()
    first.wait()
    traces_ref[...] = picked(split(held[...].T), one_hot(index_ref[0], held.shape[0]))
    for copy in copies:
        copy.wait()


def blocks_kernel(
    faces_total, core_ref, index_ref, quad_ref, pair_ref, basis_ref, applied_ref, send_ref, keep_ref, last_ref, held, acted, traces, sems
):
    count = basis_ref.shape[0]
    size = basis_ref.shape[2]
    half = size // 2
    core = core_ref[0]

    def copies(at):
        return (
            pltpu.make_async_copy(basis_ref.at[at], held.at[at], sems.at[2 * at]),
            pltpu.make_async_copy(applied_ref.at[at], acted.at[at], sems.at[2 * at + 1]),
        )

    for at in range(count):
        for copy in copies(at):
            copy.start()

    def store(element, rows, value):
        @pl.when(element // (count // 2) == core)
        def _():
            keep_ref[element % (count // 2), rows] = value

        @pl.when(element // (count // 2) != core)
        def _():
            send_ref[element % (count // 2), rows] = value

    @pl.loop(0, count)
    def _(at):
        for copy in copies(at):
            copy.wait()
        turned = held[at].T
        found = picked(split(turned), one_hot(index_ref[at], held.shape[1]))
        traces[at] = found
        width = found.shape[1] // 2
        outer, layer = found[:, :width], found[:, width:]
        total = dot3(split(turned * quad_ref[at]), split(acted[at]))
        total = total + dot3(split((2.0 * outer + layer) * (1.0 / faces_total)), split(outer), NT)
        mixed, side, diagonal = packed(0.5 * (total + total.T))
        store(at, slice(size, size + half), jnp.concatenate([mixed, side], axis=1))
        store(at, slice(size + half, None), jnp.broadcast_to(jnp.concatenate([diagonal, diagonal], axis=1), (8, size)))

    @pl.loop(0, count - 1)
    def _(at):
        following = traces[at + 1]
        width = following.shape[1] // 2
        order = one_hot(pair_ref[at], width)
        face, inside = picked(split(following[:, :width]), order), picked(split(following[:, width:]), order)
        store(at, slice(0, size), coupled(traces[at], face, inside, faces_total))

    last_ref[...] = traces[count - 1]


def coupled(own, face, inside, faces_total):
    width = own.shape[1] // 2
    outer, layer = own[:, :width], own[:, width:]
    near = split((penalty * outer + 0.5 * layer) * (-1.0 / faces_total))
    far = split(outer * (0.5 / faces_total))
    return dot3(near, split(face), NT) + dot3(far, split(inside), NT)


def last_kernel(faces_total, core_ref, pair_ref, own_ref, lead_ref, send_in, keep_in, send_ref, keep_ref, block, sem):
    width = own_ref.shape[1] // 2
    lead = split(lead_ref[...])
    face = picked(lead, one_hot(pair_ref[...], width))
    inside = picked(lead, one_hot(pair_ref[...], width, width // 2))
    block[...] = coupled(own_ref[...], face, inside, faces_total)
    at = send_ref.shape[0] - 1
    rows = pl.ds(0, block.shape[0])
    for core, ref in ((0, send_ref), (1, keep_ref)):

        @pl.when(core_ref[0] == core)
        def _():
            copy = pltpu.make_async_copy(block, ref.at[at, rows], sem)
            copy.start()
            copy.wait()


def packed(volume):
    half = volume.shape[0] // 2
    row = lax.broadcasted_iota(jnp.int32, (half, half), 0)
    column = lax.broadcasted_iota(jnp.int32, (half, half), 1)
    corner = volume[half:, half:]
    mixed = jnp.where(column >= row, volume[:half, :half], corner)
    diagonal = jnp.sum(jnp.where(column == row, corner, 0.0), axis=0, keepdims=True)
    return mixed, volume[:half, half:], diagonal


def unpacked(mixed, side, diagonal):
    half = mixed.shape[0]
    row = lax.broadcasted_iota(jnp.int32, (half, half), 0)
    column = lax.broadcasted_iota(jnp.int32, (half, half), 1)
    turned = mixed.T
    first = jnp.where(column >= row, mixed, turned)
    corner = jnp.where(column < row, mixed, jnp.where(column == row, diagonal, turned))
    top = jnp.concatenate([first, side], axis=1)
    return jnp.concatenate([top, jnp.concatenate([side.T, corner], axis=1)], axis=0)


def weights_kernel(me_ref, *refs):
    sources, (high_ref, low_ref), held, sems = refs[:8], refs[8:10], refs[10], refs[11]
    me = me_ref[0]
    size = held.shape[2]
    half = size // 2
    away_at = (0, 2, 1, 4, 3, 6, 5, 7)
    copies = [pltpu.make_async_copy(source.at[0], held.at[n], sems.at[n]) for n, source in enumerate(sources)]
    for copy in copies:
        copy.start()
    row = lax.broadcasted_iota(jnp.int32, (size, size), 0)
    diagonal = row == lax.broadcasted_iota(jnp.int32, (size, size), 1)

    for n, away in enumerate(away_at):
        copies[n].wait()
        element = away ^ me
        following = lax.rem(element + 1, len(away_at))
        volume, coupling = scaled(held[n], diagonal)
        for place, at, value in ((following, 0, coupling.T), (element, 1, volume), (element, 2, coupling)):
            high_ref[place, :, at * size : (at + 1) * size], low_ref[place, :, at * size : (at + 1) * size] = split(value)


def scaled(block, diagonal):
    size = block.shape[1]
    half = size // 2
    volume = unpacked(block[size : size + half, :half], block[size : size + half, half:], block[size + half : size + half + 1, :half])
    return (volume - jnp.where(diagonal, center, 0.0)) * (1.0 / half_width), block[:size] * (1.0 / half_width)


def outer_kernel(core_ref, first_ref, second_ref, swapped_ref, high_in, low_in, high_ref, low_ref):
    size = first_ref.shape[2]
    row = lax.broadcasted_iota(jnp.int32, (size, size), 0)
    diagonal = row == lax.broadcasted_iota(jnp.int32, (size, size), 1)
    kept = first_ref[0] + second_ref[0]
    core = core_ref[0]
    prior = jnp.where(core == 1, kept[:size], swapped_ref[0, :size]) * (1.0 / half_width)
    volume, coupling = scaled(jnp.where(core == 1, swapped_ref[0], kept), diagonal)
    last = high_in.shape[0] - 1
    high_ref[0, :, size:] = high_in[0, :, size:]
    low_ref[0, :, size:] = low_in[0, :, size:]
    high_ref[0, :, :size], low_ref[0, :, :size] = split(prior.T)
    turned = (high_in[last, :, 2 * size :].astype(jnp.float32) + low_in[last, :, 2 * size :].astype(jnp.float32)).T
    for at, value in enumerate((turned, volume, coupling)):
        high_ref[1, :, at * size : (at + 1) * size], low_ref[1, :, at * size : (at + 1) * size] = split(value)


def held_shape(rows, columns):
    return (rows, 2 * columns) if columns % 128 == 0 else (2, rows, columns)


def hold(held, at, value):
    high, low = split(value)
    size, columns = value.shape
    rows = slice(at * size, (at + 1) * size)
    if len(held.shape) == 2:
        held[rows, :columns] = high
        held[rows, columns:] = low
    else:
        held[0, rows] = high
        held[1, rows] = low


def apply_row(high, low, held, start, columns):
    rows = pl.ds(start, high.shape[1])
    if len(held.shape) == 2:
        if columns == 128:
            both = dot(high, held[rows, :])
            total = both[:, :columns] + both[:, columns:]
        else:
            total = dot(high, held[rows, :columns]) + dot(high, held[rows, columns:])
        return total + dot(low, held[rows, :columns])
    return dot(high, held[0, rows]) + (dot(high, held[1, rows]) + dot(low, held[0, rows]))


def advance(first, result, before):
    return result if first else 2.0 * result - before


def edge_kernel(first, up, high, low, high_outer, low_outer, inner, halo, old, out, held):
    size, columns = inner.shape[1:]
    count = inner.shape[0]
    local = (inner[count - 2], inner[count - 1]) if up else (inner[0], inner[1])
    beyond = (halo[0], halo[1])
    for at, value in enumerate(local + beyond if up else beyond + local):
        hold(held, at, value)
    last = high.shape[0] - 1
    rows = ((high[last], low[last]), (high_outer[1], low_outer[1])) if up else ((high_outer[0], low_outer[0]), (high[1], low[1]))
    for at, (part_high, part_low) in enumerate(rows):
        row = apply_row(part_high, part_low, held, at * size, columns)
        out[at] = advance(first, row, None if first else old[at])


def inner_kernel(first, up, high, low, edge, inner, old, out, held):
    count, size, columns = inner.shape
    for at in range(2):
        hold(held, at if up else count + at, edge[at])
    for at in range(count):
        hold(held, at + 2 if up else at, inner[at])

    @pl.loop(0, count)
    def _(at):
        place = at + (1 if up else 2)
        row = apply_row(high[place], low[place], held, pl.multiple_of(at * size, size), columns)
        out[at] = advance(first, row, None if first else old[at])


def fold_kernel(lane_ref, keep_ref, other_ref, send_ref, stay_ref):
    lane = lane_ref[0]
    half = keep_ref.shape[0] // 2
    for at in range(half):
        send_ref[at] = keep_ref[(1 - lane) * half + at] + other_ref[(1 - lane) * half + at]
        stay_ref[at] = keep_ref[lane * half + at] + other_ref[lane * half + at]


def sum_kernel(first_ref, second_ref, out_ref):
    out_ref[...] = first_ref[...] + second_ref[...]


def arrange_kernel(chunk, chunks, side_ref, vector_ref, got_ref, edge_ref, inner_ref, sems):
    half, _, width = got_ref.shape
    side = side_ref[0]
    targets = [edge_ref.at[0], edge_ref.at[1]] + [inner_ref.at[at] for at in range(2 * half - 2)]

    def moved(act):
        for element, target in enumerate(targets):
            own = vector_ref.at[element % half]
            if vector_ref.shape[2] > width:
                start = pl.multiple_of((side * chunks + chunk) * width, width)
                own = vector_ref.at[element % half, :, pl.ds(start, width)]
            for source, mine in ((own, True), (got_ref.at[element % half], False)):

                @pl.when((side == element // half) == mine)
                def _():
                    act(pltpu.make_async_copy(source, target, sems.at[element]))

    moved(lambda copy: copy.start())
    moved(lambda copy: copy.wait())


def place_pairs(out_ref, sems, side, chunks, chunk, width, pairs):
    def moved(act):
        for at, (wanted, source, element, foreign) in enumerate(pairs):

            @pl.when(side == wanted)
            def _():
                part = 1 - side if foreign else side
                start = pl.multiple_of((part * chunks + chunk) * width, width)
                act(pltpu.make_async_copy(source, out_ref.at[pl.ds(element, 2), :, pl.ds(start, width)], sems.at[chunk, at]))

    return moved


def collect_kernel(chunks, side_ref, *refs):
    sources, out_ref, sems = refs[: 3 * chunks], refs[-2], refs[-1]
    acts = []
    for chunk in range(chunks):
        edge, inner, near = sources[3 * chunk : 3 * chunk + 3]
        pairs = (
            (0, edge, 0, False),
            (0, inner.at[pl.ds(0, 2)], 2, False),
            (0, near, 2, True),
            (1, inner.at[pl.ds(2, 2)], 0, False),
            (1, inner.at[pl.ds(4, 2)], 2, False),
            (1, near, 0, True),
        )
        acts.append(place_pairs(out_ref, sems, side_ref[0], chunks, chunk, edge.shape[2], pairs))
    for act in acts:
        act(lambda copy: copy.start())
    for act in acts:
        act(lambda copy: copy.wait())


def finish_kernel(chunks, side_ref, *refs):
    sources, out_ref, sems = refs[:chunks], refs[-2], refs[-1]
    acts = []
    for chunk, far in enumerate(sources):
        pairs = ((0, far, 0, True), (1, far, 2, True))
        acts.append(place_pairs(out_ref, sems, side_ref[0], chunks, chunk, far.shape[2], pairs))
    for act in acts:
        act(lambda copy: copy.start())
    for act in acts:
        act(lambda copy: copy.wait())


def lead_and_cut(side, index, basis, vector, chunks, width):
    points, size = basis.shape[1:]
    count = vector.shape[0]
    return pl.pallas_call(
        lead_kernel,
        in_specs=[SCALARS, VMEM, ANY, ANY],
        out_specs=[VMEM] + [VMEM] * chunks,
        out_shape=[jax.ShapeDtypeStruct((size, index.shape[2]), jnp.float32)]
        + [jax.ShapeDtypeStruct((count, size, width), jnp.float32)] * chunks,
        scratch_shapes=[pltpu.VMEM((points, size), jnp.float32), pltpu.SemaphoreType.DMA((1 + chunks,))],
        compiler_params=PARAMS,
    )(side, index, far_off(basis), far_off(vector))


def blocks(core, index, quad, pairs, basis, applied, faces_total):
    count, points, size = basis.shape
    spots = index.shape[2]
    part = near_core((count // 2, size + size // 2 + 8, size))
    return pl.pallas_call(
        functools.partial(blocks_kernel, faces_total),
        in_specs=[SCALARS, VMEM, VMEM, VMEM, ANY, ANY],
        out_specs=[VMEM] * 3,
        out_shape=[part, part, near_core((size, spots))],
        scratch_shapes=[
            pltpu.VMEM((count, points, size), jnp.float32),
            pltpu.VMEM((count, points, size), jnp.float32),
            pltpu.VMEM((count, size, spots), jnp.float32),
            pltpu.SemaphoreType.DMA((2 * count,)),
        ],
        compiler_params=PARAMS,
    )(core, index, quad, pairs, far_off(basis), far_off(applied))


def last_coupling(core, pair, own, lead, send, keep, faces_total):
    size = own.shape[0]
    return pl.pallas_call(
        functools.partial(last_kernel, faces_total),
        in_specs=[SCALARS, VMEM, VMEM, VMEM, ANY, ANY],
        out_specs=[ANY] * 2,
        out_shape=[near_core(send.shape)] * 2,
        input_output_aliases={4: 0, 5: 1},
        scratch_shapes=[pltpu.VMEM((size, size), jnp.float32), pltpu.SemaphoreType.DMA],
        compiler_params=PARAMS,
    )(core, pair, own, lead, send, keep)


def weights(me, *parts):
    rows, size = parts[0].shape[1:]
    return pl.pallas_call(
        weights_kernel,
        in_specs=[SCALARS] + [ANY] * 8,
        out_specs=[VMEM] * 2,
        out_shape=[near_core((8, size, 3 * size), jnp.bfloat16)] * 2,
        scratch_shapes=[pltpu.VMEM((8, rows, size), jnp.float32), pltpu.SemaphoreType.DMA((8,))],
        compiler_params=PARAMS,
    )(me, *parts)


def outer_weights(core, first, second, swapped, high, low):
    size = first.shape[2]
    return pl.pallas_call(
        outer_kernel,
        in_specs=[SCALARS] + [VMEM] * 5,
        out_specs=[VMEM] * 2,
        out_shape=[near_core((2, size, 3 * size), jnp.bfloat16)] * 2,
        compiler_params=PARAMS,
    )(core, first, second, swapped, high, low)


def apply_edge(first, up, high, low, high_outer, low_outer, inner, halo, old):
    _, size, columns = inner.shape
    return pl.pallas_call(
        functools.partial(edge_kernel, first, up),
        in_specs=[VMEM] * 7,
        out_specs=VMEM,
        out_shape=near_core(halo.shape),
        scratch_shapes=[pltpu.VMEM(held_shape(4 * size, columns), jnp.bfloat16)],
        compiler_params=PARAMS,
    )(high, low, high_outer, low_outer, inner, close_by(halo), old)


def apply_inner(first, up, high, low, edge, inner, old):
    count, size, columns = inner.shape
    return pl.pallas_call(
        functools.partial(inner_kernel, first, up),
        in_specs=[VMEM] * 5,
        out_specs=VMEM,
        out_shape=near_core(inner.shape),
        scratch_shapes=[pltpu.VMEM(held_shape((count + 2) * size, columns), jnp.bfloat16)],
        compiler_params=PARAMS,
    )(high, low, edge, inner, old)


def folded(lane, keep, other):
    shape = (keep.shape[0] // 2, *keep.shape[1:])
    return pl.pallas_call(
        fold_kernel,
        in_specs=[SCALARS, VMEM, VMEM],
        out_specs=[VMEM] * 2,
        out_shape=[near_core(shape)] * 2,
        compiler_params=PARAMS,
    )(lane, keep, close_by(other))


def added(first, second):
    return pl.pallas_call(
        sum_kernel, in_specs=[VMEM] * 2, out_specs=VMEM, out_shape=near_core(first.shape), compiler_params=PARAMS
    )(first, close_by(second))


def arranged(side, vector, got, chunk):
    half, size, columns = got.shape
    chunks = max(vector.shape[2] // 2 // columns, 1)
    return pl.pallas_call(
        functools.partial(arrange_kernel, chunk, chunks),
        in_specs=[SCALARS, ANY, ANY],
        out_specs=[VMEM] * 2,
        out_shape=[near_core((2, size, columns)), near_core((2 * half - 2, size, columns))],
        scratch_shapes=[pltpu.SemaphoreType.DMA((2 * half,))],
        compiler_params=PARAMS,
    )(side, far_off(vector), got)


def collected(side, parts):
    count = 4
    _, size, width = parts[0][0].shape
    chunks = len(parts)
    return pl.pallas_call(
        functools.partial(collect_kernel, chunks),
        in_specs=[SCALARS] + [ANY] * (3 * chunks),
        out_specs=ANY,
        out_shape=jax.ShapeDtypeStruct((count, size, 2 * chunks * width), jnp.float32),
        scratch_shapes=[pltpu.SemaphoreType.DMA((chunks, 6))],
        compiler_params=PARAMS,
    )(side, *[value for part in parts for value in part])


def finished(side, parts, result):
    chunks = len(parts)
    return pl.pallas_call(
        functools.partial(finish_kernel, chunks),
        in_specs=[SCALARS] + [ANY] * (chunks + 1),
        out_specs=ANY,
        out_shape=jax.ShapeDtypeStruct(result.shape, jnp.float32),
        input_output_aliases={1 + chunks: 0},
        scratch_shapes=[pltpu.SemaphoreType.DMA((chunks, 2))],
        compiler_params=PARAMS,
    )(side, *parts, result)


def flipped(value, axis, bit):
    count = lax.axis_size(axis)
    return lax.ppermute(value, axis, [(i, i ^ bit) for i in range(count)])


def shifted(value, axis, steps):
    count = lax.axis_size(axis)
    return lax.ppermute(value, axis, [(i, (i + steps) % count) for i in range(count)])


def body(basis, applied, quad, face_index, face_pairing, orbitals):
    count, points, size = basis.shape
    spots = face_index.shape[2]
    columns = orbitals.shape[1]
    chunks = 2 if columns % 512 == 0 else 1
    elems, width = lax.axis_size("elem"), lax.axis_size("pts")
    faces_total = float(spots * width)
    side = lax.axis_index("elem") % 2
    core = lax.axis_index("pts") % 2
    lane = lax.axis_index("pts") // 2 % 2
    side_at = side.reshape(1).astype(jnp.int32)
    vector = orbitals.reshape(count, size, columns)

    lead_index = face_index[:1, 0:2].reshape(1, 1, 2 * spots)
    part = columns // 2 // chunks
    own = foreign = vector
    if part % 128:
        own = lax.dynamic_slice_in_dim(vector, side * part, part, axis=2)
        foreign = lax.dynamic_slice_in_dim(vector, (1 - side) * part, part, axis=2)
    lead, *foreign = lead_and_cut(1 - side_at, lead_index, basis, foreign, chunks, part)
    lead = shifted(lead, "elem", -1)
    got = [flipped(value, "elem", 1) for value in foreign]

    index = jnp.stack([face_index[:, 0], face_index[:, 2], face_index[:, 1], face_index[:, 3]], axis=1)
    index = index.reshape(count, 1, 4 * spots)
    pairs = jnp.concatenate([jnp.full_like(face_pairing, -points), face_pairing], axis=1).reshape(count, 1, 2 * spots)
    core_at = core.reshape(1).astype(jnp.int32)
    send, keep, last = blocks(core_at, index, quad.reshape(count, 1, points), pairs, basis, applied, faces_total)
    send, keep = last_coupling(core_at, pairs[-1], last, lead, send, keep, faces_total)
    half = count // 2

    lane_at = lane.reshape(1).astype(jnp.int32)
    send, stay = folded(lane_at, keep, flipped(send, "pts", 1))
    mine = added(stay, flipped(send, "pts", 2))
    bit = 4
    while bit < width:
        mine = mine + flipped(mine, "pts", bit)
        bit *= 2
    got[0], mine = lax.optimization_barrier((got[0], mine))
    state, halos = [], []

    def arrange(chunk):
        state.append(arranged(side_at, own, got[chunk], chunk))
        halos.append(shifted(state[chunk][0], "elem", -2))

    arrange(0)
    beside = flipped(mine, "pts", 2)
    across = flipped(mine, "elem", 1)
    mine_near = flipped(mine, "pts", 1)
    halos[0], across = lax.optimization_barrier((halos[0], across))
    both = flipped(across, "pts", 2)
    beside_near = flipped(beside, "pts", 1)
    across_near = flipped(across, "pts", 1)

    last = jnp.where(lane == core, mine, beside)
    flat = lambda e, p: e % elems * width + p
    holds = [(e, p) for e in range(elems) for p in range(width) if e % 2 == p % 2]
    outer = lax.ppermute(last, ("elem", "pts"), [(flat(e, p), flat(e + (2 if p % 2 else -2), p)) for e, p in holds])
    outer_side = lax.ppermute(outer, ("elem", "pts"), [(flat(e, p), flat(e ^ 1, p)) for e, p in holds])
    outer_near = flipped(outer + outer_side, "pts", 1)

    if chunks > 1:
        got[1], both = lax.optimization_barrier((got[1], both))
        arrange(1)
    both_near = flipped(both, "pts", 1)

    me = (side * 4 + core * 2 + lane).reshape(1).astype(jnp.int32)
    high, low = weights(me, mine, mine_near, beside, across, beside_near, across_near, both, both_near)
    high_outer, low_outer = outer_weights(core_at, outer, outer_side, outer_near, high, low)

    old = list(state)
    near, far = [], []
    for degree in range(DEG):
        first, up = degree == 0, degree % 2 == 0
        for c in range(chunks):
            edge, inner = state[c]
            new_inner = apply_inner(first, up, high, low, edge, inner, old[c][1])
            if degree == DEG - 1:
                near.append(flipped(jnp.where(side == 0, new_inner[2:4], new_inner[:2]), "elem", 1))
                near[c], halos[c] = lax.optimization_barrier((near[c], halos[c]))
            new_edge = apply_edge(first, up, high, low, high_outer, low_outer, inner, halos[c], old[c][0])
            old[c] = state[c]
            state[c] = new_edge, new_inner
            if degree < DEG - 1:
                halos[c] = shifted(new_edge, "elem", 2 if up else -2)
            else:
                far.append(flipped(jnp.where(side == 0, new_inner[4:], new_edge), "elem", 1))
    if part % 128:
        (edge, inner), near, far = state[0], near[0], far[0]
        lower = jnp.concatenate([edge, inner[:2]])
        mine = jnp.where(side == 0, lower, inner[2:])
        theirs = jnp.where(side == 0, jnp.concatenate([far, near]), jnp.concatenate([near, far]))
        swap = lambda first, second: jnp.concatenate([first, second], axis=2)
        result = jnp.where(side == 0, swap(mine, theirs), swap(theirs, mine))
    else:
        result = collected(side_at, [(*state[c], near[c]) for c in range(chunks)])
        result = finished(side_at, far, result)
    return result.reshape(count * size, columns)


def solution(mesh):
    return jax.shard_map(
        body,
        mesh=mesh,
        in_specs=(
            P("elem", "pts", None),
            P("elem", "pts", None),
            P("elem", "pts"),
            P("elem", None, "pts"),
            P("elem", "pts"),
            P("elem", "pts"),
        ),
        out_specs=P("elem", "pts"),
        check_vma=False,
    )
```

```python
import functools

import jax
import jax.numpy as jnp
from jax import lax
from jax.experimental import pallas as pl
from jax.experimental.pallas import tpu as pltpu
from jax.sharding import PartitionSpec as P

NB = 256
DEG = 4

penalty = 3.0
center = 4.0
half_width = 12.0

PARAMS = pltpu.CompilerParams(vmem_limit_bytes=12 * 1024 * 1024)
SCALARS = pl.BlockSpec(memory_space=pltpu.SMEM)
ANY = pl.BlockSpec(memory_space=pl.ANY)


def near_core(shape, dtype=jnp.float32):
    return pltpu.VMEM(shape, dtype)


def far_off(value):
    return pltpu.with_memory_space_constraint(value, pltpu.MemorySpace.HBM)


def close_by(value):
    return pltpu.with_memory_space_constraint(value, pltpu.MemorySpace.VMEM)
VMEM = pl.BlockSpec(memory_space=pltpu.VMEM)
NN = (((1,), (0,)), ((), ()))
NT = (((1,), (1,)), ((), ()))


def split(value):
    high = value.astype(jnp.bfloat16)
    low = (value - high.astype(jnp.float32)).astype(jnp.bfloat16)
    return high, low


def dot(first, second, dims=NN):
    return lax.dot_general(first, second, dims, preferred_element_type=jnp.float32)


def dot3(first, second, dims=NN):
    first_high, first_low = first
    second_high, second_low = second
    return dot(first_high, second_high, dims) + (dot(first_high, second_low, dims) + dot(first_low, second_high, dims))


def picked(parts, chosen):
    return dot(parts[0], chosen) + dot(parts[1], chosen)


def one_hot(index_row, rows, offset=0):
    at = lax.broadcasted_iota(jnp.int32, (rows, index_row.shape[1]), 0) - offset
    return (at == index_row).astype(jnp.float32).astype(jnp.bfloat16)


def lead_kernel(side_ref, index_ref, basis_ref, vector_ref, traces_ref, *rest):
    cut_refs, (held, sems) = rest[:-2], rest[-2:]
    first = pltpu.make_async_copy(basis_ref.at[0], held, sems.at[0])
    first.start()
    half = cut_refs[-1].shape[2]
    copies = []
    for at, out_ref in enumerate(cut_refs):
        width = out_ref.shape[2]
        element = 0 if at < len(cut_refs) - 1 else 2
        source = vector_ref.at[pl.ds(element, 2)]
        if vector_ref.shape[2] > half:
            first_column = pl.multiple_of(side_ref[0] * half, half) + (at * width if element == 0 else 0)
            source = vector_ref.at[pl.ds(element, 2), :, pl.ds(pl.multiple_of(first_column, width), width)]
        copies.append(pltpu.make_async_copy(source, out_ref, sems.at[1 + at]))
        copies[-1].start()
    first.wait()
    traces_ref[...] = picked(split(held[...].T), one_hot(index_ref[0], held.shape[0]))
    for copy in copies:
        copy.wait()


def blocks_kernel(
    faces_total, core_ref, index_ref, quad_ref, pair_ref, basis_ref, applied_ref, send_ref, keep_ref, last_ref, held, acted, traces, sems
):
    count = basis_ref.shape[0]
    size = basis_ref.shape[2]
    half = size // 2
    core = core_ref[0]

    def copies(at):
        return (
            pltpu.make_async_copy(basis_ref.at[at], held.at[at], sems.at[2 * at]),
            pltpu.make_async_copy(applied_ref.at[at], acted.at[at], sems.at[2 * at + 1]),
        )

    for at in range(count):
        for copy in copies(at):
            copy.start()

    def store(element, rows, value):
        @pl.when(element // (count // 2) == core)
        def _():
            keep_ref[element % (count // 2), rows] = value

        @pl.when(element // (count // 2) != core)
        def _():
            send_ref[element % (count // 2), rows] = value

    @pl.loop(0, count)
    def _(at):
        for copy in copies(at):
            copy.wait()
        turned = held[at].T
        found = picked(split(turned), one_hot(index_ref[at], held.shape[1]))
        traces[at] = found
        width = found.shape[1] // 2
        outer, layer = found[:, :width], found[:, width:]
        total = dot3(split(turned * quad_ref[at]), split(acted[at]))
        total = total + dot3(split((2.0 * outer + layer) * (1.0 / faces_total)), split(outer), NT)
        mixed, side, diagonal = packed(0.5 * (total + total.T))
        store(at, slice(size, size + half), jnp.concatenate([mixed, side], axis=1))
        store(at, slice(size + half, None), jnp.broadcast_to(jnp.concatenate([diagonal, diagonal], axis=1), (8, size)))

    @pl.loop(0, count - 1)
    def _(at):
        following = traces[at + 1]
        width = following.shape[1] // 2
        order = one_hot(pair_ref[at], width)
        face, inside = picked(split(following[:, :width]), order), picked(split(following[:, width:]), order)
        store(at, slice(0, size), coupled(traces[at], face, inside, faces_total))

    last_ref[...] = traces[count - 1]


def coupled(own, face, inside, faces_total):
    width = own.shape[1] // 2
    outer, layer = own[:, :width], own[:, width:]
    near = split((penalty * outer + 0.5 * layer) * (-1.0 / faces_total))
    far = split(outer * (0.5 / faces_total))
    return dot3(near, split(face), NT) + dot3(far, split(inside), NT)


def last_kernel(faces_total, core_ref, pair_ref, own_ref, lead_ref, send_in, keep_in, send_ref, keep_ref, block, sem):
    width = own_ref.shape[1] // 2
    lead = split(lead_ref[...])
    face = picked(lead, one_hot(pair_ref[...], width))
    inside = picked(lead, one_hot(pair_ref[...], width, width // 2))
    block[...] = coupled(own_ref[...], face, inside, faces_total)
    at = send_ref.shape[0] - 1
    rows = pl.ds(0, block.shape[0])
    for core, ref in ((0, send_ref), (1, keep_ref)):

        @pl.when(core_ref[0] == core)
        def _():
            copy = pltpu.make_async_copy(block, ref.at[at, rows], sem)
            copy.start()
            copy.wait()


def packed(volume):
    half = volume.shape[0] // 2
    row = lax.broadcasted_iota(jnp.int32, (half, half), 0)
    column = lax.broadcasted_iota(jnp.int32, (half, half), 1)
    corner = volume[half:, half:]
    mixed = jnp.where(column >= row, volume[:half, :half], corner)
    diagonal = jnp.sum(jnp.where(column == row, corner, 0.0), axis=0, keepdims=True)
    return mixed, volume[:half, half:], diagonal


def unpacked(mixed, side, diagonal):
    half = mixed.shape[0]
    row = lax.broadcasted_iota(jnp.int32, (half, half), 0)
    column = lax.broadcasted_iota(jnp.int32, (half, half), 1)
    turned = mixed.T
    first = jnp.where(column >= row, mixed, turned)
    corner = jnp.where(column < row, mixed, jnp.where(column == row, diagonal, turned))
    top = jnp.concatenate([first, side], axis=1)
    return jnp.concatenate([top, jnp.concatenate([side.T, corner], axis=1)], axis=0)


def weights_kernel(me_ref, *refs):
    sources, (high_ref, low_ref), held, sems = refs[:8], refs[8:10], refs[10], refs[11]
    me = me_ref[0]
    size = held.shape[2]
    half = size // 2
    away_at = (0, 2, 1, 4, 3, 6, 5, 7)
    copies = [pltpu.make_async_copy(source.at[0], held.at[n], sems.at[n]) for n, source in enumerate(sources)]
    for copy in copies:
        copy.start()
    row = lax.broadcasted_iota(jnp.int32, (size, size), 0)
    diagonal = row == lax.broadcasted_iota(jnp.int32, (size, size), 1)

    for n, away in enumerate(away_at):
        copies[n].wait()
        element = away ^ me
        following = lax.rem(element + 1, len(away_at))
        volume, coupling = scaled(held[n], diagonal)
        for place, at, value in ((following, 0, coupling.T), (element, 1, volume), (element, 2, coupling)):
            high_ref[place, :, at * size : (at + 1) * size], low_ref[place, :, at * size : (at + 1) * size] = split(value)


def scaled(block, diagonal):
    size = block.shape[1]
    half = size // 2
    volume = unpacked(block[size : size + half, :half], block[size : size + half, half:], block[size + half : size + half + 1, :half])
    return (volume - jnp.where(diagonal, center, 0.0)) * (1.0 / half_width), block[:size] * (1.0 / half_width)


def outer_kernel(core_ref, first_ref, second_ref, swapped_ref, high_in, low_in, high_ref, low_ref):
    size = first_ref.shape[2]
    row = lax.broadcasted_iota(jnp.int32, (size, size), 0)
    diagonal = row == lax.broadcasted_iota(jnp.int32, (size, size), 1)
    kept = first_ref[0] + second_ref[0]
    core = core_ref[0]
    prior = jnp.where(core == 1, kept[:size], swapped_ref[0, :size]) * (1.0 / half_width)
    volume, coupling = scaled(jnp.where(core == 1, swapped_ref[0], kept), diagonal)
    last = high_in.shape[0] - 1
    high_ref[0, :, size:] = high_in[0, :, size:]
    low_ref[0, :, size:] = low_in[0, :, size:]
    high_ref[0, :, :size], low_ref[0, :, :size] = split(prior.T)
    turned = (high_in[last, :, 2 * size :].astype(jnp.float32) + low_in[last, :, 2 * size :].astype(jnp.float32)).T
    for at, value in enumerate((turned, volume, coupling)):
        high_ref[1, :, at * size : (at + 1) * size], low_ref[1, :, at * size : (at + 1) * size] = split(value)


def held_shape(rows, columns):
    return (rows, 2 * columns) if columns % 128 == 0 else (2, rows, columns)


def hold(held, at, value):
    high, low = split(value)
    size, columns = value.shape
    rows = slice(at * size, (at + 1) * size)
    if len(held.shape) == 2:
        held[rows, :columns] = high
        held[rows, columns:] = low
    else:
        held[0, rows] = high
        held[1, rows] = low


def apply_row(high, low, held, start, columns):
    rows = pl.ds(start, high.shape[1])
    if len(held.shape) == 2:
        if columns == 128:
            both = dot(high, held[rows, :])
            total = both[:, :columns] + both[:, columns:]
        else:
            total = dot(high, held[rows, :columns]) + dot(high, held[rows, columns:])
        return total + dot(low, held[rows, :columns])
    return dot(high, held[0, rows]) + (dot(high, held[1, rows]) + dot(low, held[0, rows]))


def advance(first, result, before):
    return result if first else 2.0 * result - before


def edge_kernel(first, up, lane, high, low, high_outer, low_outer, inner, halo, old, out, held):
    count, size, _ = inner.shape
    columns = halo.shape[2]
    lanes = slice(lane, lane + columns)
    local = (inner[count - 2, :, lanes], inner[count - 1, :, lanes]) if up else (inner[0, :, lanes], inner[1, :, lanes])
    beyond = (halo[0], halo[1])
    for at, value in enumerate(local + beyond if up else beyond + local):
        hold(held, at, value)
    last = high.shape[0] - 1
    rows = ((high[last], low[last]), (high_outer[1], low_outer[1])) if up else ((high_outer[0], low_outer[0]), (high[1], low[1]))
    for at, (part_high, part_low) in enumerate(rows):
        row = apply_row(part_high, part_low, held, at * size, columns)
        out[at] = advance(first, row, None if first else old[at])


def inner_kernel(first, up, lane, high, low, inner, old, *refs):
    edges, out, held = refs[:-2], refs[-2], refs[-1]
    count, size, columns = out.shape
    lanes = slice(lane, lane + columns)
    for at in range(2):
        hold(held, at if up else count + at, jnp.concatenate([edge[at] for edge in edges], axis=1))
    for at in range(count):
        hold(held, at + 2 if up else at, inner[at, :, lanes])

    @pl.loop(0, count)
    def _(at):
        place = at + (1 if up else 2)
        row = apply_row(high[place], low[place], held, pl.multiple_of(at * size, size), columns)
        out[at] = advance(first, row, None if first else old[at, :, lanes])


def fold_kernel(lane_ref, keep_ref, other_ref, send_ref, stay_ref):
    lane = lane_ref[0]
    half = keep_ref.shape[0] // 2
    for at in range(half):
        send_ref[at] = keep_ref[(1 - lane) * half + at] + other_ref[(1 - lane) * half + at]
        stay_ref[at] = keep_ref[lane * half + at] + other_ref[lane * half + at]


def sum_kernel(first_ref, second_ref, out_ref):
    out_ref[...] = first_ref[...] + second_ref[...]


def copy_pairs(side, pairs, sems):
    def moved(act):
        for at, (wanted, source, target) in enumerate(pairs):

            @pl.when(side == wanted)
            def _():
                act(pltpu.make_async_copy(source, target, sems.at[at]))

    moved(lambda copy: copy.start())
    moved(lambda copy: copy.wait())


def own_columns(vector_ref, side, element, count, half, lane, width):
    if vector_ref.shape[2] == half:
        return vector_ref.at[pl.ds(element, count)]
    start = pl.multiple_of(pl.multiple_of(side * half, half) + lane, width)
    return vector_ref.at[pl.ds(element, count), :, pl.ds(start, width)]


def arrange_edge_kernel(half, lane, side_ref, vector_ref, got_ref, edge_ref, sems):
    own = own_columns(vector_ref, side_ref[0], 0, 2, half, lane, got_ref.shape[2])
    copy_pairs(side_ref[0], ((0, own, edge_ref), (1, got_ref, edge_ref)), sems)


def arrange_inner_kernel(chunks, side_ref, vector_ref, *refs):
    first, (second, inner_ref, sems) = refs[:chunks], refs[chunks:]
    half = second.shape[2]
    width = half // chunks
    own = lambda element, count: own_columns(vector_ref, side_ref[0], element, count, half, 0, half)
    pairs = [
        (0, own(2, 2), inner_ref.at[pl.ds(0, 2)]),
        (0, second, inner_ref.at[pl.ds(4, 2)]),
        (1, second, inner_ref.at[pl.ds(0, 2)]),
        (1, own(0, 4), inner_ref.at[pl.ds(2, 4)]),
    ]
    for at, got in enumerate(first):
        target = inner_ref.at[pl.ds(2, 2)] if chunks == 1 else inner_ref.at[pl.ds(2, 2), :, pl.ds(at * width, width)]
        pairs.append((0, got, target))
    copy_pairs(side_ref[0], pairs, sems)


def place_pairs(out_ref, sems, side, chunks, chunk, width, pairs):
    def moved(act):
        for at, (wanted, source, element, foreign) in enumerate(pairs):

            @pl.when(side == wanted)
            def _():
                part = 1 - side if foreign else side
                start = pl.multiple_of((part * chunks + chunk) * width, width)
                act(pltpu.make_async_copy(source, out_ref.at[pl.ds(element, 2), :, pl.ds(start, width)], sems.at[chunk, at]))

    return moved


def collect_kernel(chunks, side_ref, *refs):
    sources, out_ref, sems = refs[: 3 * chunks], refs[-2], refs[-1]
    acts = []
    for chunk in range(chunks):
        edge, inner, near = sources[3 * chunk : 3 * chunk + 3]
        pairs = (
            (0, edge, 0, False),
            (0, inner.at[pl.ds(0, 2)], 2, False),
            (0, near, 2, True),
            (1, inner.at[pl.ds(2, 2)], 0, False),
            (1, inner.at[pl.ds(4, 2)], 2, False),
            (1, near, 0, True),
        )
        acts.append(place_pairs(out_ref, sems, side_ref[0], chunks, chunk, edge.shape[2], pairs))
    for act in acts:
        act(lambda copy: copy.start())
    for act in acts:
        act(lambda copy: copy.wait())


def finish_kernel(chunks, side_ref, *refs):
    sources, out_ref, sems = refs[:chunks], refs[-2], refs[-1]
    acts = []
    for chunk, far in enumerate(sources):
        pairs = ((0, far, 0, True), (1, far, 2, True))
        acts.append(place_pairs(out_ref, sems, side_ref[0], chunks, chunk, far.shape[2], pairs))
    for act in acts:
        act(lambda copy: copy.start())
    for act in acts:
        act(lambda copy: copy.wait())


def lead_and_cut(side, index, basis, vector, chunks, half):
    points, size = basis.shape[1:]
    cuts = [jax.ShapeDtypeStruct((2, size, half // chunks), jnp.float32)] * chunks
    return pl.pallas_call(
        lead_kernel,
        in_specs=[SCALARS, VMEM, ANY, ANY],
        out_specs=[VMEM] * (2 + chunks),
        out_shape=[jax.ShapeDtypeStruct((size, index.shape[2]), jnp.float32), *cuts, jax.ShapeDtypeStruct((2, size, half), jnp.float32)],
        scratch_shapes=[pltpu.VMEM((points, size), jnp.float32), pltpu.SemaphoreType.DMA((2 + chunks,))],
        compiler_params=PARAMS,
    )(side, index, far_off(basis), far_off(vector))


def blocks(core, index, quad, pairs, basis, applied, faces_total):
    count, points, size = basis.shape
    spots = index.shape[2]
    part = near_core((count // 2, size + size // 2 + 8, size))
    return pl.pallas_call(
        functools.partial(blocks_kernel, faces_total),
        in_specs=[SCALARS, VMEM, VMEM, VMEM, ANY, ANY],
        out_specs=[VMEM] * 3,
        out_shape=[part, part, near_core((size, spots))],
        scratch_shapes=[
            pltpu.VMEM((count, points, size), jnp.float32),
            pltpu.VMEM((count, points, size), jnp.float32),
            pltpu.VMEM((count, size, spots), jnp.float32),
            pltpu.SemaphoreType.DMA((2 * count,)),
        ],
        compiler_params=PARAMS,
    )(core, index, quad, pairs, far_off(basis), far_off(applied))


def last_coupling(core, pair, own, lead, send, keep, faces_total):
    size = own.shape[0]
    return pl.pallas_call(
        functools.partial(last_kernel, faces_total),
        in_specs=[SCALARS, VMEM, VMEM, VMEM, ANY, ANY],
        out_specs=[ANY] * 2,
        out_shape=[near_core(send.shape)] * 2,
        input_output_aliases={4: 0, 5: 1},
        scratch_shapes=[pltpu.VMEM((size, size), jnp.float32), pltpu.SemaphoreType.DMA],
        compiler_params=PARAMS,
    )(core, pair, own, lead, send, keep)


def weights(me, *parts):
    rows, size = parts[0].shape[1:]
    return pl.pallas_call(
        weights_kernel,
        in_specs=[SCALARS] + [ANY] * 8,
        out_specs=[VMEM] * 2,
        out_shape=[near_core((8, size, 3 * size), jnp.bfloat16)] * 2,
        scratch_shapes=[pltpu.VMEM((8, rows, size), jnp.float32), pltpu.SemaphoreType.DMA((8,))],
        compiler_params=PARAMS,
    )(me, *[far_off(part) for part in parts])


def outer_weights(core, first, second, swapped, high, low):
    size = first.shape[2]
    return pl.pallas_call(
        outer_kernel,
        in_specs=[SCALARS] + [VMEM] * 5,
        out_specs=[VMEM] * 2,
        out_shape=[near_core((2, size, 3 * size), jnp.bfloat16)] * 2,
        compiler_params=PARAMS,
    )(core, first, second, swapped, high, low)


def apply_edge(first, up, lane, high, low, high_outer, low_outer, inner, halo, old):
    size, columns = halo.shape[1:]
    return pl.pallas_call(
        functools.partial(edge_kernel, first, up, lane),
        in_specs=[VMEM] * 7,
        out_specs=VMEM,
        out_shape=near_core(halo.shape),
        input_output_aliases={} if first else {6: 0},
        scratch_shapes=[pltpu.VMEM(held_shape(4 * size, columns), jnp.bfloat16)],
        compiler_params=PARAMS,
    )(high, low, high_outer, low_outer, inner, close_by(halo), old)


def apply_inner(first, up, lane, high, low, edges, inner, old):
    count, size, columns = inner.shape
    width = sum(edge.shape[2] for edge in edges)
    return pl.pallas_call(
        functools.partial(inner_kernel, first, up, lane),
        in_specs=[VMEM] * (4 + len(edges)),
        out_specs=VMEM,
        out_shape=near_core((count, size, width)),
        input_output_aliases={} if first or width < columns else {3: 0},
        scratch_shapes=[pltpu.VMEM(held_shape((count + 2) * size, width), jnp.bfloat16)],
        compiler_params=PARAMS,
    )(high, low, inner, old, *edges)


def folded(lane, keep, other):
    shape = (keep.shape[0] // 2, *keep.shape[1:])
    return pl.pallas_call(
        fold_kernel,
        in_specs=[SCALARS, VMEM, VMEM],
        out_specs=[VMEM] * 2,
        out_shape=[near_core(shape)] * 2,
        compiler_params=PARAMS,
    )(lane, keep, close_by(other))


def added(first, second):
    return pl.pallas_call(
        sum_kernel, in_specs=[VMEM] * 2, out_specs=VMEM, out_shape=near_core(first.shape), compiler_params=PARAMS
    )(first, close_by(second))


def arranged_edge(side, vector, got, half, lane):
    return pl.pallas_call(
        functools.partial(arrange_edge_kernel, half, lane),
        in_specs=[SCALARS, ANY, ANY],
        out_specs=VMEM,
        out_shape=near_core(got.shape),
        scratch_shapes=[pltpu.SemaphoreType.DMA((2,))],
        compiler_params=PARAMS,
    )(side, far_off(vector), got)


def arranged_inner(side, vector, first, second):
    _, size, half = second.shape
    chunks = len(first)
    return pl.pallas_call(
        functools.partial(arrange_inner_kernel, chunks),
        in_specs=[SCALARS] + [ANY] * (2 + chunks),
        out_specs=VMEM,
        out_shape=near_core((6, size, half)),
        scratch_shapes=[pltpu.SemaphoreType.DMA((4 + chunks,))],
        compiler_params=PARAMS,
    )(side, far_off(vector), *first, second)


def collected(side, parts):
    count = 4
    _, size, width = parts[0][0].shape
    chunks = len(parts)
    return pl.pallas_call(
        functools.partial(collect_kernel, chunks),
        in_specs=[SCALARS] + [ANY] * (3 * chunks),
        out_specs=ANY,
        out_shape=jax.ShapeDtypeStruct((count, size, 2 * chunks * width), jnp.float32),
        scratch_shapes=[pltpu.SemaphoreType.DMA((chunks, 6))],
        compiler_params=PARAMS,
    )(side, *[value for part in parts for value in part])


def finished(side, parts, result):
    chunks = len(parts)
    return pl.pallas_call(
        functools.partial(finish_kernel, chunks),
        in_specs=[SCALARS] + [ANY] * (chunks + 1),
        out_specs=ANY,
        out_shape=jax.ShapeDtypeStruct(result.shape, jnp.float32),
        input_output_aliases={1 + chunks: 0},
        scratch_shapes=[pltpu.SemaphoreType.DMA((chunks, 2))],
        compiler_params=PARAMS,
    )(side, *parts, result)


def flipped(value, axis, bit):
    count = lax.axis_size(axis)
    return lax.ppermute(value, axis, [(i, i ^ bit) for i in range(count)])


def shifted(value, axis, steps):
    count = lax.axis_size(axis)
    return lax.ppermute(value, axis, [(i, (i + steps) % count) for i in range(count)])


def body(basis, applied, quad, face_index, face_pairing, orbitals):
    count, points, size = basis.shape
    spots = face_index.shape[2]
    columns = orbitals.shape[1]
    chunks = 2 if columns % 512 == 0 else 1
    elems, width = lax.axis_size("elem"), lax.axis_size("pts")
    faces_total = float(spots * width)
    side = lax.axis_index("elem") % 2
    core = lax.axis_index("pts") % 2
    lane = lax.axis_index("pts") // 2 % 2
    side_at = side.reshape(1).astype(jnp.int32)
    vector = orbitals.reshape(count, size, columns)

    lead_index = face_index[:1, 0:2].reshape(1, 1, 2 * spots)
    wide = columns // 2
    part = wide // chunks
    own = foreign = vector
    if part % 128:
        own = lax.dynamic_slice_in_dim(vector, side * part, part, axis=2)
        foreign = lax.dynamic_slice_in_dim(vector, (1 - side) * part, part, axis=2)
    lead, *foreign = lead_and_cut(1 - side_at, lead_index, basis, foreign, chunks, wide)
    lead = shifted(lead, "elem", -1)
    got = [flipped(value, "elem", 1) for value in foreign]

    index = jnp.stack([face_index[:, 0], face_index[:, 2], face_index[:, 1], face_index[:, 3]], axis=1)
    index = index.reshape(count, 1, 4 * spots)
    pairs = jnp.concatenate([jnp.full_like(face_pairing, -points), face_pairing], axis=1).reshape(count, 1, 2 * spots)
    core_at = core.reshape(1).astype(jnp.int32)
    send, keep, last = blocks(core_at, index, quad.reshape(count, 1, points), pairs, basis, applied, faces_total)
    send, keep = last_coupling(core_at, pairs[-1], last, lead, send, keep, faces_total)
    half = count // 2

    lane_at = lane.reshape(1).astype(jnp.int32)
    send, stay = folded(lane_at, keep, flipped(send, "pts", 1))
    mine = added(stay, flipped(send, "pts", 2))
    bit = 4
    while bit < width:
        mine = mine + flipped(mine, "pts", bit)
        bit *= 2
    edges, halos = [], []
    for chunk in range(chunks):
        edges.append(arranged_edge(side_at, own, got[chunk], wide, chunk * part))
        halos.append(shifted(edges[chunk], "elem", -2))
    halos[0], got[chunks - 1], mine = lax.optimization_barrier((halos[0], got[chunks - 1], mine))
    beside = flipped(mine, "pts", 2)
    across = flipped(mine, "elem", 1)
    mine_near = flipped(mine, "pts", 1)
    both = flipped(across, "pts", 2)
    beside_near = flipped(beside, "pts", 1)
    across_near = flipped(across, "pts", 1)

    last = jnp.where(lane == core, mine, beside)
    flat = lambda e, p: e % elems * width + p
    holds = [(e, p) for e in range(elems) for p in range(width) if e % 2 == p % 2]
    outer = lax.ppermute(last, ("elem", "pts"), [(flat(e, p), flat(e + (2 if p % 2 else -2), p)) for e, p in holds])
    outer_side = lax.ppermute(outer, ("elem", "pts"), [(flat(e, p), flat(e ^ 1, p)) for e, p in holds])
    outer_near = flipped(outer + outer_side, "pts", 1)

    halos[-1], got[-1], both = lax.optimization_barrier((halos[-1], got[-1], both))
    inner = arranged_inner(side_at, own, got[:-1], got[-1])
    both_near = flipped(both, "pts", 1)

    me = (side * 4 + core * 2 + lane).reshape(1).astype(jnp.int32)
    high, low = weights(me, mine, mine_near, beside, across, beside_near, across_near, both, both_near)
    high_outer, low_outer = outer_weights(core_at, outer, outer_side, outer_near, high, low)

    old_edges, old_inner = list(edges), inner
    near, far, parts = [], [], []
    for degree in range(DEG):
        first, up, final = degree == 0, degree % 2 == 0, degree == DEG - 1
        if not final:
            new_inner = apply_inner(first, up, 0, high, low, edges, inner, old_inner)
        new_edges = []
        for c in range(chunks):
            if final:
                parts.append(apply_inner(first, up, c * part, high, low, edges[c : c + 1], inner, old_inner))
                near.append(flipped(jnp.where(side == 0, parts[c][2:4], parts[c][:2]), "elem", 1))
            new_edges.append(apply_edge(first, up, c * part, high, low, high_outer, low_outer, inner, halos[c], old_edges[c]))
            if final:
                send = jnp.where(side == 0, parts[c][4:], new_edges[c])
                near[c], send = lax.optimization_barrier((near[c], send))
                far.append(flipped(send, "elem", 1))
            else:
                halos[c] = shifted(new_edges[c], "elem", 2 if up else -2)
        old_edges, edges = edges, new_edges
        old_inner, inner = inner, new_inner
    if part % 128:
        edge, inner, near, far = edges[0], parts[0], near[0], far[0]
        lower = jnp.concatenate([edge, inner[:2]])
        mine = jnp.where(side == 0, lower, inner[2:])
        theirs = jnp.where(side == 0, jnp.concatenate([far, near]), jnp.concatenate([near, far]))
        swap = lambda first, second: jnp.concatenate([first, second], axis=2)
        result = jnp.where(side == 0, swap(mine, theirs), swap(theirs, mine))
    else:
        result = collected(side_at, [(edges[c], parts[c], near[c]) for c in range(chunks)])
        result = finished(side_at, far, result)
    return result.reshape(count * size, columns)


def solution(mesh):
    return jax.shard_map(
        body,
        mesh=mesh,
        in_specs=(
            P("elem", "pts", None),
            P("elem", "pts", None),
            P("elem", "pts"),
            P("elem", None, "pts"),
            P("elem", "pts"),
            P("elem", "pts"),
        ),
        out_specs=P("elem", "pts"),
        check_vma=False,
    )
```

```python
import functools

import jax
import jax.numpy as jnp
from jax import lax
from jax.experimental import pallas as pl
from jax.experimental.pallas import tpu as pltpu
from jax.sharding import PartitionSpec as P

NB = 256
DEG = 4

penalty = 3.0
center = 4.0
half_width = 12.0

PARAMS = pltpu.CompilerParams(vmem_limit_bytes=12 * 1024 * 1024)
SCALARS = pl.BlockSpec(memory_space=pltpu.SMEM)
ANY = pl.BlockSpec(memory_space=pl.ANY)


def near_core(shape, dtype=jnp.float32):
    return pltpu.VMEM(shape, dtype)


def far_off(value):
    return pltpu.with_memory_space_constraint(value, pltpu.MemorySpace.HBM)


def close_by(value):
    return pltpu.with_memory_space_constraint(value, pltpu.MemorySpace.VMEM)
VMEM = pl.BlockSpec(memory_space=pltpu.VMEM)
NN = (((1,), (0,)), ((), ()))
NT = (((1,), (1,)), ((), ()))


def split(value):
    high = value.astype(jnp.bfloat16)
    low = (value - high.astype(jnp.float32)).astype(jnp.bfloat16)
    return high, low


def dot(first, second, dims=NN):
    return lax.dot_general(first, second, dims, preferred_element_type=jnp.float32)


def dot3(first, second, dims=NN):
    first_high, first_low = first
    second_high, second_low = second
    return dot(first_high, second_high, dims) + (dot(first_high, second_low, dims) + dot(first_low, second_high, dims))


def picked(parts, chosen):
    return dot(parts[0], chosen) + dot(parts[1], chosen)


def one_hot(index_row, rows, offset=0):
    at = lax.broadcasted_iota(jnp.int32, (rows, index_row.shape[1]), 0) - offset
    return (at == index_row).astype(jnp.float32).astype(jnp.bfloat16)


def lead_kernel(at_ref, index_ref, basis_ref, vector_ref, traces_ref, *rest):
    cut_refs, (held, sems) = rest[:-2], rest[-2:]
    first = pltpu.make_async_copy(basis_ref.at[0], held, sems.at[0])
    first.start()
    copies = []
    for at, out_ref in enumerate(cut_refs):
        source = own_columns(vector_ref, 1 - at_ref[0], 2 * at, out_ref.shape[2])
        copies.append(pltpu.make_async_copy(source, out_ref, sems.at[1 + at]))
        copies[-1].start()
    first.wait()
    traces_ref[...] = picked(split(held[...].T), one_hot(index_ref[0], held.shape[0]))
    for copy in copies:
        copy.wait()


def blocks_kernel(
    faces_total, at_ref, index_ref, quad_ref, pair_ref, basis_ref, applied_ref, send_ref, keep_ref, last_ref, held, acted, traces, sems
):
    count = basis_ref.shape[0]
    size = basis_ref.shape[2]
    half = size // 2
    core = at_ref[1]

    def copies(at):
        return (
            pltpu.make_async_copy(basis_ref.at[at], held.at[at], sems.at[2 * at]),
            pltpu.make_async_copy(applied_ref.at[at], acted.at[at], sems.at[2 * at + 1]),
        )

    for at in range(count):
        for copy in copies(at):
            copy.start()

    def store(element, rows, value):
        @pl.when(element // (count // 2) == core)
        def _():
            keep_ref[element % (count // 2), rows] = value

        @pl.when(element // (count // 2) != core)
        def _():
            send_ref[element % (count // 2), rows] = value

    @pl.loop(0, count)
    def _(at):
        for copy in copies(at):
            copy.wait()
        turned = held[at].T
        found = picked(split(turned), one_hot(index_ref[at], held.shape[1]))
        traces[at] = found
        width = found.shape[1] // 2
        outer, layer = found[:, :width], found[:, width:]
        total = dot3(split(turned * quad_ref[at]), split(acted[at]))
        total = total + dot3(split((2.0 * outer + layer) * (1.0 / faces_total)), split(outer), NT)
        mixed, side, diagonal = packed(0.5 * (total + total.T))
        store(at, slice(size, size + half), jnp.concatenate([mixed, side], axis=1))
        store(at, slice(size + half, None), jnp.broadcast_to(jnp.concatenate([diagonal, diagonal], axis=1), (8, size)))

    @pl.loop(0, count - 1)
    def _(at):
        following = traces[at + 1]
        width = following.shape[1] // 2
        order = one_hot(pair_ref[at], width)
        face, inside = picked(split(following[:, :width]), order), picked(split(following[:, width:]), order)
        store(at, slice(0, size), coupled(traces[at], face, inside, faces_total))

    last_ref[...] = traces[count - 1]


def coupled(own, face, inside, faces_total):
    width = own.shape[1] // 2
    outer, layer = own[:, :width], own[:, width:]
    near = split((penalty * outer + 0.5 * layer) * (-1.0 / faces_total))
    far = split(outer * (0.5 / faces_total))
    return dot3(near, split(face), NT) + dot3(far, split(inside), NT)


def last_kernel(faces_total, at_ref, pair_ref, own_ref, lead_ref, send_in, keep_in, send_ref, keep_ref, block, sem):
    width = own_ref.shape[1] // 2
    lead = split(lead_ref[...])
    face = picked(lead, one_hot(pair_ref[...], width))
    inside = picked(lead, one_hot(pair_ref[...], width, width // 2))
    block[...] = coupled(own_ref[...], face, inside, faces_total)
    at = send_ref.shape[0] - 1
    rows = pl.ds(0, block.shape[0])
    for core, ref in ((0, send_ref), (1, keep_ref)):

        @pl.when(at_ref[1] == core)
        def _():
            copy = pltpu.make_async_copy(block, ref.at[at, rows], sem)
            copy.start()
            copy.wait()


def packed(volume):
    half = volume.shape[0] // 2
    row = lax.broadcasted_iota(jnp.int32, (half, half), 0)
    column = lax.broadcasted_iota(jnp.int32, (half, half), 1)
    corner = volume[half:, half:]
    mixed = jnp.where(column >= row, volume[:half, :half], corner)
    diagonal = jnp.sum(jnp.where(column == row, corner, 0.0), axis=0, keepdims=True)
    return mixed, volume[:half, half:], diagonal


def unpacked(mixed, side, diagonal):
    half = mixed.shape[0]
    row = lax.broadcasted_iota(jnp.int32, (half, half), 0)
    column = lax.broadcasted_iota(jnp.int32, (half, half), 1)
    turned = mixed.T
    first = jnp.where(column >= row, mixed, turned)
    corner = jnp.where(column < row, mixed, jnp.where(column == row, diagonal, turned))
    top = jnp.concatenate([first, side], axis=1)
    return jnp.concatenate([top, jnp.concatenate([side.T, corner], axis=1)], axis=0)


def weights_kernel(at_ref, *refs):
    sources, (high_ref, low_ref), held, sems = refs[:8], refs[8:10], refs[10], refs[11]
    me = at_ref[3]
    size = held.shape[2]
    half = size // 2
    away_at = (0, 2, 1, 4, 3, 6, 5, 7)
    copies = [pltpu.make_async_copy(source.at[0], held.at[n], sems.at[n]) for n, source in enumerate(sources)]
    for copy in copies:
        copy.start()
    row = lax.broadcasted_iota(jnp.int32, (size, size), 0)
    diagonal = row == lax.broadcasted_iota(jnp.int32, (size, size), 1)

    for n, away in enumerate(away_at):
        copies[n].wait()
        element = away ^ me
        following = lax.rem(element + 1, len(away_at))
        volume, coupling = scaled(held[n], diagonal)
        for place, at, value in ((following, 0, coupling.T), (element, 1, volume), (element, 2, coupling)):
            high_ref[place, :, at * size : (at + 1) * size], low_ref[place, :, at * size : (at + 1) * size] = split(value)


def scaled(block, diagonal):
    size = block.shape[1]
    half = size // 2
    volume = unpacked(block[size : size + half, :half], block[size : size + half, half:], block[size + half : size + half + 1, :half])
    return (volume - jnp.where(diagonal, center, 0.0)) * (1.0 / half_width), block[:size] * (1.0 / half_width)


def outer_kernel(at_ref, kept_ref, swapped_ref, high_in, low_in, high_ref, low_ref):
    size = kept_ref.shape[2]
    rows = kept_ref.shape[1] - size
    row = lax.broadcasted_iota(jnp.int32, (size, size), 0)
    diagonal = row == lax.broadcasted_iota(jnp.int32, (size, size), 1)
    lower = at_ref[1] == 1
    below = jnp.where(lower, kept_ref[0], swapped_ref[0])
    volume, coupling = scaled(below[:rows], diagonal)
    turned = coupling.T
    for at, value in enumerate(((below[rows:] * (1.0 / half_width)).T, volume, coupling)):
        high_ref[0, :, at * size : (at + 1) * size], low_ref[0, :, at * size : (at + 1) * size] = split(value)
    high_ref[1, :, :size], low_ref[1, :, :size] = split(turned)
    high_ref[1, :, size:] = high_in[0, :, size:]
    low_ref[1, :, size:] = low_in[0, :, size:]
    volume, coupling = scaled(jnp.where(lower, swapped_ref[0, :rows], kept_ref[0, :rows]), diagonal)
    last = high_in.shape[0] - 1
    turned = (high_in[last, :, 2 * size :].astype(jnp.float32) + low_in[last, :, 2 * size :].astype(jnp.float32)).T
    for at, value in enumerate((turned, volume, coupling)):
        high_ref[2, :, at * size : (at + 1) * size], low_ref[2, :, at * size : (at + 1) * size] = split(value)


def held_shape(rows, columns):
    return (rows, 2 * columns) if columns % 128 == 0 else (2, rows, columns)


def hold(held, at, value):
    high, low = split(value)
    size, columns = value.shape
    rows = slice(at * size, (at + 1) * size)
    if len(held.shape) == 2:
        held[rows, :columns] = high
        held[rows, columns:] = low
    else:
        held[0, rows] = high
        held[1, rows] = low


def apply_row(high, low, held, start, columns):
    rows = pl.ds(start, high.shape[1])
    if len(held.shape) == 2:
        if columns == 128:
            both = dot(high, held[rows, :])
            total = both[:, :columns] + both[:, columns:]
        else:
            total = dot(high, held[rows, :columns]) + dot(high, held[rows, columns:])
        return total + dot(low, held[rows, :columns])
    return dot(high, held[0, rows]) + (dot(high, held[1, rows]) + dot(low, held[0, rows]))


def hold_all(held, values):
    for at, value in enumerate(values):
        hold(held, at, value)


def first_kernel(high, low, y0, above, y1, held):
    count, size, columns = y0.shape
    hold_all(held, [y0[at] for at in range(count)] + [above[0]])

    @pl.loop(0, count - 1)
    def _(at):
        y1[at] = apply_row(high[at + 1], low[at + 1], held, pl.multiple_of(at * size, size), columns)


def second_kernel(chunks, high, low, outer_high, outer_low, y0, below, above, y1, y1_ends, *refs):
    outs, held = refs[:-1], refs[-1]
    count, size, columns = y0.shape
    row = lambda weight, start: apply_row(*weight, held, start * size, columns)
    outer = lambda at: (outer_high[at], outer_low[at])
    main = lambda at: (high[at], low[at])
    hold_all(held, (below[0], below[1], y0[0], y0[1], y0[count - 1], above[0], above[1]))
    y1_ends[0] = row(outer(0), 0)
    y1_ends[1] = row(outer(1), 1)
    y1_ends[2] = row(outer(2), 4)
    hold_all(held, (y1_ends[0], y1_ends[1], y1[0], y1[1], y1[count - 4], y1[count - 3], y1[count - 2], y1_ends[2]))
    width = columns // chunks
    for out_at, at, weight, start, element in (
        (0, 0, outer(1), 0, 0),
        (0, 1, main(1), 1, 1),
        (1, 0, main(count - 2), 4, count - 2),
        (1, 1, main(count - 1), 5, count - 1),
    ):
        value = 2.0 * row(weight, start) - y0[element]
        for chunk in range(chunks):
            outs[out_at * chunks + chunk][at] = value[:, chunk * width : (chunk + 1) * width]


def middle_kernel(chunks, at_ref, high, low, y0, y1, *refs):
    ends, (y3_kept, y4, send, held, y2, y3) = refs[: 2 * chunks], refs[2 * chunks :]
    count, size, columns = y0.shape
    row = lambda place, at: apply_row(high[place], low[place], held, pl.multiple_of(at * size, size), columns)
    hold_all(held, [y1[at] for at in range(count - 2)])

    @pl.loop(0, count - 4)
    def _(at):
        y2[at] = 2.0 * row(at + 2, at) - y0[at + 2]

    joined = lambda group, at: jnp.concatenate([end[at] for end in ends[group * chunks : (group + 1) * chunks]], axis=1)
    hold_all(held, [joined(0, 0), joined(0, 1)] + [y2[at] for at in range(count - 4)] + [joined(1, 0), joined(1, 1)])

    @pl.loop(0, count - 2)
    def _(at):
        y3[at] = 2.0 * row(at + 1, at) - y1[at]

    hold_all(held, [y3[at] for at in range(count - 2)])

    @pl.loop(0, count - 4)
    def _(at):
        y4[at] = 2.0 * row(at + 2, at) - y2[at]

    send[...] = y4[pl.ds((1 - at_ref[0]) * 2, 2)]
    for at, place in enumerate((0, 1, count - 4, count - 3)):
        y3_kept[at] = y3[place]


def last_rows_kernel(
    lane, at_ref, high, low, outer_high, outer_low, y1, y1_ends, y3, y2_low, y2_high, below, above, y4_low, y4_high, send, held
):
    size, columns = below.shape[1:]
    count = high.shape[0]
    lanes = slice(lane, lane + columns)
    row = lambda weight, start: apply_row(*weight, held, start * size, columns)
    outer = lambda at: (outer_high[at], outer_low[at])
    main = lambda at: (high[at], low[at])
    hold_all(held, (below[0], below[1], y2_low[0], y2_low[1], y2_high[0], y2_high[1], above[0], above[1]))
    lower = 2.0 * row(outer(0), 0) - y1_ends[0, :, lanes]
    low_own = 2.0 * row(outer(1), 1) - y1_ends[1, :, lanes]
    high_own = 2.0 * row(main(count - 1), 4) - y1[count - 2, :, lanes]
    upper = 2.0 * row(outer(2), 5) - y1_ends[2, :, lanes]
    hold_all(held, (lower, low_own, y3[0, :, lanes], y3[1, :, lanes], y3[2, :, lanes], y3[3, :, lanes], high_own, upper))
    y4_low[0] = 2.0 * row(outer(1), 0) - y2_low[0]
    y4_low[1] = 2.0 * row(main(1), 1) - y2_low[1]
    y4_high[0] = 2.0 * row(main(count - 2), 4) - y2_high[0]
    y4_high[1] = 2.0 * row(main(count - 1), 5) - y2_high[1]
    send[...] = jnp.where(at_ref[0] == 0, y4_high[...], y4_low[...])


def fold_kernel(at_ref, keep_ref, other_ref, send_ref, stay_ref):
    lane = at_ref[2]
    half = keep_ref.shape[0] // 2
    for at in range(half):
        send_ref[at] = keep_ref[(1 - lane) * half + at] + other_ref[(1 - lane) * half + at]
        stay_ref[at] = keep_ref[lane * half + at] + other_ref[lane * half + at]


def outer_block_kernel(at_ref, mine_ref, beside_ref, out_ref, sems):
    rows, size = mine_ref.shape[1:]

    def moved(act):
        for wanted, outer, other in ((True, mine_ref, beside_ref), (False, beside_ref, mine_ref)):

            @pl.when((at_ref[1] == at_ref[2]) == wanted)
            def _():
                act(pltpu.make_async_copy(outer.at[0], out_ref.at[0, pl.ds(0, rows)], sems.at[0]))
                act(pltpu.make_async_copy(other.at[0, pl.ds(0, size)], out_ref.at[0, pl.ds(rows, size)], sems.at[1]))

    moved(lambda copy: copy.start())
    moved(lambda copy: copy.wait())


def sum_kernel(first_ref, second_ref, out_ref):
    out_ref[...] = first_ref[...] + second_ref[...]


def copy_pairs(side, pairs, sems):
    def moved(act):
        for at, (wanted, source, target) in enumerate(pairs):

            @pl.when(side == wanted)
            def _():
                act(pltpu.make_async_copy(source, target, sems.at[at]))

    moved(lambda copy: copy.start())
    moved(lambda copy: copy.wait())


def own_columns(vector_ref, half, element, width, count=2):
    if vector_ref.shape[2] == width:
        return vector_ref.at[pl.ds(element, count)]
    return vector_ref.at[pl.ds(element, count), :, pl.ds(pl.multiple_of(half * width, width), width)]


def arrange_pair_kernel(element, wanted, at_ref, vector_ref, got_ref, out_ref, sems):
    own = own_columns(vector_ref, at_ref[0], element, got_ref.shape[2])
    copy_pairs(at_ref[0], ((wanted, own, out_ref), (1 - wanted, got_ref, out_ref)), sems)


def arrange_kernel(at_ref, vector_ref, first_ref, second_ref, out_ref, sems):
    own = own_columns(vector_ref, at_ref[0], 0, first_ref.shape[2], 4)
    pairs = []
    for side in range(2):
        pairs.append((side, own, out_ref.at[pl.ds(4 * side, 4)]))
        pairs.append((side, first_ref, out_ref.at[pl.ds(4 - 4 * side, 2)]))
        pairs.append((side, second_ref, out_ref.at[pl.ds(6 - 4 * side, 2)]))
    copy_pairs(at_ref[0], pairs, sems)


def place_pairs(out_ref, sems, side, chunks, chunk, width, pairs):
    def moved(act):
        for at, (wanted, source, element, foreign) in enumerate(pairs):

            @pl.when(side == wanted)
            def _():
                part = 1 - side if foreign else side
                start = pl.multiple_of((part * chunks + chunk) * width, width)
                act(pltpu.make_async_copy(source, out_ref.at[pl.ds(element, 2), :, pl.ds(start, width)], sems.at[chunk, at]))

    return moved


def collect_kernel(at_ref, y4, near, out_ref, sems):
    pairs = (
        (0, y4.at[pl.ds(0, 2)], 2, False),
        (0, near, 2, True),
        (1, y4.at[pl.ds(2, 2)], 0, False),
        (1, near, 0, True),
    )
    act = place_pairs(out_ref, sems, at_ref[0], 1, 0, near.shape[2], pairs)
    act(lambda copy: copy.start())
    act(lambda copy: copy.wait())


def finish_kernel(chunks, at_ref, *refs):
    sources, out_ref, sems = refs[: 3 * chunks], refs[-2], refs[-1]
    acts = []
    for chunk in range(chunks):
        y4_low, y4_high, far = sources[3 * chunk : 3 * chunk + 3]
        pairs = ((0, y4_low, 0, False), (0, far, 0, True), (1, y4_high, 2, False), (1, far, 2, True))
        acts.append(place_pairs(out_ref, sems, at_ref[0], chunks, chunk, far.shape[2], pairs))
    for act in acts:
        act(lambda copy: copy.start())
    for act in acts:
        act(lambda copy: copy.wait())


def lead_and_cut(at, index, basis, vector, half):
    points, size = basis.shape[1:]
    return pl.pallas_call(
        lead_kernel,
        in_specs=[SCALARS, VMEM, ANY, ANY],
        out_specs=[VMEM] * 3,
        out_shape=[near_core((size, index.shape[2]))] + [near_core((2, size, half))] * 2,
        scratch_shapes=[pltpu.VMEM((points, size), jnp.float32), pltpu.SemaphoreType.DMA((3,))],
        compiler_params=PARAMS,
    )(at, index, far_off(basis), far_off(vector))


def blocks(core, index, quad, pairs, basis, applied, faces_total):
    count, points, size = basis.shape
    spots = index.shape[2]
    part = near_core((count // 2, size + size // 2 + 8, size))
    return pl.pallas_call(
        functools.partial(blocks_kernel, faces_total),
        in_specs=[SCALARS, VMEM, VMEM, VMEM, ANY, ANY],
        out_specs=[VMEM] * 3,
        out_shape=[part, part, near_core((size, spots))],
        scratch_shapes=[
            pltpu.VMEM((count, points, size), jnp.float32),
            pltpu.VMEM((count, points, size), jnp.float32),
            pltpu.VMEM((count, size, spots), jnp.float32),
            pltpu.SemaphoreType.DMA((2 * count,)),
        ],
        compiler_params=PARAMS,
    )(core, index, quad, pairs, far_off(basis), far_off(applied))


def last_coupling(core, pair, own, lead, send, keep, faces_total):
    size = own.shape[0]
    return pl.pallas_call(
        functools.partial(last_kernel, faces_total),
        in_specs=[SCALARS, VMEM, VMEM, VMEM, ANY, ANY],
        out_specs=[ANY] * 2,
        out_shape=[near_core(send.shape)] * 2,
        input_output_aliases={4: 0, 5: 1},
        scratch_shapes=[pltpu.VMEM((size, size), jnp.float32), pltpu.SemaphoreType.DMA],
        compiler_params=PARAMS,
    )(core, pair, own, lead, send, keep)


def weights(me, *parts):
    rows, size = parts[0].shape[1:]
    return pl.pallas_call(
        weights_kernel,
        in_specs=[SCALARS] + [ANY] * 8,
        out_specs=[VMEM] * 2,
        out_shape=[near_core((8, size, 3 * size), jnp.bfloat16)] * 2,
        scratch_shapes=[pltpu.VMEM((8, rows, size), jnp.float32), pltpu.SemaphoreType.DMA((8,))],
        compiler_params=PARAMS,
    )(me, *[far_off(part) for part in parts])


def outer_weights(at, kept, swapped, high, low):
    size = kept.shape[2]
    return pl.pallas_call(
        outer_kernel,
        in_specs=[SCALARS] + [VMEM] * 4,
        out_specs=[VMEM] * 2,
        out_shape=[near_core((3, size, 3 * size), jnp.bfloat16)] * 2,
        compiler_params=PARAMS,
    )(at, kept, swapped, high, low)


def first_rows(high, low, y0, above):
    count, size, columns = y0.shape
    return pl.pallas_call(
        first_kernel,
        in_specs=[VMEM] * 4,
        out_specs=VMEM,
        out_shape=near_core((count - 1, size, columns)),
        scratch_shapes=[pltpu.VMEM(held_shape((count + 1) * size, columns), jnp.bfloat16)],
        compiler_params=PARAMS,
    )(high, low, y0, above)


def second_rows(chunks, high, low, outer_high, outer_low, y0, below, above, y1):
    count, size, columns = y0.shape
    return pl.pallas_call(
        functools.partial(second_kernel, chunks),
        in_specs=[VMEM] * 8,
        out_specs=[VMEM] * (1 + 2 * chunks),
        out_shape=[near_core((3, size, columns))] + [near_core((2, size, columns // chunks))] * (2 * chunks),
        scratch_shapes=[pltpu.VMEM(held_shape(8 * size, columns), jnp.bfloat16)],
        compiler_params=PARAMS,
    )(high, low, outer_high, outer_low, y0, close_by(below), close_by(above), y1)


def middle_rows(at, chunks, high, low, y0, y1, ends):
    count, size, columns = y0.shape
    return pl.pallas_call(
        functools.partial(middle_kernel, chunks),
        in_specs=[SCALARS] + [VMEM] * (4 + 2 * chunks),
        out_specs=[VMEM] * 3,
        out_shape=[near_core((4, size, columns)), near_core((count - 4, size, columns)), near_core((2, size, columns))],
        scratch_shapes=[
            pltpu.VMEM(held_shape(count * size, columns), jnp.bfloat16),
            pltpu.VMEM((count - 4, size, columns), jnp.float32),
            pltpu.VMEM((count - 2, size, columns), jnp.float32),
        ],
        compiler_params=PARAMS,
    )(at, high, low, y0, y1, *ends)


def last_rows(at, lane, high, low, outer_high, outer_low, y1, y1_ends, y3, y2_low, y2_high, below, above):
    size, columns = below.shape[1:]
    return pl.pallas_call(
        functools.partial(last_rows_kernel, lane),
        in_specs=[SCALARS] + [VMEM] * 11,
        out_specs=[VMEM] * 3,
        out_shape=[near_core(below.shape)] * 3,
        scratch_shapes=[pltpu.VMEM(held_shape(8 * size, columns), jnp.bfloat16)],
        compiler_params=PARAMS,
    )(at, high, low, outer_high, outer_low, y1, y1_ends, y3, y2_low, y2_high, close_by(below), close_by(above))


def folded(lane, keep, other):
    shape = (keep.shape[0] // 2, *keep.shape[1:])
    return pl.pallas_call(
        fold_kernel,
        in_specs=[SCALARS, VMEM, VMEM],
        out_specs=[VMEM] * 2,
        out_shape=[near_core(shape)] * 2,
        compiler_params=PARAMS,
    )(lane, keep, close_by(other))


def outer_block(at, mine, beside):
    return pl.pallas_call(
        outer_block_kernel,
        in_specs=[SCALARS, ANY, ANY],
        out_specs=VMEM,
        out_shape=near_core((1, mine.shape[1] + mine.shape[2], mine.shape[2])),
        scratch_shapes=[pltpu.SemaphoreType.DMA((2,))],
        compiler_params=PARAMS,
    )(at, mine, beside)


def added(first, second):
    return pl.pallas_call(
        sum_kernel, in_specs=[VMEM] * 2, out_specs=VMEM, out_shape=near_core(first.shape), compiler_params=PARAMS
    )(first, close_by(second))


def arranged_pair(at, element, wanted, vector, got):
    return pl.pallas_call(
        functools.partial(arrange_pair_kernel, element, wanted),
        in_specs=[SCALARS, ANY, ANY],
        out_specs=VMEM,
        out_shape=near_core(got.shape),
        scratch_shapes=[pltpu.SemaphoreType.DMA((2,))],
        compiler_params=PARAMS,
    )(at, far_off(vector), got)


def arranged(at, vector, first, second):
    return pl.pallas_call(
        arrange_kernel,
        in_specs=[SCALARS, ANY, ANY, ANY],
        out_specs=VMEM,
        out_shape=near_core((8, *first.shape[1:])),
        scratch_shapes=[pltpu.SemaphoreType.DMA((6,))],
        compiler_params=PARAMS,
    )(at, far_off(vector), first, second)


def collected(at, y4, near):
    _, size, columns = near.shape
    return pl.pallas_call(
        collect_kernel,
        in_specs=[SCALARS, ANY, ANY],
        out_specs=ANY,
        out_shape=jax.ShapeDtypeStruct((4, size, 2 * columns), jnp.float32),
        scratch_shapes=[pltpu.SemaphoreType.DMA((1, 4))],
        compiler_params=PARAMS,
    )(at, y4, near)


def finished(at, parts, result):
    chunks = len(parts)
    return pl.pallas_call(
        functools.partial(finish_kernel, chunks),
        in_specs=[SCALARS] + [ANY] * (3 * chunks + 1),
        out_specs=ANY,
        out_shape=jax.ShapeDtypeStruct(result.shape, jnp.float32),
        input_output_aliases={1 + 3 * chunks: 0},
        scratch_shapes=[pltpu.SemaphoreType.DMA((chunks, 4))],
        compiler_params=PARAMS,
    )(at, *[value for part in parts for value in part], result)


def flipped(value, axis, bit):
    count = lax.axis_size(axis)
    return lax.ppermute(value, axis, [(i, i ^ bit) for i in range(count)])


def shifted(value, axis, steps):
    count = lax.axis_size(axis)
    return lax.ppermute(value, axis, [(i, (i + steps) % count) for i in range(count)])


def body(basis, applied, quad, face_index, face_pairing, orbitals):
    count, points, size = basis.shape
    spots = face_index.shape[2]
    columns = orbitals.shape[1]
    chunks = 2 if columns % 512 == 0 else 1
    elems, width = lax.axis_size("elem"), lax.axis_size("pts")
    faces_total = float(spots * width)
    side = lax.axis_index("elem") % 2
    core = lax.axis_index("pts") % 2
    lane = lax.axis_index("pts") // 2 % 2
    vector = orbitals.reshape(count, size, columns)
    at = jnp.stack([side, core, lane, side * 4 + core * 2 + lane]).astype(jnp.int32)

    lead_index = face_index[:1, 0:2].reshape(1, 1, 2 * spots)
    index = jnp.stack([face_index[:, 0], face_index[:, 2], face_index[:, 1], face_index[:, 3]], axis=1)
    index = index.reshape(count, 1, 4 * spots)
    pairs = jnp.concatenate([jnp.full_like(face_pairing, -points), face_pairing], axis=1).reshape(count, 1, 2 * spots)
    quad = quad.reshape(count, 1, points)
    last_pair = pairs[-1]
    vector, at, lead_index, index, pairs, last_pair, quad = lax.optimization_barrier(
        (vector, at, lead_index, index, pairs, last_pair, quad)
    )
    wide = columns // 2
    part = wide // chunks
    own = foreign = vector
    if part % 128:
        own = lax.dynamic_slice_in_dim(vector, side * part, part, axis=2)
        foreign = lax.dynamic_slice_in_dim(vector, (1 - side) * part, part, axis=2)
    lead, first, second = lead_and_cut(at, lead_index, basis, foreign, wide)
    lead = shifted(lead, "elem", -1)
    first, second = flipped(first, "elem", 1), flipped(second, "elem", 1)

    send, keep, last = blocks(at, index, quad, pairs, basis, applied, faces_total)
    send, keep = last_coupling(at, last_pair, last, lead, send, keep, faces_total)
    send, stay = folded(at, keep, flipped(send, "pts", 1))
    mine = added(stay, flipped(send, "pts", 2))
    bit = 4
    while bit < width:
        mine = mine + flipped(mine, "pts", bit)
        bit *= 2
    first, mine = lax.optimization_barrier((first, mine))
    above = shifted(arranged_pair(at, 0, 0, own, first), "elem", -2)
    beside = flipped(mine, "pts", 2)
    across = flipped(mine, "elem", 1)
    beside, across = lax.optimization_barrier((beside, across))
    mine_near = flipped(mine, "pts", 1)
    both = flipped(across, "pts", 2)
    beside_near = flipped(beside, "pts", 1)
    across_near = flipped(across, "pts", 1)

    last = outer_block(at, mine, beside)
    flat = lambda e, p: e % elems * width + p
    holds = [(e, p) for e in range(elems) for p in range(width) if e % 2 == p % 2]
    outer = lax.ppermute(last, ("elem", "pts"), [(flat(e, p), flat(e + (2 if p % 2 else -2), p)) for e, p in holds])
    outer = added(outer, lax.ppermute(outer, ("elem", "pts"), [(flat(e, p), flat(e ^ 1, p)) for e, p in holds]))
    outer_near = flipped(outer, "pts", 1)

    above, second, both = lax.optimization_barrier((above, second, both))
    below = shifted(arranged_pair(at, 2, 1, own, second), "elem", 2)
    y0 = arranged(at, own, first, second)
    both_near = flipped(both, "pts", 1)

    high, low = weights(at, mine, mine_near, beside, across, beside_near, across_near, both, both_near)
    high_outer, low_outer = outer_weights(at, outer, outer_near, high, low)

    y1 = first_rows(high, low, y0, above)
    y1_ends, *ends = second_rows(chunks, high, low, high_outer, low_outer, y0, below, above, y1)
    belows = [shifted(value, "elem", 2) for value in ends[chunks:]]
    aboves = [shifted(value, "elem", -2) for value in ends[:chunks]]
    y3, y4, near = middle_rows(at, chunks, high, low, y0, y1, ends)
    near = flipped(near, "elem", 1)
    parts = []
    for c in range(chunks):
        y4_low, y4_high, far = last_rows(
            at, c * part, high, low, high_outer, low_outer, y1, y1_ends, y3, ends[c], ends[chunks + c], belows[c], aboves[c]
        )
        parts.append((y4_low, y4_high, flipped(far, "elem", 1)))
    if part % 128:
        y4_low, y4_high, far = parts[0]
        mine = jnp.where(side == 0, jnp.concatenate([y4_low, y4[:2]]), jnp.concatenate([y4[2:], y4_high]))
        theirs = jnp.where(side == 0, jnp.concatenate([far, near]), jnp.concatenate([near, far]))
        swap = lambda first, second: jnp.concatenate([first, second], axis=2)
        result = jnp.where(side == 0, swap(mine, theirs), swap(theirs, mine))
    else:
        result = finished(at, parts, collected(at, y4, near))
    return result.reshape(count * size, columns)


def solution(mesh):
    return jax.shard_map(
        body,
        mesh=mesh,
        in_specs=(
            P("elem", "pts", None),
            P("elem", "pts", None),
            P("elem", "pts"),
            P("elem", None, "pts"),
            P("elem", "pts"),
            P("elem", "pts"),
        ),
        out_specs=P("elem", "pts"),
        check_vma=False,
    )
```

```python
import functools

import jax
import jax.numpy as jnp
from jax import lax
from jax.experimental import pallas as pl
from jax.experimental.pallas import tpu as pltpu
from jax.sharding import PartitionSpec as P

NB = 256
DEG = 4

penalty = 3.0
center = 4.0
half_width = 12.0

PARAMS = pltpu.CompilerParams(vmem_limit_bytes=12 * 1024 * 1024)
SCALARS = pl.BlockSpec(memory_space=pltpu.SMEM)
ANY = pl.BlockSpec(memory_space=pl.ANY)


def near_core(shape, dtype=jnp.float32):
    return pltpu.VMEM(shape, dtype)


def far_off(value):
    return pltpu.with_memory_space_constraint(value, pltpu.MemorySpace.HBM)


def close_by(value):
    return pltpu.with_memory_space_constraint(value, pltpu.MemorySpace.VMEM)
VMEM = pl.BlockSpec(memory_space=pltpu.VMEM)
NN = (((1,), (0,)), ((), ()))
NT = (((1,), (1,)), ((), ()))


def split(value):
    high = value.astype(jnp.bfloat16)
    low = (value - high.astype(jnp.float32)).astype(jnp.bfloat16)
    return high, low


def dot(first, second, dims=NN):
    return lax.dot_general(first, second, dims, preferred_element_type=jnp.float32)


def dot3(first, second, dims=NN):
    first_high, first_low = first
    second_high, second_low = second
    return dot(first_high, second_high, dims) + (dot(first_high, second_low, dims) + dot(first_low, second_high, dims))


def picked(parts, chosen):
    return dot(parts[0], chosen) + dot(parts[1], chosen)


def one_hot(index_row, rows, offset=0):
    at = lax.broadcasted_iota(jnp.int32, (rows, index_row.shape[1]), 0) - offset
    return (at == index_row).astype(jnp.float32).astype(jnp.bfloat16)


def lead_kernel(at_ref, index_ref, basis_ref, vector_ref, traces_ref, *rest):
    cut_refs, (held, sems) = rest[:-2], rest[-2:]
    first = pltpu.make_async_copy(basis_ref.at[0], held, sems.at[0])
    first.start()
    copies = []
    for at, out_ref in enumerate(cut_refs):
        chunks = len(cut_refs) // 2
        source = own_columns(vector_ref, (1 - at_ref[0]) * chunks + at % chunks, 2 * (at // chunks), out_ref.shape[2])
        copies.append(pltpu.make_async_copy(source, out_ref, sems.at[1 + at]))
        copies[-1].start()
    first.wait()
    rows = jnp.concatenate([index_ref[0, 0:1], index_ref[0, 1:2]], axis=1)
    traces_ref[...] = picked(split(held[...].T), one_hot(rows, held.shape[0]))
    for copy in copies:
        copy.wait()


def blocks_kernel(
    faces_total, at_ref, index_ref, quad_ref, pair_ref, basis_ref, applied_ref, send_ref, keep_ref, last_ref, held, acted, traces, sems
):
    count = basis_ref.shape[0]
    size = basis_ref.shape[2]
    half = size // 2
    core = at_ref[1]

    def copies(at):
        return (
            pltpu.make_async_copy(basis_ref.at[at], held.at[at], sems.at[2 * at]),
            pltpu.make_async_copy(applied_ref.at[at], acted.at[at], sems.at[2 * at + 1]),
        )

    for at in range(count):
        for copy in copies(at):
            copy.start()

    def store(element, rows, value):
        @pl.when(element // (count // 2) == core)
        def _():
            keep_ref[element % (count // 2), rows] = value

        @pl.when(element // (count // 2) != core)
        def _():
            send_ref[element % (count // 2), rows] = value

    @pl.loop(0, count)
    def _(at):
        for copy in copies(at):
            copy.wait()
        turned = held[at].T
        rows = jnp.concatenate([index_ref[at, place : place + 1] for place in (0, 2, 1, 3)], axis=1)
        found = picked(split(turned), one_hot(rows, held.shape[1]))
        traces[at] = found
        width = found.shape[1] // 2
        outer, layer = found[:, :width], found[:, width:]
        total = dot3(split(turned * quad_ref[pl.ds(at, 1)]), split(acted[at]))
        total = total + dot3(split((2.0 * outer + layer) * (1.0 / faces_total)), split(outer), NT)
        mixed, side, diagonal = packed(0.5 * (total + total.T))
        store(at, slice(size, size + half), jnp.concatenate([mixed, side], axis=1))
        store(at, slice(size + half, None), jnp.broadcast_to(jnp.concatenate([diagonal, diagonal], axis=1), (8, size)))

    @pl.loop(0, count - 1)
    def _(at):
        following = traces[at + 1]
        width = following.shape[1] // 2
        order = one_hot(paired(pair_ref[pl.ds(at, 1)]), width)
        face, inside = picked(split(following[:, :width]), order), picked(split(following[:, width:]), order)
        store(at, slice(0, size), coupled(traces[at], face, inside, faces_total))

    last_ref[...] = traces[count - 1]


def paired(row):
    return jnp.concatenate([jnp.full_like(row, -2 * row.shape[1] - 1), row], axis=1)


def coupled(own, face, inside, faces_total):
    width = own.shape[1] // 2
    outer, layer = own[:, :width], own[:, width:]
    near = split((penalty * outer + 0.5 * layer) * (-1.0 / faces_total))
    far = split(outer * (0.5 / faces_total))
    return dot3(near, split(face), NT) + dot3(far, split(inside), NT)


def last_kernel(faces_total, at_ref, pair_ref, own_ref, lead_ref, send_in, keep_in, send_ref, keep_ref, block, sem):
    width = own_ref.shape[1] // 2
    lead = split(lead_ref[...])
    order = paired(pair_ref[pl.ds(pair_ref.shape[0] - 1, 1)])
    face = picked(lead, one_hot(order, width))
    inside = picked(lead, one_hot(order, width, width // 2))
    block[...] = coupled(own_ref[...], face, inside, faces_total)
    at = send_ref.shape[0] - 1
    rows = pl.ds(0, block.shape[0])
    for core, ref in ((0, send_ref), (1, keep_ref)):

        @pl.when(at_ref[1] == core)
        def _():
            copy = pltpu.make_async_copy(block, ref.at[at, rows], sem)
            copy.start()
            copy.wait()


def packed(volume):
    half = volume.shape[0] // 2
    row = lax.broadcasted_iota(jnp.int32, (half, half), 0)
    column = lax.broadcasted_iota(jnp.int32, (half, half), 1)
    corner = volume[half:, half:]
    mixed = jnp.where(column >= row, volume[:half, :half], corner)
    diagonal = jnp.sum(jnp.where(column == row, corner, 0.0), axis=0, keepdims=True)
    return mixed, volume[:half, half:], diagonal


def unpacked(mixed, side, diagonal):
    half = mixed.shape[0]
    row = lax.broadcasted_iota(jnp.int32, (half, half), 0)
    column = lax.broadcasted_iota(jnp.int32, (half, half), 1)
    turned = mixed.T
    first = jnp.where(column >= row, mixed, turned)
    corner = jnp.where(column < row, mixed, jnp.where(column == row, diagonal, turned))
    top = jnp.concatenate([first, side], axis=1)
    return jnp.concatenate([top, jnp.concatenate([side.T, corner], axis=1)], axis=0)


def weights_kernel(at_ref, *refs):
    sources, (high_ref, low_ref), held, sems = refs[:8], refs[8:10], refs[10], refs[11]
    me = at_ref[3]
    size = held.shape[2]
    half = size // 2
    away_at = (0, 2, 1, 4, 3, 6, 5, 7)
    copies = [pltpu.make_async_copy(source.at[0], held.at[n], sems.at[n]) for n, source in enumerate(sources)]
    for copy in copies:
        copy.start()
    row = lax.broadcasted_iota(jnp.int32, (size, size), 0)
    diagonal = row == lax.broadcasted_iota(jnp.int32, (size, size), 1)

    for n, away in enumerate(away_at):
        copies[n].wait()
        element = away ^ me
        following = lax.rem(element + 1, len(away_at))
        volume, coupling = scaled(held[n], diagonal)
        for place, at, value in ((following, 0, coupling.T), (element, 1, volume), (element, 2, coupling)):
            high_ref[place, :, at * size : (at + 1) * size], low_ref[place, :, at * size : (at + 1) * size] = split(value)


def scaled(block, diagonal):
    size = block.shape[1]
    half = size // 2
    volume = unpacked(block[size : size + half, :half], block[size : size + half, half:], block[size + half : size + half + 1, :half])
    return (volume - jnp.where(diagonal, center, 0.0)) * (1.0 / half_width), block[:size] * (1.0 / half_width)


def outer_kernel(at_ref, kept_ref, swapped_ref, high_in, low_in, high_ref, low_ref):
    size = kept_ref.shape[2]
    rows = kept_ref.shape[1] - size
    row = lax.broadcasted_iota(jnp.int32, (size, size), 0)
    diagonal = row == lax.broadcasted_iota(jnp.int32, (size, size), 1)
    lower = at_ref[1] == 1
    below = jnp.where(lower, kept_ref[0], swapped_ref[0])
    volume, coupling = scaled(below[:rows], diagonal)
    turned = coupling.T
    for at, value in enumerate(((below[rows:] * (1.0 / half_width)).T, volume, coupling)):
        high_ref[0, :, at * size : (at + 1) * size], low_ref[0, :, at * size : (at + 1) * size] = split(value)
    high_ref[1, :, :size], low_ref[1, :, :size] = split(turned)
    high_ref[1, :, size:] = high_in[0, :, size:]
    low_ref[1, :, size:] = low_in[0, :, size:]
    volume, coupling = scaled(jnp.where(lower, swapped_ref[0, :rows], kept_ref[0, :rows]), diagonal)
    last = high_in.shape[0] - 1
    turned = (high_in[last, :, 2 * size :].astype(jnp.float32) + low_in[last, :, 2 * size :].astype(jnp.float32)).T
    for at, value in enumerate((turned, volume, coupling)):
        high_ref[2, :, at * size : (at + 1) * size], low_ref[2, :, at * size : (at + 1) * size] = split(value)


def held_shape(rows, columns):
    return (rows, 2 * columns) if columns % 128 == 0 else (2, rows, columns)


def hold(held, at, value):
    high, low = split(value)
    size, columns = value.shape
    rows = slice(at * size, (at + 1) * size)
    if len(held.shape) == 2:
        held[rows, :columns] = high
        held[rows, columns:] = low
    else:
        held[0, rows] = high
        held[1, rows] = low


def apply_row(high, low, held, start, columns):
    rows = pl.ds(start, high.shape[1])
    if len(held.shape) == 2:
        if columns == 128:
            both = dot(high, held[rows, :])
            total = both[:, :columns] + both[:, columns:]
        else:
            total = dot(high, held[rows, :columns]) + dot(high, held[rows, columns:])
        return total + dot(low, held[rows, :columns])
    return dot(high, held[0, rows]) + (dot(high, held[1, rows]) + dot(low, held[0, rows]))


def hold_all(held, values):
    for at, value in enumerate(values):
        hold(held, at, value)


def first_kernel(high, low, y0, above, y1, held):
    count, size, columns = y0.shape
    hold_all(held, [y0[at] for at in range(count)] + [above[0]])

    @pl.loop(0, count - 1)
    def _(at):
        y1[at] = apply_row(high[at + 1], low[at + 1], held, pl.multiple_of(at * size, size), columns)


def second_kernel(chunks, high, low, outer_high, outer_low, y0, below, above, y1, y1_ends, *refs):
    outs, held = refs[:-1], refs[-1]
    count, size, columns = y0.shape
    row = lambda weight, start: apply_row(*weight, held, start * size, columns)
    outer = lambda at: (outer_high[at], outer_low[at])
    main = lambda at: (high[at], low[at])
    hold_all(held, (below[0], below[1], y0[0], y0[1], y0[count - 1], above[0], above[1]))
    y1_ends[0] = row(outer(0), 0)
    y1_ends[1] = row(outer(1), 1)
    y1_ends[2] = row(outer(2), 4)
    hold_all(held, (y1_ends[0], y1_ends[1], y1[0], y1[1], y1[count - 4], y1[count - 3], y1[count - 2], y1_ends[2]))
    width = columns // chunks
    for out_at, at, weight, start, element in (
        (0, 0, outer(1), 0, 0),
        (0, 1, main(1), 1, 1),
        (1, 0, main(count - 2), 4, count - 2),
        (1, 1, main(count - 1), 5, count - 1),
    ):
        value = 2.0 * row(weight, start) - y0[element]
        for chunk in range(chunks):
            outs[out_at * chunks + chunk][at] = value[:, chunk * width : (chunk + 1) * width]


def middle_kernel(chunks, at_ref, high, low, y0, y1, *refs):
    ends, (y3_kept, y4, send, held, y2, y3) = refs[: 2 * chunks], refs[2 * chunks :]
    count, size, columns = y0.shape
    row = lambda place, at: apply_row(high[place], low[place], held, pl.multiple_of(at * size, size), columns)
    hold_all(held, [y1[at] for at in range(count - 2)])

    @pl.loop(0, count - 4)
    def _(at):
        y2[at] = 2.0 * row(at + 2, at) - y0[at + 2]

    joined = lambda group, at: jnp.concatenate([end[at] for end in ends[group * chunks : (group + 1) * chunks]], axis=1)
    hold_all(held, [joined(0, 0), joined(0, 1)] + [y2[at] for at in range(count - 4)] + [joined(1, 0), joined(1, 1)])

    @pl.loop(0, count - 2)
    def _(at):
        y3[at] = 2.0 * row(at + 1, at) - y1[at]

    hold_all(held, [y3[at] for at in range(count - 2)])

    @pl.loop(0, count - 4)
    def _(at):
        y4[at] = 2.0 * row(at + 2, at) - y2[at]

    send[...] = y4[pl.ds((1 - at_ref[0]) * 2, 2)]
    for at, place in enumerate((0, 1, count - 4, count - 3)):
        y3_kept[at] = y3[place]


def last_rows_kernel(
    lane, at_ref, high, low, outer_high, outer_low, y1, y1_ends, y3, y2_low, y2_high, below, above, y4_low, y4_high, send, held
):
    size, columns = below.shape[1:]
    count = high.shape[0]
    lanes = slice(lane, lane + columns)
    row = lambda weight, start: apply_row(*weight, held, start * size, columns)
    outer = lambda at: (outer_high[at], outer_low[at])
    main = lambda at: (high[at], low[at])
    hold_all(held, (below[0], below[1], y2_low[0], y2_low[1], y2_high[0], y2_high[1], above[0], above[1]))
    lower = 2.0 * row(outer(0), 0) - y1_ends[0, :, lanes]
    low_own = 2.0 * row(outer(1), 1) - y1_ends[1, :, lanes]
    high_own = 2.0 * row(main(count - 1), 4) - y1[count - 2, :, lanes]
    upper = 2.0 * row(outer(2), 5) - y1_ends[2, :, lanes]
    hold_all(held, (lower, low_own, y3[0, :, lanes], y3[1, :, lanes], y3[2, :, lanes], y3[3, :, lanes], high_own, upper))
    y4_low[0] = 2.0 * row(outer(1), 0) - y2_low[0]
    y4_low[1] = 2.0 * row(main(1), 1) - y2_low[1]
    y4_high[0] = 2.0 * row(main(count - 2), 4) - y2_high[0]
    y4_high[1] = 2.0 * row(main(count - 1), 5) - y2_high[1]
    send[...] = jnp.where(at_ref[0] == 0, y4_high[...], y4_low[...])


def fold_kernel(at_ref, keep_ref, other_ref, send_ref, stay_ref):
    lane = at_ref[2]
    half = keep_ref.shape[0] // 2
    for at in range(half):
        send_ref[at] = keep_ref[(1 - lane) * half + at] + other_ref[(1 - lane) * half + at]
        stay_ref[at] = keep_ref[lane * half + at] + other_ref[lane * half + at]


def outer_block_kernel(at_ref, mine_ref, beside_ref, out_ref, sems):
    rows, size = mine_ref.shape[1:]

    def moved(act):
        for wanted, outer, other in ((True, mine_ref, beside_ref), (False, beside_ref, mine_ref)):

            @pl.when((at_ref[1] == at_ref[2]) == wanted)
            def _():
                act(pltpu.make_async_copy(outer.at[0], out_ref.at[0, pl.ds(0, rows)], sems.at[0]))
                act(pltpu.make_async_copy(other.at[0, pl.ds(0, size)], out_ref.at[0, pl.ds(rows, size)], sems.at[1]))

    moved(lambda copy: copy.start())
    moved(lambda copy: copy.wait())


def sum_kernel(first_ref, second_ref, out_ref):
    out_ref[...] = first_ref[...] + second_ref[...]


def copy_pairs(side, pairs, sems):
    def moved(act):
        for at, (wanted, source, target) in enumerate(pairs):

            @pl.when(side == wanted)
            def _():
                act(pltpu.make_async_copy(source, target, sems.at[at]))

    moved(lambda copy: copy.start())
    moved(lambda copy: copy.wait())


def own_columns(vector_ref, half, element, width, count=2):
    if vector_ref.shape[2] == width:
        return vector_ref.at[pl.ds(element, count)]
    return vector_ref.at[pl.ds(element, count), :, pl.ds(pl.multiple_of(half * width, width), width)]


def chunk_of(ref, element, chunk, width):
    rows = pl.ds(element, 2)
    return ref.at[rows] if ref.shape[2] == width else ref.at[rows, :, pl.ds(chunk * width, width)]


def arrange_pair_kernel(element, wanted, at_ref, vector_ref, *refs):
    got_refs, (out_ref, sems) = refs[:-2], refs[-2:]
    pairs = [(wanted, own_columns(vector_ref, at_ref[0], element, out_ref.shape[2]), out_ref)]
    for chunk, got_ref in enumerate(got_refs):
        pairs.append((1 - wanted, got_ref, chunk_of(out_ref, 0, chunk, got_ref.shape[2])))
    copy_pairs(at_ref[0], pairs, sems)


def arrange_kernel(at_ref, vector_ref, *refs):
    got_refs, (out_ref, sems) = refs[:-2], refs[-2:]
    own = own_columns(vector_ref, at_ref[0], 0, out_ref.shape[2], 4)
    chunks = len(got_refs) // 2
    pairs = []
    for side in range(2):
        pairs.append((side, own, out_ref.at[pl.ds(4 * side, 4)]))
        for at, got_ref in enumerate(got_refs):
            element = 4 - 4 * side + 2 * (at // chunks)
            pairs.append((side, got_ref, chunk_of(out_ref, element, at % chunks, got_ref.shape[2])))
    copy_pairs(at_ref[0], pairs, sems)


def place_pairs(out_ref, sems, side, chunks, chunk, width, pairs):
    def moved(act):
        for at, (wanted, source, element, foreign) in enumerate(pairs):

            @pl.when(side == wanted)
            def _():
                part = 1 - side if foreign else side
                start = pl.multiple_of((part * chunks + chunk) * width, width)
                act(pltpu.make_async_copy(source, out_ref.at[pl.ds(element, 2), :, pl.ds(start, width)], sems.at[chunk, at]))

    return moved


def collect_kernel(at_ref, y4, near, out_ref, sems):
    pairs = (
        (0, y4.at[pl.ds(0, 2)], 2, False),
        (0, near, 2, True),
        (1, y4.at[pl.ds(2, 2)], 0, False),
        (1, near, 0, True),
    )
    act = place_pairs(out_ref, sems, at_ref[0], 1, 0, near.shape[2], pairs)
    act(lambda copy: copy.start())
    act(lambda copy: copy.wait())


def finish_kernel(chunks, at_ref, *refs):
    sources, out_ref, sems = refs[: 3 * chunks], refs[-2], refs[-1]
    acts = []
    for chunk in range(chunks):
        y4_low, y4_high, far = sources[3 * chunk : 3 * chunk + 3]
        pairs = ((0, y4_low, 0, False), (0, far, 0, True), (1, y4_high, 2, False), (1, far, 2, True))
        acts.append(place_pairs(out_ref, sems, at_ref[0], chunks, chunk, far.shape[2], pairs))
    for act in acts:
        act(lambda copy: copy.start())
    for act in acts:
        act(lambda copy: copy.wait())


def lead_and_cut(at, index, basis, vector, half, chunks):
    points, size = basis.shape[1:]
    return pl.pallas_call(
        lead_kernel,
        in_specs=[SCALARS, VMEM, ANY, ANY],
        out_specs=[VMEM] * (1 + 2 * chunks),
        out_shape=[near_core((size, 2 * index.shape[2]))] + [near_core((2, size, half // chunks))] * (2 * chunks),
        scratch_shapes=[pltpu.VMEM((points, size), jnp.float32), pltpu.SemaphoreType.DMA((1 + 2 * chunks,))],
        compiler_params=PARAMS,
    )(at, index, far_off(basis), far_off(vector))


def blocks(core, index, quad, pairs, basis, applied, faces_total):
    count, points, size = basis.shape
    spots = 4 * index.shape[2]
    part = near_core((count // 2, size + size // 2 + 8, size))
    return pl.pallas_call(
        functools.partial(blocks_kernel, faces_total),
        in_specs=[SCALARS, VMEM, VMEM, VMEM, ANY, ANY],
        out_specs=[VMEM] * 3,
        out_shape=[part, part, near_core((size, spots))],
        scratch_shapes=[
            pltpu.VMEM((count, points, size), jnp.float32),
            pltpu.VMEM((count, points, size), jnp.float32),
            pltpu.VMEM((count, size, spots), jnp.float32),
            pltpu.SemaphoreType.DMA((2 * count,)),
        ],
        compiler_params=PARAMS,
    )(core, index, quad, pairs, far_off(basis), far_off(applied))


def last_coupling(core, pair, own, lead, send, keep, faces_total):
    size = own.shape[0]
    return pl.pallas_call(
        functools.partial(last_kernel, faces_total),
        in_specs=[SCALARS, VMEM, VMEM, VMEM, ANY, ANY],
        out_specs=[ANY] * 2,
        out_shape=[near_core(send.shape)] * 2,
        input_output_aliases={4: 0, 5: 1},
        scratch_shapes=[pltpu.VMEM((size, size), jnp.float32), pltpu.SemaphoreType.DMA],
        compiler_params=PARAMS,
    )(core, pair, own, lead, send, keep)


def weights(me, *parts):
    rows, size = parts[0].shape[1:]
    return pl.pallas_call(
        weights_kernel,
        in_specs=[SCALARS] + [ANY] * 8,
        out_specs=[VMEM] * 2,
        out_shape=[near_core((8, size, 3 * size), jnp.bfloat16)] * 2,
        scratch_shapes=[pltpu.VMEM((8, rows, size), jnp.float32), pltpu.SemaphoreType.DMA((8,))],
        compiler_params=PARAMS,
    )(me, *[far_off(part) for part in parts])


def outer_weights(at, kept, swapped, high, low):
    size = kept.shape[2]
    return pl.pallas_call(
        outer_kernel,
        in_specs=[SCALARS] + [VMEM] * 4,
        out_specs=[VMEM] * 2,
        out_shape=[near_core((3, size, 3 * size), jnp.bfloat16)] * 2,
        compiler_params=PARAMS,
    )(at, kept, swapped, high, low)


def first_rows(high, low, y0, above):
    count, size, columns = y0.shape
    return pl.pallas_call(
        first_kernel,
        in_specs=[VMEM] * 4,
        out_specs=VMEM,
        out_shape=near_core((count - 1, size, columns)),
        scratch_shapes=[pltpu.VMEM(held_shape((count + 1) * size, columns), jnp.bfloat16)],
        compiler_params=PARAMS,
    )(high, low, y0, above)


def second_rows(chunks, high, low, outer_high, outer_low, y0, below, above, y1):
    count, size, columns = y0.shape
    return pl.pallas_call(
        functools.partial(second_kernel, chunks),
        in_specs=[VMEM] * 8,
        out_specs=[VMEM] * (1 + 2 * chunks),
        out_shape=[near_core((3, size, columns))] + [near_core((2, size, columns // chunks))] * (2 * chunks),
        scratch_shapes=[pltpu.VMEM(held_shape(8 * size, columns), jnp.bfloat16)],
        compiler_params=PARAMS,
    )(high, low, outer_high, outer_low, y0, close_by(below), close_by(above), y1)


def middle_rows(at, chunks, high, low, y0, y1, ends):
    count, size, columns = y0.shape
    return pl.pallas_call(
        functools.partial(middle_kernel, chunks),
        in_specs=[SCALARS] + [VMEM] * (4 + 2 * chunks),
        out_specs=[VMEM] * 3,
        out_shape=[near_core((4, size, columns)), near_core((count - 4, size, columns)), near_core((2, size, columns))],
        scratch_shapes=[
            pltpu.VMEM(held_shape(count * size, columns), jnp.bfloat16),
            pltpu.VMEM((count - 4, size, columns), jnp.float32),
            pltpu.VMEM((count - 2, size, columns), jnp.float32),
        ],
        compiler_params=PARAMS,
    )(at, high, low, y0, y1, *ends)


def last_rows(at, lane, high, low, outer_high, outer_low, y1, y1_ends, y3, y2_low, y2_high, below, above):
    size, columns = below.shape[1:]
    return pl.pallas_call(
        functools.partial(last_rows_kernel, lane),
        in_specs=[SCALARS] + [VMEM] * 11,
        out_specs=[VMEM] * 3,
        out_shape=[near_core(below.shape)] * 3,
        scratch_shapes=[pltpu.VMEM(held_shape(8 * size, columns), jnp.bfloat16)],
        compiler_params=PARAMS,
    )(at, high, low, outer_high, outer_low, y1, y1_ends, y3, y2_low, y2_high, close_by(below), close_by(above))


def folded(lane, keep, other):
    shape = (keep.shape[0] // 2, *keep.shape[1:])
    return pl.pallas_call(
        fold_kernel,
        in_specs=[SCALARS, VMEM, VMEM],
        out_specs=[VMEM] * 2,
        out_shape=[near_core(shape)] * 2,
        compiler_params=PARAMS,
    )(lane, keep, close_by(other))


def outer_block(at, mine, beside):
    return pl.pallas_call(
        outer_block_kernel,
        in_specs=[SCALARS, ANY, ANY],
        out_specs=VMEM,
        out_shape=near_core((1, mine.shape[1] + mine.shape[2], mine.shape[2])),
        scratch_shapes=[pltpu.SemaphoreType.DMA((2,))],
        compiler_params=PARAMS,
    )(at, mine, beside)


def added(first, second):
    return pl.pallas_call(
        sum_kernel, in_specs=[VMEM] * 2, out_specs=VMEM, out_shape=near_core(first.shape), compiler_params=PARAMS
    )(first, close_by(second))


def arranged_pair(at, element, wanted, vector, got):
    _, size, width = got[0].shape
    return pl.pallas_call(
        functools.partial(arrange_pair_kernel, element, wanted),
        in_specs=[SCALARS] + [ANY] * (1 + len(got)),
        out_specs=VMEM,
        out_shape=near_core((2, size, width * len(got))),
        scratch_shapes=[pltpu.SemaphoreType.DMA((1 + len(got),))],
        compiler_params=PARAMS,
    )(at, far_off(vector), *got)


def arranged(at, vector, got):
    _, size, width = got[0].shape
    return pl.pallas_call(
        arrange_kernel,
        in_specs=[SCALARS] + [ANY] * (1 + len(got)),
        out_specs=VMEM,
        out_shape=near_core((8, size, width * len(got) // 2)),
        scratch_shapes=[pltpu.SemaphoreType.DMA((2 + 2 * len(got),))],
        compiler_params=PARAMS,
    )(at, far_off(vector), *got)


def collected(at, y4, near):
    _, size, columns = near.shape
    return pl.pallas_call(
        collect_kernel,
        in_specs=[SCALARS, ANY, ANY],
        out_specs=ANY,
        out_shape=jax.ShapeDtypeStruct((4, size, 2 * columns), jnp.float32),
        scratch_shapes=[pltpu.SemaphoreType.DMA((1, 4))],
        compiler_params=PARAMS,
    )(at, y4, near)


def finished(at, parts, result):
    chunks = len(parts)
    return pl.pallas_call(
        functools.partial(finish_kernel, chunks),
        in_specs=[SCALARS] + [ANY] * (3 * chunks + 1),
        out_specs=ANY,
        out_shape=jax.ShapeDtypeStruct(result.shape, jnp.float32),
        input_output_aliases={1 + 3 * chunks: 0},
        scratch_shapes=[pltpu.SemaphoreType.DMA((chunks, 4))],
        compiler_params=PARAMS,
    )(at, *[value for part in parts for value in part], result)


def flipped(value, axis, bit):
    count = lax.axis_size(axis)
    return lax.ppermute(value, axis, [(i, i ^ bit) for i in range(count)])


def shifted(value, axis, steps):
    count = lax.axis_size(axis)
    return lax.ppermute(value, axis, [(i, (i + steps) % count) for i in range(count)])


def body(basis, applied, quad, face_index, face_pairing, orbitals):
    count, points, size = basis.shape
    spots = face_index.shape[2]
    columns = orbitals.shape[1]
    chunks = 2 if columns % 512 == 0 else 1
    elems, width = lax.axis_size("elem"), lax.axis_size("pts")
    faces_total = float(spots * width)
    side = lax.axis_index("elem") % 2
    core = lax.axis_index("pts") % 2
    lane = lax.axis_index("pts") // 2 % 2
    vector = orbitals.reshape(count, size, columns)
    at = jnp.stack([side, core, lane, side * 4 + core * 2 + lane]).astype(jnp.int32)

    vector, at = lax.optimization_barrier((vector, at))
    wide = columns // 2
    part = wide // chunks
    own = foreign = vector
    if part % 128:
        own = lax.dynamic_slice_in_dim(vector, side * part, part, axis=2)
        foreign = lax.dynamic_slice_in_dim(vector, (1 - side) * part, part, axis=2)
    lead, *got = lead_and_cut(at, face_index, basis, foreign, wide, chunks)
    lead = shifted(lead, "elem", -1)
    got = [flipped(value, "elem", 1) for value in got]

    send, keep, last = blocks(at, face_index, quad, face_pairing, basis, applied, faces_total)
    send, keep = last_coupling(at, face_pairing, last, lead, send, keep, faces_total)
    got[0], send = lax.optimization_barrier((got[0], send))
    send, stay = folded(at, keep, flipped(send, "pts", 1))
    received = flipped(send, "pts", 2)
    pair_low = arranged_pair(at, 0, 0, own, got[:chunks])
    pair_low, received = lax.optimization_barrier((pair_low, received))
    mine = added(stay, received)
    bit = 4
    while bit < width:
        mine = mine + flipped(mine, "pts", bit)
        bit *= 2
    above = shifted(pair_low, "elem", -2)
    beside = flipped(mine, "pts", 2)
    across = flipped(mine, "elem", 1)
    above, beside, across = lax.optimization_barrier((above, beside, across))
    mine_near = flipped(mine, "pts", 1)
    both = flipped(across, "pts", 2)
    beside_near = flipped(beside, "pts", 1)
    across_near = flipped(across, "pts", 1)

    last = outer_block(at, mine, beside)
    flat = lambda e, p: e % elems * width + p
    holds = [(e, p) for e in range(elems) for p in range(width) if e % 2 == p % 2]
    outer = lax.ppermute(last, ("elem", "pts"), [(flat(e, p), flat(e + (2 if p % 2 else -2), p)) for e, p in holds])
    passed = lax.ppermute(outer, ("elem", "pts"), [(flat(e, p), flat(e ^ 1, p)) for e, p in holds])
    got[chunks:], both = lax.optimization_barrier((got[chunks:], both))

    below = shifted(arranged_pair(at, 2, 1, own, got[chunks:]), "elem", 2)
    y0 = arranged(at, own, got)
    both_near = flipped(both, "pts", 1)

    high, low = weights(at, mine, mine_near, beside, across, beside_near, across_near, both, both_near)

    y1 = first_rows(high, low, y0, above)
    below, y1, passed = lax.optimization_barrier((below, y1, passed))
    outer = added(outer, passed)
    high_outer, low_outer = outer_weights(at, outer, flipped(outer, "pts", 1), high, low)
    y1_ends, *ends = second_rows(chunks, high, low, high_outer, low_outer, y0, below, above, y1)
    belows = [shifted(value, "elem", 2) for value in ends[chunks:]]
    aboves = [shifted(value, "elem", -2) for value in ends[:chunks]]
    y3, y4, near = middle_rows(at, chunks, high, low, y0, y1, ends)
    near = flipped(near, "elem", 1)
    parts = []
    for c in range(chunks):
        y4_low, y4_high, far = last_rows(
            at, c * part, high, low, high_outer, low_outer, y1, y1_ends, y3, ends[c], ends[chunks + c], belows[c], aboves[c]
        )
        parts.append((y4_low, y4_high, flipped(far, "elem", 1)))
    if part % 128:
        y4_low, y4_high, far = parts[0]
        mine = jnp.where(side == 0, jnp.concatenate([y4_low, y4[:2]]), jnp.concatenate([y4[2:], y4_high]))
        theirs = jnp.where(side == 0, jnp.concatenate([far, near]), jnp.concatenate([near, far]))
        swap = lambda first, second: jnp.concatenate([first, second], axis=2)
        result = jnp.where(side == 0, swap(mine, theirs), swap(theirs, mine))
    else:
        result = finished(at, parts, collected(at, y4, near))
    return result.reshape(count * size, columns)


def solution(mesh):
    return jax.shard_map(
        body,
        mesh=mesh,
        in_specs=(
            P("elem", "pts", None),
            P("elem", "pts", None),
            P("elem", "pts"),
            P("elem", None, "pts"),
            P("elem", "pts"),
            P("elem", "pts"),
        ),
        out_specs=P("elem", "pts"),
        check_vma=False,
    )
```

```python
import functools

import jax
import jax.numpy as jnp
from jax import lax
from jax.experimental import pallas as pl
from jax.experimental.pallas import tpu as pltpu
from jax.sharding import PartitionSpec as P

NB = 256
DEG = 4

penalty = 3.0
center = 4.0
half_width = 12.0

PARAMS = pltpu.CompilerParams(vmem_limit_bytes=12 * 1024 * 1024)
SCALARS = pl.BlockSpec(memory_space=pltpu.SMEM)
ANY = pl.BlockSpec(memory_space=pl.ANY)


def near_core(shape, dtype=jnp.float32):
    return pltpu.VMEM(shape, dtype)


def far_off(value):
    return pltpu.with_memory_space_constraint(value, pltpu.MemorySpace.HBM)


def close_by(value):
    return pltpu.with_memory_space_constraint(value, pltpu.MemorySpace.VMEM)
VMEM = pl.BlockSpec(memory_space=pltpu.VMEM)
NN = (((1,), (0,)), ((), ()))
NT = (((1,), (1,)), ((), ()))


def split(value):
    high = value.astype(jnp.bfloat16)
    low = (value - high.astype(jnp.float32)).astype(jnp.bfloat16)
    return high, low


def dot(first, second, dims=NN):
    return lax.dot_general(first, second, dims, preferred_element_type=jnp.float32)


def dot3(first, second, dims=NN):
    first_high, first_low = first
    second_high, second_low = second
    return dot(first_high, second_high, dims) + (dot(first_high, second_low, dims) + dot(first_low, second_high, dims))


def picked(parts, chosen):
    return dot(parts[0], chosen) + dot(parts[1], chosen)


def one_hot(index_row, rows, offset=0):
    at = lax.broadcasted_iota(jnp.int32, (rows, index_row.shape[1]), 0) - offset
    return (at == index_row).astype(jnp.float32).astype(jnp.bfloat16)


def lead_kernel(at_ref, index_ref, basis_ref, vector_ref, traces_ref, *rest):
    cut_refs, (held, sems) = rest[:-2], rest[-2:]
    first = pltpu.make_async_copy(basis_ref.at[0], held, sems.at[0])
    first.start()
    copies = []
    for at, out_ref in enumerate(cut_refs):
        chunks = len(cut_refs) // 2
        source = own_columns(vector_ref, (1 - at_ref[0]) * chunks + at % chunks, 2 * (at // chunks), out_ref.shape[2])
        copies.append(pltpu.make_async_copy(source, out_ref, sems.at[1 + at]))
        copies[-1].start()
    first.wait()
    rows = jnp.concatenate([index_ref[0, 0:1], index_ref[0, 1:2]], axis=1)
    traces_ref[...] = picked(split(held[...].T), one_hot(rows, held.shape[0]))
    for copy in copies:
        copy.wait()


def blocks_kernel(
    faces_total, at_ref, index_ref, quad_ref, pair_ref, basis_ref, applied_ref, send_ref, keep_ref, last_ref, held, acted, traces, sems
):
    count = basis_ref.shape[0]
    size = basis_ref.shape[2]
    half = size // 2
    core = at_ref[1]

    def copies(at):
        return (
            pltpu.make_async_copy(basis_ref.at[at], held.at[at], sems.at[2 * at]),
            pltpu.make_async_copy(applied_ref.at[at], acted.at[at], sems.at[2 * at + 1]),
        )

    for at in range(count):
        for copy in copies(at):
            copy.start()

    def store(element, rows, value):
        @pl.when(element // (count // 2) == core)
        def _():
            keep_ref[element % (count // 2), rows] = value

        @pl.when(element // (count // 2) != core)
        def _():
            send_ref[element % (count // 2), rows] = value

    @pl.loop(0, count)
    def _(at):
        for copy in copies(at):
            copy.wait()
        turned = held[at].T
        rows = jnp.concatenate([index_ref[at, place : place + 1] for place in (0, 2, 1, 3)], axis=1)
        found = picked(split(turned), one_hot(rows, held.shape[1]))
        traces[at] = found
        width = found.shape[1] // 2
        outer, layer = found[:, :width], found[:, width:]
        total = dot3(split(turned * quad_ref[pl.ds(at, 1)]), split(acted[at]))
        total = total + dot3(split((2.0 * outer + layer) * (1.0 / faces_total)), split(outer), NT)
        mixed, side, diagonal = packed(0.5 * (total + total.T))
        store(at, slice(size, size + half), jnp.concatenate([mixed, side], axis=1))
        store(at, slice(size + half, None), jnp.broadcast_to(jnp.concatenate([diagonal, diagonal], axis=1), (8, size)))

    @pl.loop(0, count - 1)
    def _(at):
        following = traces[at + 1]
        width = following.shape[1] // 2
        order = one_hot(paired(pair_ref[pl.ds(at, 1)]), width)
        face, inside = picked(split(following[:, :width]), order), picked(split(following[:, width:]), order)
        store(at, slice(0, size), coupled(traces[at], face, inside, faces_total))

    last_ref[...] = traces[count - 1]


def paired(row):
    return jnp.concatenate([jnp.full_like(row, -2 * row.shape[1] - 1), row], axis=1)


def coupled(own, face, inside, faces_total):
    width = own.shape[1] // 2
    outer, layer = own[:, :width], own[:, width:]
    near = split((penalty * outer + 0.5 * layer) * (-1.0 / faces_total))
    far = split(outer * (0.5 / faces_total))
    return dot3(near, split(face), NT) + dot3(far, split(inside), NT)


def last_kernel(faces_total, at_ref, pair_ref, own_ref, lead_ref, send_in, keep_in, send_ref, keep_ref, block, sem):
    width = own_ref.shape[1] // 2
    lead = split(lead_ref[...])
    order = paired(pair_ref[pl.ds(pair_ref.shape[0] - 1, 1)])
    face = picked(lead, one_hot(order, width))
    inside = picked(lead, one_hot(order, width, width // 2))
    block[...] = coupled(own_ref[...], face, inside, faces_total)
    at = send_ref.shape[0] - 1
    rows = pl.ds(0, block.shape[0])
    for core, ref in ((0, send_ref), (1, keep_ref)):

        @pl.when(at_ref[1] == core)
        def _():
            copy = pltpu.make_async_copy(block, ref.at[at, rows], sem)
            copy.start()
            copy.wait()


def packed(volume):
    half = volume.shape[0] // 2
    row = lax.broadcasted_iota(jnp.int32, (half, half), 0)
    column = lax.broadcasted_iota(jnp.int32, (half, half), 1)
    corner = volume[half:, half:]
    mixed = jnp.where(column >= row, volume[:half, :half], corner)
    diagonal = jnp.sum(jnp.where(column == row, corner, 0.0), axis=0, keepdims=True)
    return mixed, volume[:half, half:], diagonal


def unpacked(mixed, side, diagonal):
    half = mixed.shape[0]
    row = lax.broadcasted_iota(jnp.int32, (half, half), 0)
    column = lax.broadcasted_iota(jnp.int32, (half, half), 1)
    turned = mixed.T
    first = jnp.where(column >= row, mixed, turned)
    corner = jnp.where(column < row, mixed, jnp.where(column == row, diagonal, turned))
    top = jnp.concatenate([first, side], axis=1)
    return jnp.concatenate([top, jnp.concatenate([side.T, corner], axis=1)], axis=0)


def weights_kernel(aways, at_ref, *refs):
    sources, (high_ref, low_ref), held, sems = refs[: len(aways)], refs[-4:-2], refs[-2], refs[-1]
    size = held.shape[2]
    copies = [pltpu.make_async_copy(source.at[0], held.at[n], sems.at[n]) for n, source in enumerate(sources)]
    for copy in copies:
        copy.start()
    diagonal = diagonal_of(size)
    for n, away in enumerate(aways):
        copies[n].wait()
        element = away ^ at_ref[3]
        following = lax.rem(element + 1, high_ref.shape[0])
        volume, coupling = scaled(held[n], diagonal)
        for place, at, value in ((following, 0, coupling.T), (element, 1, volume), (element, 2, coupling)):
            high_ref[place, :, at * size : (at + 1) * size], low_ref[place, :, at * size : (at + 1) * size] = split(value)


def late_weights_kernel(aways, at_ref, *refs):
    count = len(aways)
    sources, targets = refs[:count], refs[count + 2 : count + 4]
    held, built, sems, out_sems = refs[count + 4 :]
    size = held.shape[2]
    copies = [pltpu.make_async_copy(source.at[0], held.at[n], sems.at[n]) for n, source in enumerate(sources)]
    for copy in copies:
        copy.start()
    diagonal = diagonal_of(size)
    stores = []
    for n, away in enumerate(aways):
        copies[n].wait()
        element = away ^ at_ref[3]
        following = lax.rem(element + 1, targets[0].shape[0])
        volume, coupling = scaled(held[n], diagonal)
        for at, value in enumerate((coupling.T, volume, coupling)):
            built[n, 0, :, at * size : (at + 1) * size], built[n, 1, :, at * size : (at + 1) * size] = split(value)
        for part, target in enumerate(targets):
            for at, (place, first, last) in enumerate(((following, 0, 1), (element, 1, 3))):
                columns = pl.ds(first * size, (last - first) * size)
                store = pltpu.make_async_copy(built.at[n, part, :, columns], target.at[place, :, columns], out_sems.at[n, part, at])
                store.start()
                stores.append(store)
    for store in stores:
        store.wait()


def diagonal_of(size):
    return lax.broadcasted_iota(jnp.int32, (size, size), 0) == lax.broadcasted_iota(jnp.int32, (size, size), 1)


def scaled(block, diagonal):
    size = block.shape[1]
    half = size // 2
    volume = unpacked(block[size : size + half, :half], block[size : size + half, half:], block[size + half : size + half + 1, :half])
    return (volume - jnp.where(diagonal, center, 0.0)) * (1.0 / half_width), block[:size] * (1.0 / half_width)


def outer_kernel(at_ref, kept_ref, swapped_ref, high_in, low_in, high_ref, low_ref):
    size = kept_ref.shape[2]
    rows = kept_ref.shape[1] - size
    row = lax.broadcasted_iota(jnp.int32, (size, size), 0)
    diagonal = row == lax.broadcasted_iota(jnp.int32, (size, size), 1)
    lower = at_ref[1] == 1
    below = jnp.where(lower, kept_ref[0], swapped_ref[0])
    volume, coupling = scaled(below[:rows], diagonal)
    turned = coupling.T
    for at, value in enumerate(((below[rows:] * (1.0 / half_width)).T, volume, coupling)):
        high_ref[0, :, at * size : (at + 1) * size], low_ref[0, :, at * size : (at + 1) * size] = split(value)
    high_ref[1, :, :size], low_ref[1, :, :size] = split(turned)
    high_ref[1, :, size:] = high_in[0, :, size:]
    low_ref[1, :, size:] = low_in[0, :, size:]
    volume, coupling = scaled(jnp.where(lower, swapped_ref[0, :rows], kept_ref[0, :rows]), diagonal)
    last = high_in.shape[0] - 1
    turned = (high_in[last, :, 2 * size :].astype(jnp.float32) + low_in[last, :, 2 * size :].astype(jnp.float32)).T
    for at, value in enumerate((turned, volume, coupling)):
        high_ref[2, :, at * size : (at + 1) * size], low_ref[2, :, at * size : (at + 1) * size] = split(value)


def held_shape(rows, columns):
    return (rows, 2 * columns) if columns % 128 == 0 else (2, rows, columns)


def hold(held, at, value):
    high, low = split(value)
    size, columns = value.shape
    rows = slice(at * size, (at + 1) * size)
    if len(held.shape) == 2:
        held[rows, :columns] = high
        held[rows, columns:] = low
    else:
        held[0, rows] = high
        held[1, rows] = low


def apply_row(high, low, held, start, columns):
    rows = pl.ds(start, high.shape[1])
    if len(held.shape) == 2:
        if columns == 128:
            both = dot(high, held[rows, :])
            total = both[:, :columns] + both[:, columns:]
        else:
            total = dot(high, held[rows, :columns]) + dot(high, held[rows, columns:])
        return total + dot(low, held[rows, :columns])
    return dot(high, held[0, rows]) + (dot(high, held[1, rows]) + dot(low, held[0, rows]))


def hold_all(held, values):
    for at, value in enumerate(values):
        hold(held, at, value)


def first_kernel(high, low, y0, above, y1, held):
    count, size, columns = y0.shape
    hold_all(held, [y0[at] for at in range(count)] + [above[0]])

    @pl.loop(0, count - 1, unroll=7)
    def _(at):
        y1[at] = apply_row(high[at + 1], low[at + 1], held, pl.multiple_of(at * size, size), columns)


def second_kernel(chunks, high, low, outer_high, outer_low, y0, below, above, y1, y1_ends, *refs):
    outs, held = refs[:-1], refs[-1]
    count, size, columns = y0.shape
    row = lambda weight, start: apply_row(*weight, held, start * size, columns)
    outer = lambda at: (outer_high[at], outer_low[at])
    main = lambda at: (high[at], low[at])
    hold_all(held, (below[0], below[1], y0[0], y0[1], y0[count - 1], above[0], above[1]))
    y1_ends[0] = row(outer(0), 0)
    y1_ends[1] = row(outer(1), 1)
    y1_ends[2] = row(outer(2), 4)
    hold_all(held, (y1_ends[0], y1_ends[1], y1[0], y1[1], y1[count - 4], y1[count - 3], y1[count - 2], y1_ends[2]))
    width = columns // chunks
    for out_at, at, weight, start, element in (
        (0, 0, outer(1), 0, 0),
        (0, 1, main(1), 1, 1),
        (1, 0, main(count - 2), 4, count - 2),
        (1, 1, main(count - 1), 5, count - 1),
    ):
        value = 2.0 * row(weight, start) - y0[element]
        for chunk in range(chunks):
            outs[out_at * chunks + chunk][at] = value[:, chunk * width : (chunk + 1) * width]


def middle_kernel(chunks, at_ref, high, low, y0, y1, *refs):
    ends, (y3_kept, y4, send, held, y2, y3) = refs[: 2 * chunks], refs[2 * chunks :]
    count, size, columns = y0.shape
    row = lambda place, at: apply_row(high[place], low[place], held, pl.multiple_of(at * size, size), columns)
    hold_all(held, [y1[at] for at in range(count - 2)])

    @pl.loop(0, count - 4, unroll=4)
    def _(at):
        y2[at] = 2.0 * row(at + 2, at) - y0[at + 2]

    joined = lambda group, at: jnp.concatenate([end[at] for end in ends[group * chunks : (group + 1) * chunks]], axis=1)
    hold_all(held, [joined(0, 0), joined(0, 1)] + [y2[at] for at in range(count - 4)] + [joined(1, 0), joined(1, 1)])

    @pl.loop(0, count - 2, unroll=6)
    def _(at):
        y3[at] = 2.0 * row(at + 1, at) - y1[at]

    hold_all(held, [y3[at] for at in range(count - 2)])

    @pl.loop(0, count - 4, unroll=4)
    def _(at):
        y4[at] = 2.0 * row(at + 2, at) - y2[at]

    send[...] = y4[pl.ds((1 - at_ref[0]) * 2, 2)]
    for at, place in enumerate((0, 1, count - 4, count - 3)):
        y3_kept[at] = y3[place]


def last_rows_kernel(
    lane, at_ref, high, low, outer_high, outer_low, y1, y1_ends, y3, y2_low, y2_high, below, above, y4_low, y4_high, send, held
):
    size, columns = below.shape[1:]
    count = high.shape[0]
    lanes = slice(lane, lane + columns)
    row = lambda weight, start: apply_row(*weight, held, start * size, columns)
    outer = lambda at: (outer_high[at], outer_low[at])
    main = lambda at: (high[at], low[at])
    hold_all(held, (below[0], below[1], y2_low[0], y2_low[1], y2_high[0], y2_high[1], above[0], above[1]))
    lower = 2.0 * row(outer(0), 0) - y1_ends[0, :, lanes]
    low_own = 2.0 * row(outer(1), 1) - y1_ends[1, :, lanes]
    high_own = 2.0 * row(main(count - 1), 4) - y1[count - 2, :, lanes]
    upper = 2.0 * row(outer(2), 5) - y1_ends[2, :, lanes]
    hold_all(held, (lower, low_own, y3[0, :, lanes], y3[1, :, lanes], y3[2, :, lanes], y3[3, :, lanes], high_own, upper))
    y4_low[0] = 2.0 * row(outer(1), 0) - y2_low[0]
    y4_low[1] = 2.0 * row(main(1), 1) - y2_low[1]
    y4_high[0] = 2.0 * row(main(count - 2), 4) - y2_high[0]
    y4_high[1] = 2.0 * row(main(count - 1), 5) - y2_high[1]
    send[...] = jnp.where(at_ref[0] == 0, y4_high[...], y4_low[...])


def fold_kernel(at_ref, keep_ref, other_ref, send_ref, stay_ref):
    lane = at_ref[2]
    half = keep_ref.shape[0] // 2
    for at in range(half):
        send_ref[at] = keep_ref[(1 - lane) * half + at] + other_ref[(1 - lane) * half + at]
        stay_ref[at] = keep_ref[lane * half + at] + other_ref[lane * half + at]


def outer_block_kernel(at_ref, mine_ref, beside_ref, out_ref, sems):
    rows, size = mine_ref.shape[1:]

    def moved(act):
        for wanted, outer, other in ((True, mine_ref, beside_ref), (False, beside_ref, mine_ref)):

            @pl.when((at_ref[1] == at_ref[2]) == wanted)
            def _():
                act(pltpu.make_async_copy(outer.at[0], out_ref.at[0, pl.ds(0, rows)], sems.at[0]))
                act(pltpu.make_async_copy(other.at[0, pl.ds(0, size)], out_ref.at[0, pl.ds(rows, size)], sems.at[1]))

    moved(lambda copy: copy.start())
    moved(lambda copy: copy.wait())


def sum_kernel(first_ref, second_ref, out_ref):
    out_ref[...] = first_ref[...] + second_ref[...]


def copy_pairs(side, pairs, sems):
    def moved(act):
        for at, (wanted, source, target) in enumerate(pairs):

            @pl.when(side == wanted)
            def _():
                act(pltpu.make_async_copy(source, target, sems.at[at]))

    moved(lambda copy: copy.start())
    moved(lambda copy: copy.wait())


def own_columns(vector_ref, half, element, width, count=2):
    if vector_ref.shape[2] == width:
        return vector_ref.at[pl.ds(element, count)]
    return vector_ref.at[pl.ds(element, count), :, pl.ds(pl.multiple_of(half * width, width), width)]


def chunk_of(ref, element, chunk, width):
    rows = pl.ds(element, 2)
    return ref.at[rows] if ref.shape[2] == width else ref.at[rows, :, pl.ds(chunk * width, width)]


def arrange_pair_kernel(element, wanted, at_ref, vector_ref, *refs):
    got_refs, (out_ref, sems) = refs[:-2], refs[-2:]
    pairs = [(wanted, own_columns(vector_ref, at_ref[0], element, out_ref.shape[2]), out_ref)]
    for chunk, got_ref in enumerate(got_refs):
        pairs.append((1 - wanted, got_ref, chunk_of(out_ref, 0, chunk, got_ref.shape[2])))
    copy_pairs(at_ref[0], pairs, sems)


def arrange_kernel(at_ref, vector_ref, *refs):
    got_refs, (out_ref, sems) = refs[:-2], refs[-2:]
    own = own_columns(vector_ref, at_ref[0], 0, out_ref.shape[2], 4)
    chunks = len(got_refs) // 2
    pairs = []
    for side in range(2):
        pairs.append((side, own, out_ref.at[pl.ds(4 * side, 4)]))
        for at, got_ref in enumerate(got_refs):
            element = 4 - 4 * side + 2 * (at // chunks)
            pairs.append((side, got_ref, chunk_of(out_ref, element, at % chunks, got_ref.shape[2])))
    copy_pairs(at_ref[0], pairs, sems)


def place_pairs(out_ref, sems, side, chunks, chunk, width, pairs):
    def moved(act):
        for at, (wanted, source, element, foreign) in enumerate(pairs):

            @pl.when(side == wanted)
            def _():
                part = 1 - side if foreign else side
                start = pl.multiple_of((part * chunks + chunk) * width, width)
                act(pltpu.make_async_copy(source, out_ref.at[pl.ds(element, 2), :, pl.ds(start, width)], sems.at[chunk, at]))

    return moved


def collect_kernel(at_ref, y4, near, out_ref, sems):
    pairs = (
        (0, y4.at[pl.ds(0, 2)], 2, False),
        (0, near, 2, True),
        (1, y4.at[pl.ds(2, 2)], 0, False),
        (1, near, 0, True),
    )
    act = place_pairs(out_ref, sems, at_ref[0], 1, 0, near.shape[2], pairs)
    act(lambda copy: copy.start())
    act(lambda copy: copy.wait())


def finish_kernel(chunks, at_ref, *refs):
    sources, out_ref, sems = refs[: 3 * chunks], refs[-2], refs[-1]
    acts = []
    for chunk in range(chunks):
        y4_low, y4_high, far = sources[3 * chunk : 3 * chunk + 3]
        pairs = ((0, y4_low, 0, False), (0, far, 0, True), (1, y4_high, 2, False), (1, far, 2, True))
        acts.append(place_pairs(out_ref, sems, at_ref[0], chunks, chunk, far.shape[2], pairs))
    for act in acts:
        act(lambda copy: copy.start())
    for act in acts:
        act(lambda copy: copy.wait())


def lead_and_cut(at, index, basis, vector, half, chunks):
    points, size = basis.shape[1:]
    return pl.pallas_call(
        lead_kernel,
        in_specs=[SCALARS, VMEM, ANY, ANY],
        out_specs=[VMEM] * (1 + 2 * chunks),
        out_shape=[near_core((size, 2 * index.shape[2]))] + [near_core((2, size, half // chunks))] * (2 * chunks),
        scratch_shapes=[pltpu.VMEM((points, size), jnp.float32), pltpu.SemaphoreType.DMA((1 + 2 * chunks,))],
        compiler_params=PARAMS,
    )(at, index, far_off(basis), far_off(vector))


def blocks(core, index, quad, pairs, basis, applied, faces_total):
    count, points, size = basis.shape
    spots = 4 * index.shape[2]
    part = near_core((count // 2, size + size // 2 + 8, size))
    return pl.pallas_call(
        functools.partial(blocks_kernel, faces_total),
        in_specs=[SCALARS, VMEM, VMEM, VMEM, ANY, ANY],
        out_specs=[VMEM] * 3,
        out_shape=[part, part, near_core((size, spots))],
        scratch_shapes=[
            pltpu.VMEM((count, points, size), jnp.float32),
            pltpu.VMEM((count, points, size), jnp.float32),
            pltpu.VMEM((count, size, spots), jnp.float32),
            pltpu.SemaphoreType.DMA((2 * count,)),
        ],
        compiler_params=PARAMS,
    )(core, index, quad, pairs, far_off(basis), far_off(applied))


def last_coupling(core, pair, own, lead, send, keep, faces_total):
    size = own.shape[0]
    return pl.pallas_call(
        functools.partial(last_kernel, faces_total),
        in_specs=[SCALARS, VMEM, VMEM, VMEM, ANY, ANY],
        out_specs=[ANY] * 2,
        out_shape=[near_core(send.shape)] * 2,
        input_output_aliases={4: 0, 5: 1},
        scratch_shapes=[pltpu.VMEM((size, size), jnp.float32), pltpu.SemaphoreType.DMA],
        compiler_params=PARAMS,
    )(core, pair, own, lead, send, keep)


def weights(at, pieces):
    aways = tuple(pieces)
    rows, size = pieces[aways[0]].shape[1:]
    return pl.pallas_call(
        functools.partial(weights_kernel, aways),
        in_specs=[SCALARS] + [ANY] * len(aways),
        out_specs=[VMEM] * 2,
        out_shape=[near_core((8, size, 3 * size), jnp.bfloat16)] * 2,
        scratch_shapes=[pltpu.VMEM((len(aways), rows, size), jnp.float32), pltpu.SemaphoreType.DMA((len(aways),))],
        compiler_params=PARAMS,
    )(at, *pieces.values())


def late_weights(at, pieces, high, low):
    aways = tuple(pieces)
    count = len(aways)
    rows, size = pieces[aways[0]].shape[1:]
    return pl.pallas_call(
        functools.partial(late_weights_kernel, aways),
        in_specs=[SCALARS] + [ANY] * (count + 2),
        out_specs=[ANY] * 2,
        out_shape=[near_core(high.shape, jnp.bfloat16)] * 2,
        input_output_aliases={1 + count: 0, 2 + count: 1},
        scratch_shapes=[
            pltpu.VMEM((count, rows, size), jnp.float32),
            pltpu.VMEM((count, 2, size, 3 * size), jnp.bfloat16),
            pltpu.SemaphoreType.DMA((count,)),
            pltpu.SemaphoreType.DMA((count, 2, 2)),
        ],
        compiler_params=PARAMS,
    )(at, *pieces.values(), high, low)


def outer_weights(at, kept, swapped, high, low):
    size = kept.shape[2]
    return pl.pallas_call(
        outer_kernel,
        in_specs=[SCALARS] + [VMEM] * 4,
        out_specs=[VMEM] * 2,
        out_shape=[near_core((3, size, 3 * size), jnp.bfloat16)] * 2,
        compiler_params=PARAMS,
    )(at, kept, swapped, high, low)


def first_rows(high, low, y0, above):
    count, size, columns = y0.shape
    return pl.pallas_call(
        first_kernel,
        in_specs=[VMEM] * 4,
        out_specs=VMEM,
        out_shape=near_core((count - 1, size, columns)),
        scratch_shapes=[pltpu.VMEM(held_shape((count + 1) * size, columns), jnp.bfloat16)],
        compiler_params=PARAMS,
    )(high, low, y0, above)


def second_rows(chunks, high, low, outer_high, outer_low, y0, below, above, y1):
    count, size, columns = y0.shape
    return pl.pallas_call(
        functools.partial(second_kernel, chunks),
        in_specs=[VMEM] * 8,
        out_specs=[VMEM] * (1 + 2 * chunks),
        out_shape=[near_core((3, size, columns))] + [near_core((2, size, columns // chunks))] * (2 * chunks),
        scratch_shapes=[pltpu.VMEM(held_shape(8 * size, columns), jnp.bfloat16)],
        compiler_params=PARAMS,
    )(high, low, outer_high, outer_low, y0, close_by(below), close_by(above), y1)


def middle_rows(at, chunks, high, low, y0, y1, ends):
    count, size, columns = y0.shape
    return pl.pallas_call(
        functools.partial(middle_kernel, chunks),
        in_specs=[SCALARS] + [VMEM] * (4 + 2 * chunks),
        out_specs=[VMEM] * 3,
        out_shape=[near_core((4, size, columns)), near_core((count - 4, size, columns)), near_core((2, size, columns))],
        scratch_shapes=[
            pltpu.VMEM(held_shape(count * size, columns), jnp.bfloat16),
            pltpu.VMEM((count - 4, size, columns), jnp.float32),
            pltpu.VMEM((count - 2, size, columns), jnp.float32),
        ],
        compiler_params=PARAMS,
    )(at, high, low, y0, y1, *ends)


def last_rows(at, lane, high, low, outer_high, outer_low, y1, y1_ends, y3, y2_low, y2_high, below, above):
    size, columns = below.shape[1:]
    return pl.pallas_call(
        functools.partial(last_rows_kernel, lane),
        in_specs=[SCALARS] + [VMEM] * 11,
        out_specs=[VMEM] * 3,
        out_shape=[near_core(below.shape)] * 3,
        scratch_shapes=[pltpu.VMEM(held_shape(8 * size, columns), jnp.bfloat16)],
        compiler_params=PARAMS,
    )(at, high, low, outer_high, outer_low, y1, y1_ends, y3, y2_low, y2_high, close_by(below), close_by(above))


def folded(lane, keep, other):
    shape = (keep.shape[0] // 2, *keep.shape[1:])
    return pl.pallas_call(
        fold_kernel,
        in_specs=[SCALARS, VMEM, VMEM],
        out_specs=[VMEM] * 2,
        out_shape=[near_core(shape)] * 2,
        compiler_params=PARAMS,
    )(lane, keep, close_by(other))


def outer_block(at, mine, beside):
    return pl.pallas_call(
        outer_block_kernel,
        in_specs=[SCALARS, ANY, ANY],
        out_specs=VMEM,
        out_shape=near_core((1, mine.shape[1] + mine.shape[2], mine.shape[2])),
        scratch_shapes=[pltpu.SemaphoreType.DMA((2,))],
        compiler_params=PARAMS,
    )(at, mine, beside)


def added(first, second):
    return pl.pallas_call(
        sum_kernel, in_specs=[VMEM] * 2, out_specs=VMEM, out_shape=near_core(first.shape), compiler_params=PARAMS
    )(first, close_by(second))


def arranged_pair(at, element, wanted, vector, got):
    _, size, width = got[0].shape
    return pl.pallas_call(
        functools.partial(arrange_pair_kernel, element, wanted),
        in_specs=[SCALARS] + [ANY] * (1 + len(got)),
        out_specs=VMEM,
        out_shape=near_core((2, size, width * len(got))),
        scratch_shapes=[pltpu.SemaphoreType.DMA((1 + len(got),))],
        compiler_params=PARAMS,
    )(at, far_off(vector), *got)


def arranged(at, vector, got):
    _, size, width = got[0].shape
    return pl.pallas_call(
        arrange_kernel,
        in_specs=[SCALARS] + [ANY] * (1 + len(got)),
        out_specs=VMEM,
        out_shape=near_core((8, size, width * len(got) // 2)),
        scratch_shapes=[pltpu.SemaphoreType.DMA((2 + 2 * len(got),))],
        compiler_params=PARAMS,
    )(at, far_off(vector), *got)


def collected(at, y4, near):
    _, size, columns = near.shape
    return pl.pallas_call(
        collect_kernel,
        in_specs=[SCALARS, ANY, ANY],
        out_specs=ANY,
        out_shape=jax.ShapeDtypeStruct((4, size, 2 * columns), jnp.float32),
        scratch_shapes=[pltpu.SemaphoreType.DMA((1, 4))],
        compiler_params=PARAMS,
    )(at, y4, near)


def finished(at, parts, result):
    chunks = len(parts)
    return pl.pallas_call(
        functools.partial(finish_kernel, chunks),
        in_specs=[SCALARS] + [ANY] * (3 * chunks + 1),
        out_specs=ANY,
        out_shape=jax.ShapeDtypeStruct(result.shape, jnp.float32),
        input_output_aliases={1 + 3 * chunks: 0},
        scratch_shapes=[pltpu.SemaphoreType.DMA((chunks, 4))],
        compiler_params=PARAMS,
    )(at, *[value for part in parts for value in part], result)


def flipped(value, axis, bit):
    count = lax.axis_size(axis)
    return lax.ppermute(value, axis, [(i, i ^ bit) for i in range(count)])


def shifted(value, axis, steps):
    count = lax.axis_size(axis)
    return lax.ppermute(value, axis, [(i, (i + steps) % count) for i in range(count)])


def body(basis, applied, quad, face_index, face_pairing, orbitals):
    count, points, size = basis.shape
    spots = face_index.shape[2]
    columns = orbitals.shape[1]
    chunks = 2 if columns % 512 == 0 else 1
    elems, width = lax.axis_size("elem"), lax.axis_size("pts")
    faces_total = float(spots * width)
    side = lax.axis_index("elem") % 2
    core = lax.axis_index("pts") % 2
    lane = lax.axis_index("pts") // 2 % 2
    vector = orbitals.reshape(count, size, columns)
    at = jnp.stack([side, core, lane, side * 4 + core * 2 + lane]).astype(jnp.int32)

    vector, at = lax.optimization_barrier((vector, at))
    wide = columns // 2
    part = wide // chunks
    own = foreign = vector
    if part % 128:
        own = lax.dynamic_slice_in_dim(vector, side * part, part, axis=2)
        foreign = lax.dynamic_slice_in_dim(vector, (1 - side) * part, part, axis=2)
    lead, *got = lead_and_cut(at, face_index, basis, foreign, wide, chunks)
    lead = shifted(lead, "elem", -1)
    got = [flipped(value, "elem", 1) for value in got]

    send, keep, last = blocks(at, face_index, quad, face_pairing, basis, applied, faces_total)
    send, keep = last_coupling(at, face_pairing, last, lead, send, keep, faces_total)
    got[0], send = lax.optimization_barrier((got[0], send))
    send, stay = folded(at, keep, flipped(send, "pts", 1))
    received = flipped(send, "pts", 2)
    pair_low = arranged_pair(at, 0, 0, own, got[:chunks])
    pair_low, received = lax.optimization_barrier((pair_low, received))
    mine = added(stay, received)
    bit = 4
    while bit < width:
        mine = mine + flipped(mine, "pts", bit)
        bit *= 2
    above = shifted(pair_low, "elem", -2)
    beside = flipped(mine, "pts", 2)
    across = flipped(mine, "elem", 1)
    above, beside, across, got[chunks] = lax.optimization_barrier((above, beside, across, got[chunks]))
    mine_near = flipped(mine, "pts", 1)
    both = flipped(across, "pts", 2)
    beside_near = flipped(beside, "pts", 1)
    across_near = flipped(across, "pts", 1)

    last = outer_block(at, mine, beside)
    flat = lambda e, p: e % elems * width + p
    holds = [(e, p) for e in range(elems) for p in range(width) if e % 2 == p % 2]
    outer = lax.ppermute(last, ("elem", "pts"), [(flat(e, p), flat(e + (2 if p % 2 else -2), p)) for e, p in holds])
    passed = lax.ppermute(outer, ("elem", "pts"), [(flat(e, p), flat(e ^ 1, p)) for e, p in holds])
    got[chunks:], both = lax.optimization_barrier((got[chunks:], both))

    below = shifted(arranged_pair(at, 2, 1, own, got[chunks:]), "elem", 2)
    y0 = arranged(at, own, got)
    both_near = flipped(both, "pts", 1)

    high, low = weights(at, {0: mine, 2: mine_near, 1: beside, 4: across, 3: beside_near, 6: across_near})
    high, low = late_weights(at, {5: both, 7: both_near}, high, low)

    y1 = first_rows(high, low, y0, above)
    below, y1, passed = lax.optimization_barrier((below, y1, passed))
    outer = added(outer, passed)
    high_outer, low_outer = outer_weights(at, outer, flipped(outer, "pts", 1), high, low)
    y1_ends, *ends = second_rows(chunks, high, low, high_outer, low_outer, y0, below, above, y1)
    belows = [shifted(value, "elem", 2) for value in ends[chunks:]]
    aboves = [shifted(value, "elem", -2) for value in ends[:chunks]]
    y3, y4, near = middle_rows(at, chunks, high, low, y0, y1, ends)
    near = flipped(near, "elem", 1)
    parts = []
    for c in range(chunks):
        y4_low, y4_high, far = last_rows(
            at, c * part, high, low, high_outer, low_outer, y1, y1_ends, y3, ends[c], ends[chunks + c], belows[c], aboves[c]
        )
        parts.append((y4_low, y4_high, flipped(far, "elem", 1)))
    if part % 128:
        y4_low, y4_high, far = parts[0]
        mine = jnp.where(side == 0, jnp.concatenate([y4_low, y4[:2]]), jnp.concatenate([y4[2:], y4_high]))
        theirs = jnp.where(side == 0, jnp.concatenate([far, near]), jnp.concatenate([near, far]))
        swap = lambda first, second: jnp.concatenate([first, second], axis=2)
        result = jnp.where(side == 0, swap(mine, theirs), swap(theirs, mine))
    else:
        result = finished(at, parts, collected(at, y4, near))
    return result.reshape(count * size, columns)


def solution(mesh):
    return jax.shard_map(
        body,
        mesh=mesh,
        in_specs=(
            P("elem", "pts", None),
            P("elem", "pts", None),
            P("elem", "pts"),
            P("elem", None, "pts"),
            P("elem", "pts"),
            P("elem", "pts"),
        ),
        out_specs=P("elem", "pts"),
        check_vma=False,
    )
```

```python
import functools

import jax
import jax.numpy as jnp
from jax import lax
from jax.experimental import pallas as pl
from jax.experimental.pallas import tpu as pltpu
from jax.sharding import PartitionSpec as P

NB = 256
DEG = 4

penalty = 3.0
center = 4.0
half_width = 12.0

PARAMS = pltpu.CompilerParams(vmem_limit_bytes=12 * 1024 * 1024)
SCALARS = pl.BlockSpec(memory_space=pltpu.SMEM)
ANY = pl.BlockSpec(memory_space=pl.ANY)


def near_core(shape, dtype=jnp.float32):
    return pltpu.VMEM(shape, dtype)


def far_off(value):
    return pltpu.with_memory_space_constraint(value, pltpu.MemorySpace.HBM)


def close_by(value):
    return pltpu.with_memory_space_constraint(value, pltpu.MemorySpace.VMEM)
VMEM = pl.BlockSpec(memory_space=pltpu.VMEM)
NN = (((1,), (0,)), ((), ()))
NT = (((1,), (1,)), ((), ()))


def split(value):
    high = value.astype(jnp.bfloat16)
    low = (value - high.astype(jnp.float32)).astype(jnp.bfloat16)
    return high, low


def dot(first, second, dims=NN):
    return lax.dot_general(first, second, dims, preferred_element_type=jnp.float32)


def dot3(first, second, dims=NN):
    first_high, first_low = first
    second_high, second_low = second
    return dot(first_high, second_high, dims) + (dot(first_high, second_low, dims) + dot(first_low, second_high, dims))


def picked(parts, chosen):
    return dot(parts[0], chosen) + dot(parts[1], chosen)


def one_hot(index_row, rows, offset=0):
    at = lax.broadcasted_iota(jnp.int32, (rows, index_row.shape[1]), 0) - offset
    return (at == index_row).astype(jnp.float32).astype(jnp.bfloat16)


def lead_kernel(at_ref, index_ref, basis_ref, vector_ref, traces_ref, *rest):
    cut_refs, (held, sems) = rest[:-2], rest[-2:]
    first = pltpu.make_async_copy(basis_ref.at[0], held, sems.at[0])
    first.start()
    copies = []
    for at, out_ref in enumerate(cut_refs):
        chunks = len(cut_refs) // 2
        source = own_columns(vector_ref, (1 - at_ref[0]) * chunks + at % chunks, 2 * (at // chunks), out_ref.shape[2])
        copies.append(pltpu.make_async_copy(source, out_ref, sems.at[1 + at]))
        copies[-1].start()
    first.wait()
    rows = jnp.concatenate([index_ref[0, 0:1], index_ref[0, 1:2]], axis=1)
    traces_ref[...] = picked(split(held[...].T), one_hot(rows, held.shape[0]))
    for copy in copies:
        copy.wait()


def blocks_kernel(
    faces_total, at_ref, index_ref, quad_ref, pair_ref, basis_ref, applied_ref, send_ref, keep_ref, last_ref, held, acted, traces, sems
):
    count = basis_ref.shape[0]
    size = basis_ref.shape[2]
    half = size // 2
    core = at_ref[1]

    def copies(at):
        return (
            pltpu.make_async_copy(basis_ref.at[at], held.at[at], sems.at[2 * at]),
            pltpu.make_async_copy(applied_ref.at[at], acted.at[at], sems.at[2 * at + 1]),
        )

    for at in range(count):
        for copy in copies(at):
            copy.start()

    def store(element, rows, value):
        @pl.when(element // (count // 2) == core)
        def _():
            keep_ref[element % (count // 2), rows] = value

        @pl.when(element // (count // 2) != core)
        def _():
            send_ref[element % (count // 2), rows] = value

    @pl.loop(0, count)
    def _(at):
        for copy in copies(at):
            copy.wait()
        turned = held[at].T
        rows = jnp.concatenate([index_ref[at, place : place + 1] for place in (0, 2, 1, 3)], axis=1)
        found = picked(split(turned), one_hot(rows, held.shape[1]))
        traces[at] = found
        width = found.shape[1] // 2
        outer, layer = found[:, :width], found[:, width:]
        total = dot3(split(turned * quad_ref[pl.ds(at, 1)]), split(acted[at]))
        total = total + dot3(split((2.0 * outer + layer) * (1.0 / faces_total)), split(outer), NT)
        mixed, side, diagonal = packed(0.5 * (total + total.T))
        store(at, slice(size, size + half), jnp.concatenate([mixed, side], axis=1))
        store(at, slice(size + half, None), jnp.broadcast_to(jnp.concatenate([diagonal, diagonal], axis=1), (8, size)))

    @pl.loop(0, count - 1)
    def _(at):
        following = traces[at + 1]
        width = following.shape[1] // 2
        order = one_hot(paired(pair_ref[pl.ds(at, 1)]), width)
        face, inside = picked(split(following[:, :width]), order), picked(split(following[:, width:]), order)
        store(at, slice(0, size), coupled(traces[at], face, inside, faces_total))

    last_ref[...] = traces[count - 1]


def paired(row):
    return jnp.concatenate([jnp.full_like(row, -2 * row.shape[1] - 1), row], axis=1)


def coupled(own, face, inside, faces_total):
    width = own.shape[1] // 2
    outer, layer = own[:, :width], own[:, width:]
    near = split((penalty * outer + 0.5 * layer) * (-1.0 / faces_total))
    far = split(outer * (0.5 / faces_total))
    return dot3(near, split(face), NT) + dot3(far, split(inside), NT)


def last_kernel(faces_total, at_ref, pair_ref, own_ref, lead_ref, send_in, keep_in, send_ref, keep_ref, block, sem):
    width = own_ref.shape[1] // 2
    lead = split(lead_ref[...])
    order = paired(pair_ref[pl.ds(pair_ref.shape[0] - 1, 1)])
    face = picked(lead, one_hot(order, width))
    inside = picked(lead, one_hot(order, width, width // 2))
    block[...] = coupled(own_ref[...], face, inside, faces_total)
    at = send_ref.shape[0] - 1
    rows = pl.ds(0, block.shape[0])
    for core, ref in ((0, send_ref), (1, keep_ref)):

        @pl.when(at_ref[1] == core)
        def _():
            copy = pltpu.make_async_copy(block, ref.at[at, rows], sem)
            copy.start()
            copy.wait()


def packed(volume):
    half = volume.shape[0] // 2
    row = lax.broadcasted_iota(jnp.int32, (half, half), 0)
    column = lax.broadcasted_iota(jnp.int32, (half, half), 1)
    corner = volume[half:, half:]
    mixed = jnp.where(column >= row, volume[:half, :half], corner)
    diagonal = jnp.sum(jnp.where(column == row, corner, 0.0), axis=0, keepdims=True)
    return mixed, volume[:half, half:], diagonal


def unpacked(mixed, side, diagonal):
    half = mixed.shape[0]
    row = lax.broadcasted_iota(jnp.int32, (half, half), 0)
    column = lax.broadcasted_iota(jnp.int32, (half, half), 1)
    turned = mixed.T
    first = jnp.where(column >= row, mixed, turned)
    corner = jnp.where(column < row, mixed, jnp.where(column == row, diagonal, turned))
    top = jnp.concatenate([first, side], axis=1)
    return jnp.concatenate([top, jnp.concatenate([side.T, corner], axis=1)], axis=0)


def weights_kernel(aways, at_ref, *refs):
    sources, (high_ref, low_ref), held, sems = refs[: len(aways)], refs[-4:-2], refs[-2], refs[-1]
    size = held.shape[2]
    copies = [pltpu.make_async_copy(source.at[0], held.at[n], sems.at[n]) for n, source in enumerate(sources)]
    for copy in copies:
        copy.start()
    diagonal = diagonal_of(size)
    for n, away in enumerate(aways):
        copies[n].wait()
        element = away ^ at_ref[3]
        following = lax.rem(element + 1, high_ref.shape[0])
        volume, coupling = scaled(held[n], diagonal)
        for place, at, value in ((following, 0, coupling.T), (element, 1, volume), (element, 2, coupling)):
            high_ref[place, :, at * size : (at + 1) * size], low_ref[place, :, at * size : (at + 1) * size] = split(value)


def late_weights_kernel(aways, at_ref, *refs):
    count = len(aways)
    sources, targets = refs[:count], refs[count + 2 : count + 4]
    held, built, sems, out_sems = refs[count + 4 :]
    size = held.shape[2]
    copies = [pltpu.make_async_copy(source.at[0], held.at[n], sems.at[n]) for n, source in enumerate(sources)]
    for copy in copies:
        copy.start()
    diagonal = diagonal_of(size)
    stores = []
    for n, away in enumerate(aways):
        copies[n].wait()
        element = away ^ at_ref[3]
        following = lax.rem(element + 1, targets[0].shape[0])
        volume, coupling = scaled(held[n], diagonal)
        for at, value in enumerate((coupling.T, volume, coupling)):
            built[n, 0, :, at * size : (at + 1) * size], built[n, 1, :, at * size : (at + 1) * size] = split(value)
        for part, target in enumerate(targets):
            for at, (place, first, last) in enumerate(((following, 0, 1), (element, 1, 3))):
                columns = pl.ds(first * size, (last - first) * size)
                store = pltpu.make_async_copy(built.at[n, part, :, columns], target.at[place, :, columns], out_sems.at[n, part, at])
                store.start()
                stores.append(store)
    for store in stores:
        store.wait()


def diagonal_of(size):
    return lax.broadcasted_iota(jnp.int32, (size, size), 0) == lax.broadcasted_iota(jnp.int32, (size, size), 1)


def scaled(block, diagonal):
    size = block.shape[1]
    half = size // 2
    volume = unpacked(block[size : size + half, :half], block[size : size + half, half:], block[size + half : size + half + 1, :half])
    return (volume - jnp.where(diagonal, center, 0.0)) * (1.0 / half_width), block[:size] * (1.0 / half_width)


def outer_kernel(at_ref, kept_ref, swapped_ref, high_in, low_in, high_ref, low_ref):
    size = kept_ref.shape[2]
    rows = kept_ref.shape[1] - size
    row = lax.broadcasted_iota(jnp.int32, (size, size), 0)
    diagonal = row == lax.broadcasted_iota(jnp.int32, (size, size), 1)
    lower = at_ref[1] == 1
    below = jnp.where(lower, kept_ref[0], swapped_ref[0])
    volume, coupling = scaled(below[:rows], diagonal)
    turned = coupling.T
    for at, value in enumerate(((below[rows:] * (1.0 / half_width)).T, volume, coupling)):
        high_ref[0, :, at * size : (at + 1) * size], low_ref[0, :, at * size : (at + 1) * size] = split(value)
    high_ref[1, :, :size], low_ref[1, :, :size] = split(turned)
    high_ref[1, :, size:] = high_in[0, :, size:]
    low_ref[1, :, size:] = low_in[0, :, size:]
    volume, coupling = scaled(jnp.where(lower, swapped_ref[0, :rows], kept_ref[0, :rows]), diagonal)
    last = high_in.shape[0] - 1
    turned = (high_in[last, :, 2 * size :].astype(jnp.float32) + low_in[last, :, 2 * size :].astype(jnp.float32)).T
    for at, value in enumerate((turned, volume, coupling)):
        high_ref[2, :, at * size : (at + 1) * size], low_ref[2, :, at * size : (at + 1) * size] = split(value)


def held_shape(rows, columns):
    return (rows, 2 * columns) if columns % 128 == 0 else (2, rows, columns)


def hold(held, at, value):
    high, low = split(value)
    size, columns = value.shape
    rows = slice(at * size, (at + 1) * size)
    if len(held.shape) == 2:
        held[rows, :columns] = high
        held[rows, columns:] = low
    else:
        held[0, rows] = high
        held[1, rows] = low


def apply_row(high, low, held, start, columns):
    rows = pl.ds(start, high.shape[1])
    if len(held.shape) == 2:
        if columns == 128:
            both = dot(high, held[rows, :])
            total = both[:, :columns] + both[:, columns:]
        else:
            total = dot(high, held[rows, :columns]) + dot(high, held[rows, columns:])
        return total + dot(low, held[rows, :columns])
    return dot(high, held[0, rows]) + (dot(high, held[1, rows]) + dot(low, held[0, rows]))


def hold_all(held, values):
    for at, value in enumerate(values):
        hold(held, at, value)


def first_kernel(high, low, y0, above, y1, held):
    count, size, columns = y0.shape
    hold_all(held, [y0[at] for at in range(count)] + [above[0]])

    @pl.loop(0, count - 1, unroll=7)
    def _(at):
        y1[at] = apply_row(high[at + 1], low[at + 1], held, pl.multiple_of(at * size, size), columns)


def second_kernel(chunks, high, low, outer_high, outer_low, y0, below, above, y1, y1_ends, *refs):
    outs, held = refs[:-1], refs[-1]
    count, size, columns = y0.shape
    row = lambda weight, start: apply_row(*weight, held, start * size, columns)
    outer = lambda at: (outer_high[at], outer_low[at])
    main = lambda at: (high[at], low[at])
    hold_all(held, (below[0], below[1], y0[0], y0[1], y0[count - 1], above[0], above[1]))
    y1_ends[0] = row(outer(0), 0)
    y1_ends[1] = row(outer(1), 1)
    y1_ends[2] = row(outer(2), 4)
    hold_all(held, (y1_ends[0], y1_ends[1], y1[0], y1[1], y1[count - 4], y1[count - 3], y1[count - 2], y1_ends[2]))
    width = columns // chunks
    for out_at, at, weight, start, element in (
        (0, 0, outer(1), 0, 0),
        (0, 1, main(1), 1, 1),
        (1, 0, main(count - 2), 4, count - 2),
        (1, 1, main(count - 1), 5, count - 1),
    ):
        value = 2.0 * row(weight, start) - y0[element]
        for chunk in range(chunks):
            outs[out_at * chunks + chunk][at] = value[:, chunk * width : (chunk + 1) * width]


def middle_kernel(chunks, at_ref, high, low, y0, y1, *refs):
    ends, (y3_kept, y4, send, held, y2, y3) = refs[: 2 * chunks], refs[2 * chunks :]
    count, size, columns = y0.shape
    row = lambda place, at: apply_row(high[place], low[place], held, pl.multiple_of(at * size, size), columns)
    hold_all(held, [y1[at] for at in range(count - 2)])

    @pl.loop(0, count - 4, unroll=4)
    def _(at):
        y2[at] = 2.0 * row(at + 2, at) - y0[at + 2]

    joined = lambda group, at: jnp.concatenate([end[at] for end in ends[group * chunks : (group + 1) * chunks]], axis=1)
    hold_all(held, [joined(0, 0), joined(0, 1)] + [y2[at] for at in range(count - 4)] + [joined(1, 0), joined(1, 1)])

    @pl.loop(0, count - 2, unroll=6)
    def _(at):
        y3[at] = 2.0 * row(at + 1, at) - y1[at]

    hold_all(held, [y3[at] for at in range(count - 2)])

    @pl.loop(0, count - 4, unroll=4)
    def _(at):
        y4[at] = 2.0 * row(at + 2, at) - y2[at]

    send[...] = y4[pl.ds((1 - at_ref[0]) * 2, 2)]
    for at, place in enumerate((0, 1, count - 4, count - 3)):
        y3_kept[at] = y3[place]


def last_rows_kernel(
    lane, foreign, at_ref, high, low, outer_high, outer_low, y1, y1_ends, y3, y2_low, y2_high, below, above, y4, held
):
    size, columns = below.shape[1:]
    count = high.shape[0]
    lanes = slice(lane, lane + columns)
    row = lambda weight, start: apply_row(*weight, held, start * size, columns)
    outer = lambda at: (outer_high[at], outer_low[at])
    main = lambda at: (high[at], low[at])

    @pl.when((at_ref[0] == 0) == foreign)
    def _():
        hold_all(held, (y2_high[0], y2_high[1], above[0], above[1]))
        inside = 2.0 * row(main(count - 1), 0) - y1[count - 2, :, lanes]
        outside = 2.0 * row(outer(2), 1) - y1_ends[2, :, lanes]
        hold_all(held, (y3[2, :, lanes], y3[3, :, lanes], inside, outside))
        y4[0] = 2.0 * row(main(count - 2), 0) - y2_high[0]
        y4[1] = 2.0 * row(main(count - 1), 1) - y2_high[1]

    @pl.when((at_ref[0] == 0) != foreign)
    def _():
        hold_all(held, (below[0], below[1], y2_low[0], y2_low[1]))
        outside = 2.0 * row(outer(0), 0) - y1_ends[0, :, lanes]
        inside = 2.0 * row(outer(1), 1) - y1_ends[1, :, lanes]
        hold_all(held, (outside, inside, y3[0, :, lanes], y3[1, :, lanes]))
        y4[0] = 2.0 * row(outer(1), 0) - y2_low[0]
        y4[1] = 2.0 * row(main(1), 1) - y2_low[1]


def fold_kernel(at_ref, keep_ref, other_ref, send_ref, stay_ref):
    lane = at_ref[2]
    half = keep_ref.shape[0] // 2
    for at in range(half):
        send_ref[at] = keep_ref[(1 - lane) * half + at] + other_ref[(1 - lane) * half + at]
        stay_ref[at] = keep_ref[lane * half + at] + other_ref[lane * half + at]


def outer_block_kernel(at_ref, mine_ref, beside_ref, out_ref, sems):
    rows, size = mine_ref.shape[1:]

    def moved(act):
        for wanted, outer, other in ((True, mine_ref, beside_ref), (False, beside_ref, mine_ref)):

            @pl.when((at_ref[1] == at_ref[2]) == wanted)
            def _():
                act(pltpu.make_async_copy(outer.at[0], out_ref.at[0, pl.ds(0, rows)], sems.at[0]))
                act(pltpu.make_async_copy(other.at[0, pl.ds(0, size)], out_ref.at[0, pl.ds(rows, size)], sems.at[1]))

    moved(lambda copy: copy.start())
    moved(lambda copy: copy.wait())


def sum_kernel(first_ref, second_ref, out_ref):
    out_ref[...] = first_ref[...] + second_ref[...]


def copy_pairs(side, pairs, sems):
    def moved(act):
        for at, (wanted, source, target) in enumerate(pairs):

            @pl.when(side == wanted)
            def _():
                act(pltpu.make_async_copy(source, target, sems.at[at]))

    moved(lambda copy: copy.start())
    moved(lambda copy: copy.wait())


def own_columns(vector_ref, half, element, width, count=2):
    if vector_ref.shape[2] == width:
        return vector_ref.at[pl.ds(element, count)]
    return vector_ref.at[pl.ds(element, count), :, pl.ds(pl.multiple_of(half * width, width), width)]


def chunk_of(ref, element, chunk, width):
    rows = pl.ds(element, 2)
    return ref.at[rows] if ref.shape[2] == width else ref.at[rows, :, pl.ds(chunk * width, width)]


def arrange_pair_kernel(element, wanted, at_ref, vector_ref, *refs):
    got_refs, (out_ref, sems) = refs[:-2], refs[-2:]
    pairs = [(wanted, own_columns(vector_ref, at_ref[0], element, out_ref.shape[2]), out_ref)]
    for chunk, got_ref in enumerate(got_refs):
        pairs.append((1 - wanted, got_ref, chunk_of(out_ref, 0, chunk, got_ref.shape[2])))
    copy_pairs(at_ref[0], pairs, sems)


def arrange_kernel(at_ref, vector_ref, *refs):
    got_refs, (out_ref, sems) = refs[:-2], refs[-2:]
    own = own_columns(vector_ref, at_ref[0], 0, out_ref.shape[2], 4)
    chunks = len(got_refs) // 2
    pairs = []
    for side in range(2):
        pairs.append((side, own, out_ref.at[pl.ds(4 * side, 4)]))
        for at, got_ref in enumerate(got_refs):
            element = 4 - 4 * side + 2 * (at // chunks)
            pairs.append((side, got_ref, chunk_of(out_ref, element, at % chunks, got_ref.shape[2])))
    copy_pairs(at_ref[0], pairs, sems)


def place_pairs(out_ref, sems, side, chunks, chunk, width, pairs):
    def moved(act):
        for at, (wanted, source, element, foreign) in enumerate(pairs):

            @pl.when(side == wanted)
            def _():
                part = 1 - side if foreign else side
                start = pl.multiple_of((part * chunks + chunk) * width, width)
                act(pltpu.make_async_copy(source, out_ref.at[pl.ds(element, 2), :, pl.ds(start, width)], sems.at[chunk, at]))

    return moved


def collect_kernel(at_ref, y4, near, out_ref, sems):
    pairs = (
        (0, y4.at[pl.ds(0, 2)], 2, False),
        (0, near, 2, True),
        (1, y4.at[pl.ds(2, 2)], 0, False),
        (1, near, 0, True),
    )
    act = place_pairs(out_ref, sems, at_ref[0], 1, 0, near.shape[2], pairs)
    act(lambda copy: copy.start())
    act(lambda copy: copy.wait())


def finish_kernel(chunks, at_ref, *refs):
    sources, out_ref, sems = refs[: 2 * chunks], refs[-2], refs[-1]
    acts = []
    for chunk in range(chunks):
        own, far = sources[2 * chunk : 2 * chunk + 2]
        pairs = ((0, own, 0, False), (0, far, 0, True), (1, own, 2, False), (1, far, 2, True))
        acts.append(place_pairs(out_ref, sems, at_ref[0], chunks, chunk, far.shape[2], pairs))
    for act in acts:
        act(lambda copy: copy.start())
    for act in acts:
        act(lambda copy: copy.wait())


def lead_and_cut(at, index, basis, vector, half, chunks):
    points, size = basis.shape[1:]
    return pl.pallas_call(
        lead_kernel,
        in_specs=[SCALARS, VMEM, ANY, ANY],
        out_specs=[VMEM] * (1 + 2 * chunks),
        out_shape=[near_core((size, 2 * index.shape[2]))] + [near_core((2, size, half // chunks))] * (2 * chunks),
        scratch_shapes=[pltpu.VMEM((points, size), jnp.float32), pltpu.SemaphoreType.DMA((1 + 2 * chunks,))],
        compiler_params=PARAMS,
    )(at, index, far_off(basis), far_off(vector))


def blocks(core, index, quad, pairs, basis, applied, faces_total):
    count, points, size = basis.shape
    spots = 4 * index.shape[2]
    part = near_core((count // 2, size + size // 2 + 8, size))
    return pl.pallas_call(
        functools.partial(blocks_kernel, faces_total),
        in_specs=[SCALARS, VMEM, VMEM, VMEM, ANY, ANY],
        out_specs=[VMEM] * 3,
        out_shape=[part, part, near_core((size, spots))],
        scratch_shapes=[
            pltpu.VMEM((count, points, size), jnp.float32),
            pltpu.VMEM((count, points, size), jnp.float32),
            pltpu.VMEM((count, size, spots), jnp.float32),
            pltpu.SemaphoreType.DMA((2 * count,)),
        ],
        compiler_params=PARAMS,
    )(core, index, quad, pairs, far_off(basis), far_off(applied))


def last_coupling(core, pair, own, lead, send, keep, faces_total):
    size = own.shape[0]
    return pl.pallas_call(
        functools.partial(last_kernel, faces_total),
        in_specs=[SCALARS, VMEM, VMEM, VMEM, ANY, ANY],
        out_specs=[ANY] * 2,
        out_shape=[near_core(send.shape)] * 2,
        input_output_aliases={4: 0, 5: 1},
        scratch_shapes=[pltpu.VMEM((size, size), jnp.float32), pltpu.SemaphoreType.DMA],
        compiler_params=PARAMS,
    )(core, pair, own, lead, send, keep)


def weights(at, pieces):
    aways = tuple(pieces)
    rows, size = pieces[aways[0]].shape[1:]
    return pl.pallas_call(
        functools.partial(weights_kernel, aways),
        in_specs=[SCALARS] + [ANY] * len(aways),
        out_specs=[VMEM] * 2,
        out_shape=[near_core((8, size, 3 * size), jnp.bfloat16)] * 2,
        scratch_shapes=[pltpu.VMEM((len(aways), rows, size), jnp.float32), pltpu.SemaphoreType.DMA((len(aways),))],
        compiler_params=PARAMS,
    )(at, *pieces.values())


def late_weights(at, pieces, high, low):
    aways = tuple(pieces)
    count = len(aways)
    rows, size = pieces[aways[0]].shape[1:]
    return pl.pallas_call(
        functools.partial(late_weights_kernel, aways),
        in_specs=[SCALARS] + [ANY] * (count + 2),
        out_specs=[ANY] * 2,
        out_shape=[near_core(high.shape, jnp.bfloat16)] * 2,
        input_output_aliases={1 + count: 0, 2 + count: 1},
        scratch_shapes=[
            pltpu.VMEM((count, rows, size), jnp.float32),
            pltpu.VMEM((count, 2, size, 3 * size), jnp.bfloat16),
            pltpu.SemaphoreType.DMA((count,)),
            pltpu.SemaphoreType.DMA((count, 2, 2)),
        ],
        compiler_params=PARAMS,
    )(at, *pieces.values(), high, low)


def outer_weights(at, kept, swapped, high, low):
    size = kept.shape[2]
    return pl.pallas_call(
        outer_kernel,
        in_specs=[SCALARS] + [VMEM] * 4,
        out_specs=[VMEM] * 2,
        out_shape=[near_core((3, size, 3 * size), jnp.bfloat16)] * 2,
        compiler_params=PARAMS,
    )(at, kept, swapped, high, low)


def first_rows(high, low, y0, above):
    count, size, columns = y0.shape
    return pl.pallas_call(
        first_kernel,
        in_specs=[VMEM] * 4,
        out_specs=VMEM,
        out_shape=near_core((count - 1, size, columns)),
        scratch_shapes=[pltpu.VMEM(held_shape((count + 1) * size, columns), jnp.bfloat16)],
        compiler_params=PARAMS,
    )(high, low, y0, above)


def second_rows(chunks, high, low, outer_high, outer_low, y0, below, above, y1):
    count, size, columns = y0.shape
    return pl.pallas_call(
        functools.partial(second_kernel, chunks),
        in_specs=[VMEM] * 8,
        out_specs=[VMEM] * (1 + 2 * chunks),
        out_shape=[near_core((3, size, columns))] + [near_core((2, size, columns // chunks))] * (2 * chunks),
        scratch_shapes=[pltpu.VMEM(held_shape(8 * size, columns), jnp.bfloat16)],
        compiler_params=PARAMS,
    )(high, low, outer_high, outer_low, y0, close_by(below), close_by(above), y1)


def middle_rows(at, chunks, high, low, y0, y1, ends):
    count, size, columns = y0.shape
    return pl.pallas_call(
        functools.partial(middle_kernel, chunks),
        in_specs=[SCALARS] + [VMEM] * (4 + 2 * chunks),
        out_specs=[VMEM] * 3,
        out_shape=[near_core((4, size, columns)), near_core((count - 4, size, columns)), near_core((2, size, columns))],
        scratch_shapes=[
            pltpu.VMEM(held_shape(count * size, columns), jnp.bfloat16),
            pltpu.VMEM((count - 4, size, columns), jnp.float32),
            pltpu.VMEM((count - 2, size, columns), jnp.float32),
        ],
        compiler_params=PARAMS,
    )(at, high, low, y0, y1, *ends)


def last_rows(at, lane, foreign, high, low, outer_high, outer_low, y1, y1_ends, y3, y2_low, y2_high, below, above):
    size, columns = below.shape[1:]
    return pl.pallas_call(
        functools.partial(last_rows_kernel, lane, foreign),
        in_specs=[SCALARS] + [VMEM] * 11,
        out_specs=VMEM,
        out_shape=near_core(below.shape),
        scratch_shapes=[pltpu.VMEM(held_shape(4 * size, columns), jnp.bfloat16)],
        compiler_params=PARAMS,
    )(at, high, low, outer_high, outer_low, y1, y1_ends, y3, y2_low, y2_high, close_by(below), close_by(above))


def folded(lane, keep, other):
    shape = (keep.shape[0] // 2, *keep.shape[1:])
    return pl.pallas_call(
        fold_kernel,
        in_specs=[SCALARS, VMEM, VMEM],
        out_specs=[VMEM] * 2,
        out_shape=[near_core(shape)] * 2,
        compiler_params=PARAMS,
    )(lane, keep, close_by(other))


def outer_block(at, mine, beside):
    return pl.pallas_call(
        outer_block_kernel,
        in_specs=[SCALARS, ANY, ANY],
        out_specs=VMEM,
        out_shape=near_core((1, mine.shape[1] + mine.shape[2], mine.shape[2])),
        scratch_shapes=[pltpu.SemaphoreType.DMA((2,))],
        compiler_params=PARAMS,
    )(at, mine, beside)


def added(first, second):
    return pl.pallas_call(
        sum_kernel, in_specs=[VMEM] * 2, out_specs=VMEM, out_shape=near_core(first.shape), compiler_params=PARAMS
    )(first, close_by(second))


def arranged_pair(at, element, wanted, vector, got):
    _, size, width = got[0].shape
    return pl.pallas_call(
        functools.partial(arrange_pair_kernel, element, wanted),
        in_specs=[SCALARS] + [ANY] * (1 + len(got)),
        out_specs=VMEM,
        out_shape=near_core((2, size, width * len(got))),
        scratch_shapes=[pltpu.SemaphoreType.DMA((1 + len(got),))],
        compiler_params=PARAMS,
    )(at, far_off(vector), *got)


def arranged(at, vector, got):
    _, size, width = got[0].shape
    return pl.pallas_call(
        arrange_kernel,
        in_specs=[SCALARS] + [ANY] * (1 + len(got)),
        out_specs=VMEM,
        out_shape=near_core((8, size, width * len(got) // 2)),
        scratch_shapes=[pltpu.SemaphoreType.DMA((2 + 2 * len(got),))],
        compiler_params=PARAMS,
    )(at, far_off(vector), *got)


def collected(at, y4, near):
    _, size, columns = near.shape
    return pl.pallas_call(
        collect_kernel,
        in_specs=[SCALARS, ANY, ANY],
        out_specs=ANY,
        out_shape=jax.ShapeDtypeStruct((4, size, 2 * columns), jnp.float32),
        scratch_shapes=[pltpu.SemaphoreType.DMA((1, 4))],
        compiler_params=PARAMS,
    )(at, y4, near)


def finished(at, parts, result):
    chunks = len(parts)
    return pl.pallas_call(
        functools.partial(finish_kernel, chunks),
        in_specs=[SCALARS] + [ANY] * (2 * chunks + 1),
        out_specs=ANY,
        out_shape=jax.ShapeDtypeStruct(result.shape, jnp.float32),
        input_output_aliases={1 + 2 * chunks: 0},
        scratch_shapes=[pltpu.SemaphoreType.DMA((chunks, 4))],
        compiler_params=PARAMS,
    )(at, *[value for part in parts for value in part], result)


def flipped(value, axis, bit):
    count = lax.axis_size(axis)
    return lax.ppermute(value, axis, [(i, i ^ bit) for i in range(count)])


def shifted(value, axis, steps):
    count = lax.axis_size(axis)
    return lax.ppermute(value, axis, [(i, (i + steps) % count) for i in range(count)])


def body(basis, applied, quad, face_index, face_pairing, orbitals):
    count, points, size = basis.shape
    spots = face_index.shape[2]
    columns = orbitals.shape[1]
    chunks = 2 if columns % 512 == 0 else 1
    elems, width = lax.axis_size("elem"), lax.axis_size("pts")
    faces_total = float(spots * width)
    side = lax.axis_index("elem") % 2
    core = lax.axis_index("pts") % 2
    lane = lax.axis_index("pts") // 2 % 2
    vector = orbitals.reshape(count, size, columns)
    at = jnp.stack([side, core, lane, side * 4 + core * 2 + lane]).astype(jnp.int32)

    vector, at = lax.optimization_barrier((vector, at))
    wide = columns // 2
    part = wide // chunks
    own = foreign = vector
    if part % 128:
        own = lax.dynamic_slice_in_dim(vector, side * part, part, axis=2)
        foreign = lax.dynamic_slice_in_dim(vector, (1 - side) * part, part, axis=2)
    lead, *got = lead_and_cut(at, face_index, basis, foreign, wide, chunks)
    lead = shifted(lead, "elem", -1)
    got = [flipped(value, "elem", 1) for value in got]

    send, keep, last = blocks(at, face_index, quad, face_pairing, basis, applied, faces_total)
    send, keep = last_coupling(at, face_pairing, last, lead, send, keep, faces_total)
    got[0], send = lax.optimization_barrier((got[0], send))
    send, stay = folded(at, keep, flipped(send, "pts", 1))
    received = flipped(send, "pts", 2)
    pair_low = arranged_pair(at, 0, 0, own, got[:chunks])
    pair_low, received = lax.optimization_barrier((pair_low, received))
    mine = added(stay, received)
    bit = 4
    while bit < width:
        mine = mine + flipped(mine, "pts", bit)
        bit *= 2
    above = shifted(pair_low, "elem", -2)
    beside = flipped(mine, "pts", 2)
    across = flipped(mine, "elem", 1)
    above, beside, across, got[chunks] = lax.optimization_barrier((above, beside, across, got[chunks]))
    mine_near = flipped(mine, "pts", 1)
    both = flipped(across, "pts", 2)
    beside_near = flipped(beside, "pts", 1)
    across_near = flipped(across, "pts", 1)

    last = outer_block(at, mine, beside)
    flat = lambda e, p: e % elems * width + p
    holds = [(e, p) for e in range(elems) for p in range(width) if e % 2 == p % 2]
    outer = lax.ppermute(last, ("elem", "pts"), [(flat(e, p), flat(e + (2 if p % 2 else -2), p)) for e, p in holds])
    passed = lax.ppermute(outer, ("elem", "pts"), [(flat(e, p), flat(e ^ 1, p)) for e, p in holds])

    outer, got[-1] = lax.optimization_barrier((outer, got[-1]))
    below = shifted(arranged_pair(at, 2, 1, own, got[chunks:]), "elem", 2)
    y0 = arranged(at, own, got)
    both_near = flipped(both, "pts", 1)

    high, low = weights(at, {0: mine, 2: mine_near, 1: beside, 4: across, 3: beside_near, 6: across_near})
    high, low = late_weights(at, {5: both, 7: both_near}, high, low)

    y1 = first_rows(high, low, y0, above)
    below, y1, passed = lax.optimization_barrier((below, y1, passed))
    outer = added(outer, passed)
    high_outer, low_outer = outer_weights(at, outer, flipped(outer, "pts", 1), high, low)
    y1_ends, *ends = second_rows(chunks, high, low, high_outer, low_outer, y0, below, above, y1)
    belows = [shifted(value, "elem", 2) for value in ends[chunks:]]
    aboves = [shifted(value, "elem", -2) for value in ends[:chunks]]
    y3, y4, near = middle_rows(at, chunks, high, low, y0, y1, ends)
    near = flipped(near, "elem", 1)
    parts = []
    for c in range(chunks):
        given = (high, low, high_outer, low_outer, y1, y1_ends, y3, ends[c], ends[chunks + c], belows[c], aboves[c])
        far = flipped(last_rows(at, c * part, True, *given), "elem", 1)
        parts.append((last_rows(at, c * part, False, *given), far))
    if part % 128:
        ((ends_own, far),) = parts
        mine = jnp.where(side == 0, jnp.concatenate([ends_own, y4[:2]]), jnp.concatenate([y4[2:], ends_own]))
        theirs = jnp.where(side == 0, jnp.concatenate([far, near]), jnp.concatenate([near, far]))
        swap = lambda first, second: jnp.concatenate([first, second], axis=2)
        result = jnp.where(side == 0, swap(mine, theirs), swap(theirs, mine))
    else:
        result = finished(at, parts, collected(at, y4, near))
    return result.reshape(count * size, columns)


def solution(mesh):
    return jax.shard_map(
        body,
        mesh=mesh,
        in_specs=(
            P("elem", "pts", None),
            P("elem", "pts", None),
            P("elem", "pts"),
            P("elem", None, "pts"),
            P("elem", "pts"),
            P("elem", "pts"),
        ),
        out_specs=P("elem", "pts"),
        check_vma=False,
    )
```

```python
import functools

import jax
import jax.numpy as jnp
from jax import lax
from jax.experimental import pallas as pl
from jax.experimental.pallas import tpu as pltpu
from jax.sharding import PartitionSpec as P

NB = 256
DEG = 4

penalty = 3.0
center = 4.0
half_width = 12.0

PARAMS = pltpu.CompilerParams(vmem_limit_bytes=12 * 1024 * 1024)
SCALARS = pl.BlockSpec(memory_space=pltpu.SMEM)
ANY = pl.BlockSpec(memory_space=pl.ANY)


def near_core(shape, dtype=jnp.float32):
    return pltpu.VMEM(shape, dtype)


def far_off(value):
    return pltpu.with_memory_space_constraint(value, pltpu.MemorySpace.HBM)


def close_by(value):
    return pltpu.with_memory_space_constraint(value, pltpu.MemorySpace.VMEM)
VMEM = pl.BlockSpec(memory_space=pltpu.VMEM)
NN = (((1,), (0,)), ((), ()))
NT = (((1,), (1,)), ((), ()))


def split(value):
    high = value.astype(jnp.bfloat16)
    low = (value - high.astype(jnp.float32)).astype(jnp.bfloat16)
    return high, low


def dot(first, second, dims=NN):
    return lax.dot_general(first, second, dims, preferred_element_type=jnp.float32)


def dot3(first, second, dims=NN):
    first_high, first_low = first
    second_high, second_low = second
    return dot(first_high, second_high, dims) + (dot(first_high, second_low, dims) + dot(first_low, second_high, dims))


def picked(parts, chosen):
    return dot(parts[0], chosen) + dot(parts[1], chosen)


def one_hot(index_row, rows, offset=0):
    at = lax.broadcasted_iota(jnp.int32, (rows, index_row.shape[1]), 0) - offset
    return (at == index_row).astype(jnp.float32).astype(jnp.bfloat16)


def lead_kernel(at_ref, index_ref, basis_ref, vector_ref, traces_ref, *rest):
    cut_refs, (held, sems) = rest[:-2], rest[-2:]
    first = pltpu.make_async_copy(basis_ref.at[0], held, sems.at[0])
    first.start()
    copies = []
    for at, out_ref in enumerate(cut_refs):
        chunks = len(cut_refs) // 2
        source = own_columns(vector_ref, (1 - at_ref[0]) * chunks + at % chunks, 2 * (at // chunks), out_ref.shape[2])
        copies.append(pltpu.make_async_copy(source, out_ref, sems.at[1 + at]))
        copies[-1].start()
    first.wait()
    rows = jnp.concatenate([index_ref[0, 0:1], index_ref[0, 1:2]], axis=1)
    traces_ref[...] = picked(split(held[...].T), one_hot(rows, held.shape[0]))
    for copy in copies:
        copy.wait()


def blocks_kernel(
    faces_total, at_ref, index_ref, quad_ref, pair_ref, basis_ref, applied_ref, send_ref, keep_ref, last_ref, held, acted, traces, sems
):
    count = basis_ref.shape[0]
    size = basis_ref.shape[2]
    half = size // 2
    core = at_ref[1]

    def copies(at):
        return (
            pltpu.make_async_copy(basis_ref.at[at], held.at[at], sems.at[2 * at]),
            pltpu.make_async_copy(applied_ref.at[at], acted.at[at], sems.at[2 * at + 1]),
        )

    for at in range(count):
        for copy in copies(at):
            copy.start()

    def store(element, rows, value):
        @pl.when(element // (count // 2) == core)
        def _():
            keep_ref[element % (count // 2), rows] = value

        @pl.when(element // (count // 2) != core)
        def _():
            send_ref[element % (count // 2), rows] = value

    @pl.loop(0, count)
    def _(at):
        for copy in copies(at):
            copy.wait()
        turned = held[at].T
        rows = jnp.concatenate([index_ref[at, place : place + 1] for place in (0, 2, 1, 3)], axis=1)
        found = picked(split(turned), one_hot(rows, held.shape[1]))
        traces[at] = found
        width = found.shape[1] // 2
        outer, layer = found[:, :width], found[:, width:]
        total = dot3(split(turned * quad_ref[pl.ds(at, 1)]), split(acted[at]))
        total = total + dot3(split((2.0 * outer + layer) * (1.0 / faces_total)), split(outer), NT)
        mixed, side, diagonal = packed(0.5 * (total + total.T))
        store(at, slice(size, size + half), jnp.concatenate([mixed, side], axis=1))
        store(at, slice(size + half, None), jnp.broadcast_to(jnp.concatenate([diagonal, diagonal], axis=1), (8, size)))

    @pl.loop(0, count - 1)
    def _(at):
        following = traces[at + 1]
        width = following.shape[1] // 2
        order = one_hot(paired(pair_ref[pl.ds(at, 1)]), width)
        face, inside = picked(split(following[:, :width]), order), picked(split(following[:, width:]), order)
        store(at, slice(0, size), coupled(traces[at], face, inside, faces_total))

    last_ref[...] = traces[count - 1]


def paired(row):
    return jnp.concatenate([jnp.full_like(row, -2 * row.shape[1] - 1), row], axis=1)


def coupled(own, face, inside, faces_total):
    width = own.shape[1] // 2
    outer, layer = own[:, :width], own[:, width:]
    near = split((penalty * outer + 0.5 * layer) * (-1.0 / faces_total))
    far = split(outer * (0.5 / faces_total))
    return dot3(near, split(face), NT) + dot3(far, split(inside), NT)


def last_kernel(faces_total, at_ref, pair_ref, own_ref, lead_ref, send_in, keep_in, send_ref, keep_ref, block, sem):
    width = own_ref.shape[1] // 2
    lead = split(lead_ref[...])
    order = paired(pair_ref[pl.ds(pair_ref.shape[0] - 1, 1)])
    face = picked(lead, one_hot(order, width))
    inside = picked(lead, one_hot(order, width, width // 2))
    block[...] = coupled(own_ref[...], face, inside, faces_total)
    at = send_ref.shape[0] - 1
    rows = pl.ds(0, block.shape[0])
    for core, ref in ((0, send_ref), (1, keep_ref)):

        @pl.when(at_ref[1] == core)
        def _():
            copy = pltpu.make_async_copy(block, ref.at[at, rows], sem)
            copy.start()
            copy.wait()


def packed(volume):
    half = volume.shape[0] // 2
    row = lax.broadcasted_iota(jnp.int32, (half, half), 0)
    column = lax.broadcasted_iota(jnp.int32, (half, half), 1)
    corner = volume[half:, half:]
    mixed = jnp.where(column >= row, volume[:half, :half], corner)
    diagonal = jnp.sum(jnp.where(column == row, corner, 0.0), axis=0, keepdims=True)
    return mixed, volume[:half, half:], diagonal


def unpacked(mixed, side, diagonal):
    half = mixed.shape[0]
    row = lax.broadcasted_iota(jnp.int32, (half, half), 0)
    column = lax.broadcasted_iota(jnp.int32, (half, half), 1)
    turned = mixed.T
    first = jnp.where(column >= row, mixed, turned)
    corner = jnp.where(column < row, mixed, jnp.where(column == row, diagonal, turned))
    top = jnp.concatenate([first, side], axis=1)
    return jnp.concatenate([top, jnp.concatenate([side.T, corner], axis=1)], axis=0)


def weights_kernel(aways, at_ref, *refs):
    sources, (high_ref, low_ref), held, sems = refs[: len(aways)], refs[-4:-2], refs[-2], refs[-1]
    size = held.shape[2]
    copies = [pltpu.make_async_copy(source.at[0], held.at[n], sems.at[n]) for n, source in enumerate(sources)]
    for copy in copies:
        copy.start()
    diagonal = diagonal_of(size)
    for n, away in enumerate(aways):
        copies[n].wait()
        element = away ^ at_ref[3]
        following = lax.rem(element + 1, high_ref.shape[0])
        volume, coupling = scaled(held[n], diagonal)
        for place, at, value in ((following, 0, coupling.T), (element, 1, volume), (element, 2, coupling)):
            high_ref[place, :, at * size : (at + 1) * size], low_ref[place, :, at * size : (at + 1) * size] = split(value)


def late_weights_kernel(aways, at_ref, *refs):
    count = len(aways)
    sources, targets = refs[:count], refs[count + 2 : count + 4]
    held, built, sems, out_sems = refs[count + 4 :]
    size = held.shape[2]
    copies = [pltpu.make_async_copy(source.at[0], held.at[n], sems.at[n]) for n, source in enumerate(sources)]
    for copy in copies:
        copy.start()
    diagonal = diagonal_of(size)
    stores = []
    for n, away in enumerate(aways):
        copies[n].wait()
        element = away ^ at_ref[3]
        following = lax.rem(element + 1, targets[0].shape[0])
        volume, coupling = scaled(held[n], diagonal)
        for at, value in enumerate((coupling.T, volume, coupling)):
            built[n, 0, :, at * size : (at + 1) * size], built[n, 1, :, at * size : (at + 1) * size] = split(value)
        for part, target in enumerate(targets):
            for at, (place, first, last) in enumerate(((following, 0, 1), (element, 1, 3))):
                columns = pl.ds(first * size, (last - first) * size)
                store = pltpu.make_async_copy(built.at[n, part, :, columns], target.at[place, :, columns], out_sems.at[n, part, at])
                store.start()
                stores.append(store)
    for store in stores:
        store.wait()


def diagonal_of(size):
    return lax.broadcasted_iota(jnp.int32, (size, size), 0) == lax.broadcasted_iota(jnp.int32, (size, size), 1)


def scaled(block, diagonal):
    size = block.shape[1]
    half = size // 2
    volume = unpacked(block[size : size + half, :half], block[size : size + half, half:], block[size + half : size + half + 1, :half])
    return (volume - jnp.where(diagonal, center, 0.0)) * (1.0 / half_width), block[:size] * (1.0 / half_width)


def outer_kernel(at_ref, kept_ref, swapped_ref, high_in, low_in, high_ref, low_ref):
    size = kept_ref.shape[2]
    rows = kept_ref.shape[1] - size
    row = lax.broadcasted_iota(jnp.int32, (size, size), 0)
    diagonal = row == lax.broadcasted_iota(jnp.int32, (size, size), 1)
    lower = at_ref[1] == 1
    below = jnp.where(lower, kept_ref[0], swapped_ref[0])
    volume, coupling = scaled(below[:rows], diagonal)
    turned = coupling.T
    for at, value in enumerate(((below[rows:] * (1.0 / half_width)).T, volume, coupling)):
        high_ref[0, :, at * size : (at + 1) * size], low_ref[0, :, at * size : (at + 1) * size] = split(value)
    high_ref[1, :, :size], low_ref[1, :, :size] = split(turned)
    high_ref[1, :, size:] = high_in[0, :, size:]
    low_ref[1, :, size:] = low_in[0, :, size:]
    volume, coupling = scaled(jnp.where(lower, swapped_ref[0, :rows], kept_ref[0, :rows]), diagonal)
    last = high_in.shape[0] - 1
    turned = (high_in[last, :, 2 * size :].astype(jnp.float32) + low_in[last, :, 2 * size :].astype(jnp.float32)).T
    for at, value in enumerate((turned, volume, coupling)):
        high_ref[2, :, at * size : (at + 1) * size], low_ref[2, :, at * size : (at + 1) * size] = split(value)


def held_shape(rows, columns):
    return (rows, 2 * columns) if columns % 128 == 0 else (2, rows, columns)


def hold(held, at, value):
    high, low = split(value)
    size, columns = value.shape
    rows = slice(at * size, (at + 1) * size)
    if len(held.shape) == 2:
        held[rows, :columns] = high
        held[rows, columns:] = low
    else:
        held[0, rows] = high
        held[1, rows] = low


def apply_row(high, low, held, start, columns):
    rows = pl.ds(start, high.shape[1])
    if len(held.shape) == 2:
        if columns == 128:
            both = dot(high, held[rows, :])
            total = both[:, :columns] + both[:, columns:]
        else:
            total = dot(high, held[rows, :columns]) + dot(high, held[rows, columns:])
        return total + dot(low, held[rows, :columns])
    return dot(high, held[0, rows]) + (dot(high, held[1, rows]) + dot(low, held[0, rows]))


def hold_all(held, values):
    for at, value in enumerate(values):
        hold(held, at, value)


def first_kernel(high, low, y0, above, y1, held):
    count, size, columns = y0.shape
    hold_all(held, [y0[at] for at in range(count)] + [above[0]])

    @pl.loop(0, count - 1, unroll=7)
    def _(at):
        y1[at] = apply_row(high[at + 1], low[at + 1], held, pl.multiple_of(at * size, size), columns)


def second_kernel(chunks, high, low, outer_high, outer_low, y0, below, above, y1, y1_ends, *refs):
    outs, held = refs[:-1], refs[-1]
    count, size, columns = y0.shape
    row = lambda weight, start: apply_row(*weight, held, start * size, columns)
    outer = lambda at: (outer_high[at], outer_low[at])
    main = lambda at: (high[at], low[at])
    hold_all(held, (below[0], below[1], y0[0], y0[1], y0[count - 1], above[0], above[1]))
    y1_ends[0] = row(outer(0), 0)
    y1_ends[1] = row(outer(1), 1)
    y1_ends[2] = row(outer(2), 4)
    hold_all(held, (y1_ends[0], y1_ends[1], y1[0], y1[1], y1[count - 4], y1[count - 3], y1[count - 2], y1_ends[2]))
    width = columns // chunks
    for out_at, at, weight, start, element in (
        (0, 0, outer(1), 0, 0),
        (0, 1, main(1), 1, 1),
        (1, 0, main(count - 2), 4, count - 2),
        (1, 1, main(count - 1), 5, count - 1),
    ):
        value = 2.0 * row(weight, start) - y0[element]
        for chunk in range(chunks):
            outs[out_at * chunks + chunk][at] = value[:, chunk * width : (chunk + 1) * width]


def middle_kernel(chunks, at_ref, high, low, y0, y1, *refs):
    ends, (y3_kept, y4, send, held, y2, y3) = refs[: 2 * chunks], refs[2 * chunks :]
    count, size, columns = y0.shape
    row = lambda place, at: apply_row(high[place], low[place], held, pl.multiple_of(at * size, size), columns)
    hold_all(held, [y1[at] for at in range(count - 2)])

    @pl.loop(0, count - 4, unroll=4)
    def _(at):
        y2[at] = 2.0 * row(at + 2, at) - y0[at + 2]

    joined = lambda group, at: jnp.concatenate([end[at] for end in ends[group * chunks : (group + 1) * chunks]], axis=1)
    hold_all(held, [joined(0, 0), joined(0, 1)] + [y2[at] for at in range(count - 4)] + [joined(1, 0), joined(1, 1)])

    @pl.loop(0, count - 2, unroll=6)
    def _(at):
        y3[at] = 2.0 * row(at + 1, at) - y1[at]

    hold_all(held, [y3[at] for at in range(count - 2)])

    @pl.loop(0, count - 4, unroll=4)
    def _(at):
        y4[at] = 2.0 * row(at + 2, at) - y2[at]

    send[...] = y4[pl.ds((1 - at_ref[0]) * 2, 2)]
    for at, place in enumerate((0, 1, count - 4, count - 3)):
        y3_kept[at] = y3[place]


def last_rows_kernel(
    lane, foreign, at_ref, high, low, outer_high, outer_low, y1, y1_ends, y3, y2_low, y2_high, below, above, y4, held
):
    size, columns = y4.shape[1:]
    count = high.shape[0]
    lanes = slice(lane, lane + columns)
    row = lambda weight, start: apply_row(*weight, held, start * size, columns)
    outer = lambda at: (outer_high[at], outer_low[at])
    main = lambda at: (high[at], low[at])

    @pl.when((at_ref[0] == 0) == foreign)
    def _():
        hold_all(held, (y2_high[0], y2_high[1], above[0], above[1]))
        inside = 2.0 * row(main(count - 1), 0) - y1[count - 2, :, lanes]
        outside = 2.0 * row(outer(2), 1) - y1_ends[2, :, lanes]
        hold_all(held, (y3[2, :, lanes], y3[3, :, lanes], inside, outside))
        y4[0] = 2.0 * row(main(count - 2), 0) - y2_high[0]
        y4[1] = 2.0 * row(main(count - 1), 1) - y2_high[1]

    @pl.when((at_ref[0] == 0) != foreign)
    def _():
        hold_all(held, (below[0], below[1], y2_low[0], y2_low[1]))
        outside = 2.0 * row(outer(0), 0) - y1_ends[0, :, lanes]
        inside = 2.0 * row(outer(1), 1) - y1_ends[1, :, lanes]
        hold_all(held, (outside, inside, y3[0, :, lanes], y3[1, :, lanes]))
        y4[0] = 2.0 * row(outer(1), 0) - y2_low[0]
        y4[1] = 2.0 * row(main(1), 1) - y2_low[1]


def own_rows_kernel(chunks, at_ref, *refs):
    shared, groups, (y4, held) = refs[:7], refs[7:-2], refs[-2:]
    joined = [
        [jnp.concatenate([ref[at] for ref in groups[group * chunks : (group + 1) * chunks]], axis=1) for at in range(2)]
        for group in range(4)
    ]
    last_rows_kernel(0, False, at_ref, *shared, *joined, y4, held)


def fold_kernel(at_ref, keep_ref, other_ref, send_ref, stay_ref):
    lane = at_ref[2]
    half = keep_ref.shape[0] // 2
    for at in range(half):
        send_ref[at] = keep_ref[(1 - lane) * half + at] + other_ref[(1 - lane) * half + at]
        stay_ref[at] = keep_ref[lane * half + at] + other_ref[lane * half + at]


def outer_block_kernel(at_ref, mine_ref, beside_ref, out_ref, sems):
    rows, size = mine_ref.shape[1:]

    def moved(act):
        for wanted, outer, other in ((True, mine_ref, beside_ref), (False, beside_ref, mine_ref)):

            @pl.when((at_ref[1] == at_ref[2]) == wanted)
            def _():
                act(pltpu.make_async_copy(outer.at[0], out_ref.at[0, pl.ds(0, rows)], sems.at[0]))
                act(pltpu.make_async_copy(other.at[0, pl.ds(0, size)], out_ref.at[0, pl.ds(rows, size)], sems.at[1]))

    moved(lambda copy: copy.start())
    moved(lambda copy: copy.wait())


def sum_kernel(first_ref, second_ref, out_ref):
    out_ref[...] = first_ref[...] + second_ref[...]


def copy_pairs(side, pairs, sems):
    def moved(act):
        for at, (wanted, source, target) in enumerate(pairs):

            @pl.when(side == wanted)
            def _():
                act(pltpu.make_async_copy(source, target, sems.at[at]))

    moved(lambda copy: copy.start())
    moved(lambda copy: copy.wait())


def own_columns(vector_ref, half, element, width, count=2):
    if vector_ref.shape[2] == width:
        return vector_ref.at[pl.ds(element, count)]
    return vector_ref.at[pl.ds(element, count), :, pl.ds(pl.multiple_of(half * width, width), width)]


def chunk_of(ref, element, chunk, width):
    rows = pl.ds(element, 2)
    return ref.at[rows] if ref.shape[2] == width else ref.at[rows, :, pl.ds(chunk * width, width)]


def arrange_pair_kernel(element, wanted, at_ref, vector_ref, *refs):
    got_refs, (out_ref, sems) = refs[:-2], refs[-2:]
    pairs = [(wanted, own_columns(vector_ref, at_ref[0], element, out_ref.shape[2]), out_ref)]
    for chunk, got_ref in enumerate(got_refs):
        pairs.append((1 - wanted, got_ref, chunk_of(out_ref, 0, chunk, got_ref.shape[2])))
    copy_pairs(at_ref[0], pairs, sems)


def arrange_kernel(at_ref, vector_ref, *refs):
    got_refs, (out_ref, sems) = refs[:-2], refs[-2:]
    own = own_columns(vector_ref, at_ref[0], 0, out_ref.shape[2], 4)
    chunks = len(got_refs) // 2
    pairs = []
    for side in range(2):
        pairs.append((side, own, out_ref.at[pl.ds(4 * side, 4)]))
        for at, got_ref in enumerate(got_refs):
            element = 4 - 4 * side + 2 * (at // chunks)
            pairs.append((side, got_ref, chunk_of(out_ref, element, at % chunks, got_ref.shape[2])))
    copy_pairs(at_ref[0], pairs, sems)


def place_pairs(out_ref, sems, side, chunks, chunk, width, pairs):
    def moved(act):
        for at, (wanted, source, element, foreign) in enumerate(pairs):

            @pl.when(side == wanted)
            def _():
                part = 1 - side if foreign else side
                start = pl.multiple_of((part * chunks + chunk) * width, width)
                act(pltpu.make_async_copy(source, out_ref.at[pl.ds(element, 2), :, pl.ds(start, width)], sems.at[chunk, at]))

    return moved


def collect_kernel(at_ref, y4, own, near, out_ref, sems):
    pairs = (
        (0, own, 0, False),
        (1, own, 2, False),
        (0, y4.at[pl.ds(0, 2)], 2, False),
        (0, near, 2, True),
        (1, y4.at[pl.ds(2, 2)], 0, False),
        (1, near, 0, True),
    )
    act = place_pairs(out_ref, sems, at_ref[0], 1, 0, near.shape[2], pairs)
    act(lambda copy: copy.start())
    act(lambda copy: copy.wait())


def finish_kernel(chunks, at_ref, *refs):
    sources, out_ref, sems = refs[:chunks], refs[-2], refs[-1]
    acts = []
    for chunk in range(chunks):
        far = sources[chunk]
        pairs = ((0, far, 0, True), (1, far, 2, True))
        acts.append(place_pairs(out_ref, sems, at_ref[0], chunks, chunk, far.shape[2], pairs))
    for act in acts:
        act(lambda copy: copy.start())
    for act in acts:
        act(lambda copy: copy.wait())


def lead_and_cut(at, index, basis, vector, half, chunks):
    points, size = basis.shape[1:]
    return pl.pallas_call(
        lead_kernel,
        in_specs=[SCALARS, VMEM, ANY, ANY],
        out_specs=[VMEM] * (1 + 2 * chunks),
        out_shape=[near_core((size, 2 * index.shape[2]))] + [near_core((2, size, half // chunks))] * (2 * chunks),
        scratch_shapes=[pltpu.VMEM((points, size), jnp.float32), pltpu.SemaphoreType.DMA((1 + 2 * chunks,))],
        compiler_params=PARAMS,
    )(at, index, far_off(basis), far_off(vector))


def blocks(core, index, quad, pairs, basis, applied, faces_total):
    count, points, size = basis.shape
    spots = 4 * index.shape[2]
    part = near_core((count // 2, size + size // 2 + 8, size))
    return pl.pallas_call(
        functools.partial(blocks_kernel, faces_total),
        in_specs=[SCALARS, VMEM, VMEM, VMEM, ANY, ANY],
        out_specs=[VMEM] * 3,
        out_shape=[part, part, near_core((size, spots))],
        scratch_shapes=[
            pltpu.VMEM((count, points, size), jnp.float32),
            pltpu.VMEM((count, points, size), jnp.float32),
            pltpu.VMEM((count, size, spots), jnp.float32),
            pltpu.SemaphoreType.DMA((2 * count,)),
        ],
        compiler_params=PARAMS,
    )(core, index, quad, pairs, far_off(basis), far_off(applied))


def last_coupling(core, pair, own, lead, send, keep, faces_total):
    size = own.shape[0]
    return pl.pallas_call(
        functools.partial(last_kernel, faces_total),
        in_specs=[SCALARS, VMEM, VMEM, VMEM, ANY, ANY],
        out_specs=[ANY] * 2,
        out_shape=[near_core(send.shape)] * 2,
        input_output_aliases={4: 0, 5: 1},
        scratch_shapes=[pltpu.VMEM((size, size), jnp.float32), pltpu.SemaphoreType.DMA],
        compiler_params=PARAMS,
    )(core, pair, own, lead, send, keep)


def weights(at, pieces):
    aways = tuple(pieces)
    rows, size = pieces[aways[0]].shape[1:]
    return pl.pallas_call(
        functools.partial(weights_kernel, aways),
        in_specs=[SCALARS] + [ANY] * len(aways),
        out_specs=[VMEM] * 2,
        out_shape=[near_core((8, size, 3 * size), jnp.bfloat16)] * 2,
        scratch_shapes=[pltpu.VMEM((len(aways), rows, size), jnp.float32), pltpu.SemaphoreType.DMA((len(aways),))],
        compiler_params=PARAMS,
    )(at, *pieces.values())


def late_weights(at, pieces, high, low):
    aways = tuple(pieces)
    count = len(aways)
    rows, size = pieces[aways[0]].shape[1:]
    return pl.pallas_call(
        functools.partial(late_weights_kernel, aways),
        in_specs=[SCALARS] + [ANY] * (count + 2),
        out_specs=[ANY] * 2,
        out_shape=[near_core(high.shape, jnp.bfloat16)] * 2,
        input_output_aliases={1 + count: 0, 2 + count: 1},
        scratch_shapes=[
            pltpu.VMEM((count, rows, size), jnp.float32),
            pltpu.VMEM((count, 2, size, 3 * size), jnp.bfloat16),
            pltpu.SemaphoreType.DMA((count,)),
            pltpu.SemaphoreType.DMA((count, 2, 2)),
        ],
        compiler_params=PARAMS,
    )(at, *pieces.values(), high, low)


def outer_weights(at, kept, swapped, high, low):
    size = kept.shape[2]
    return pl.pallas_call(
        outer_kernel,
        in_specs=[SCALARS] + [VMEM] * 4,
        out_specs=[VMEM] * 2,
        out_shape=[near_core((3, size, 3 * size), jnp.bfloat16)] * 2,
        compiler_params=PARAMS,
    )(at, kept, swapped, high, low)


def first_rows(high, low, y0, above):
    count, size, columns = y0.shape
    return pl.pallas_call(
        first_kernel,
        in_specs=[VMEM] * 4,
        out_specs=VMEM,
        out_shape=near_core((count - 1, size, columns)),
        scratch_shapes=[pltpu.VMEM(held_shape((count + 1) * size, columns), jnp.bfloat16)],
        compiler_params=PARAMS,
    )(high, low, y0, above)


def second_rows(chunks, high, low, outer_high, outer_low, y0, below, above, y1):
    count, size, columns = y0.shape
    return pl.pallas_call(
        functools.partial(second_kernel, chunks),
        in_specs=[VMEM] * 8,
        out_specs=[VMEM] * (1 + 2 * chunks),
        out_shape=[near_core((3, size, columns))] + [near_core((2, size, columns // chunks))] * (2 * chunks),
        scratch_shapes=[pltpu.VMEM(held_shape(8 * size, columns), jnp.bfloat16)],
        compiler_params=PARAMS,
    )(high, low, outer_high, outer_low, y0, close_by(below), close_by(above), y1)


def middle_rows(at, chunks, high, low, y0, y1, ends):
    count, size, columns = y0.shape
    return pl.pallas_call(
        functools.partial(middle_kernel, chunks),
        in_specs=[SCALARS] + [VMEM] * (4 + 2 * chunks),
        out_specs=[VMEM] * 3,
        out_shape=[near_core((4, size, columns)), near_core((count - 4, size, columns)), near_core((2, size, columns))],
        scratch_shapes=[
            pltpu.VMEM(held_shape(count * size, columns), jnp.bfloat16),
            pltpu.VMEM((count - 4, size, columns), jnp.float32),
            pltpu.VMEM((count - 2, size, columns), jnp.float32),
        ],
        compiler_params=PARAMS,
    )(at, high, low, y0, y1, *ends)


def last_rows(at, lane, foreign, high, low, outer_high, outer_low, y1, y1_ends, y3, y2_low, y2_high, below, above):
    size, columns = below.shape[1:]
    return pl.pallas_call(
        functools.partial(last_rows_kernel, lane, foreign),
        in_specs=[SCALARS] + [VMEM] * 11,
        out_specs=VMEM,
        out_shape=near_core(below.shape),
        scratch_shapes=[pltpu.VMEM(held_shape(4 * size, columns), jnp.bfloat16)],
        compiler_params=PARAMS,
    )(at, high, low, outer_high, outer_low, y1, y1_ends, y3, y2_low, y2_high, close_by(below), close_by(above))


def own_rows(at, shared, groups):
    chunks = len(groups[0])
    _, size, width = groups[0][0].shape
    return pl.pallas_call(
        functools.partial(own_rows_kernel, chunks),
        in_specs=[SCALARS] + [VMEM] * (7 + 4 * chunks),
        out_specs=VMEM,
        out_shape=near_core((2, size, chunks * width)),
        scratch_shapes=[pltpu.VMEM(held_shape(4 * size, chunks * width), jnp.bfloat16)],
        compiler_params=PARAMS,
    )(at, *shared, *[value for group in groups for value in group])


def folded(lane, keep, other):
    shape = (keep.shape[0] // 2, *keep.shape[1:])
    return pl.pallas_call(
        fold_kernel,
        in_specs=[SCALARS, VMEM, VMEM],
        out_specs=[VMEM] * 2,
        out_shape=[near_core(shape)] * 2,
        compiler_params=PARAMS,
    )(lane, keep, close_by(other))


def outer_block(at, mine, beside):
    return pl.pallas_call(
        outer_block_kernel,
        in_specs=[SCALARS, ANY, ANY],
        out_specs=VMEM,
        out_shape=near_core((1, mine.shape[1] + mine.shape[2], mine.shape[2])),
        scratch_shapes=[pltpu.SemaphoreType.DMA((2,))],
        compiler_params=PARAMS,
    )(at, mine, beside)


def added(first, second):
    return pl.pallas_call(
        sum_kernel, in_specs=[VMEM] * 2, out_specs=VMEM, out_shape=near_core(first.shape), compiler_params=PARAMS
    )(first, close_by(second))


def arranged_pair(at, element, wanted, vector, got):
    _, size, width = got[0].shape
    return pl.pallas_call(
        functools.partial(arrange_pair_kernel, element, wanted),
        in_specs=[SCALARS] + [ANY] * (1 + len(got)),
        out_specs=VMEM,
        out_shape=near_core((2, size, width * len(got))),
        scratch_shapes=[pltpu.SemaphoreType.DMA((1 + len(got),))],
        compiler_params=PARAMS,
    )(at, far_off(vector), *got)


def arranged(at, vector, got):
    _, size, width = got[0].shape
    return pl.pallas_call(
        arrange_kernel,
        in_specs=[SCALARS] + [ANY] * (1 + len(got)),
        out_specs=VMEM,
        out_shape=near_core((8, size, width * len(got) // 2)),
        scratch_shapes=[pltpu.SemaphoreType.DMA((2 + 2 * len(got),))],
        compiler_params=PARAMS,
    )(at, far_off(vector), *got)


def collected(at, y4, own, near):
    _, size, columns = near.shape
    return pl.pallas_call(
        collect_kernel,
        in_specs=[SCALARS, ANY, ANY, ANY],
        out_specs=ANY,
        out_shape=jax.ShapeDtypeStruct((4, size, 2 * columns), jnp.float32),
        scratch_shapes=[pltpu.SemaphoreType.DMA((1, 6))],
        compiler_params=PARAMS,
    )(at, y4, own, near)


def finished(at, parts, result):
    chunks = len(parts)
    return pl.pallas_call(
        functools.partial(finish_kernel, chunks),
        in_specs=[SCALARS] + [ANY] * (chunks + 1),
        out_specs=ANY,
        out_shape=jax.ShapeDtypeStruct(result.shape, jnp.float32),
        input_output_aliases={1 + chunks: 0},
        scratch_shapes=[pltpu.SemaphoreType.DMA((chunks, 4))],
        compiler_params=PARAMS,
    )(at, *parts, result)


def flipped(value, axis, bit):
    count = lax.axis_size(axis)
    return lax.ppermute(value, axis, [(i, i ^ bit) for i in range(count)])


def shifted(value, axis, steps):
    count = lax.axis_size(axis)
    return lax.ppermute(value, axis, [(i, (i + steps) % count) for i in range(count)])


def body(basis, applied, quad, face_index, face_pairing, orbitals):
    count, points, size = basis.shape
    spots = face_index.shape[2]
    columns = orbitals.shape[1]
    chunks = 2 if columns % 512 == 0 else 1
    elems, width = lax.axis_size("elem"), lax.axis_size("pts")
    faces_total = float(spots * width)
    side = lax.axis_index("elem") % 2
    core = lax.axis_index("pts") % 2
    lane = lax.axis_index("pts") // 2 % 2
    vector = orbitals.reshape(count, size, columns)
    at = jnp.stack([side, core, lane, side * 4 + core * 2 + lane]).astype(jnp.int32)

    vector, at = lax.optimization_barrier((vector, at))
    wide = columns // 2
    part = wide // chunks
    own = foreign = vector
    if part % 128:
        own = lax.dynamic_slice_in_dim(vector, side * part, part, axis=2)
        foreign = lax.dynamic_slice_in_dim(vector, (1 - side) * part, part, axis=2)
    lead, *got = lead_and_cut(at, face_index, basis, foreign, wide, chunks)
    lead = shifted(lead, "elem", -1)
    got = [flipped(value, "elem", 1) for value in got]

    send, keep, last = blocks(at, face_index, quad, face_pairing, basis, applied, faces_total)
    send, keep = last_coupling(at, face_pairing, last, lead, send, keep, faces_total)
    got[0], send = lax.optimization_barrier((got[0], send))
    send, stay = folded(at, keep, flipped(send, "pts", 1))
    received = flipped(send, "pts", 2)
    pair_low = arranged_pair(at, 0, 0, own, got[:chunks])
    pair_low, received = lax.optimization_barrier((pair_low, received))
    mine = added(stay, received)
    bit = 4
    while bit < width:
        mine = mine + flipped(mine, "pts", bit)
        bit *= 2
    above = shifted(pair_low, "elem", -2)
    beside = flipped(mine, "pts", 2)
    across = flipped(mine, "elem", 1)
    above, beside, across, got[chunks] = lax.optimization_barrier((above, beside, across, got[chunks]))
    mine_near = flipped(mine, "pts", 1)
    both = flipped(across, "pts", 2)
    beside_near = flipped(beside, "pts", 1)
    across_near = flipped(across, "pts", 1)

    last = outer_block(at, mine, beside)
    flat = lambda e, p: e % elems * width + p
    holds = [(e, p) for e in range(elems) for p in range(width) if e % 2 == p % 2]
    outer = lax.ppermute(last, ("elem", "pts"), [(flat(e, p), flat(e + (2 if p % 2 else -2), p)) for e, p in holds])
    passed = lax.ppermute(outer, ("elem", "pts"), [(flat(e, p), flat(e ^ 1, p)) for e, p in holds])

    outer, got[-1] = lax.optimization_barrier((outer, got[-1]))
    below = shifted(arranged_pair(at, 2, 1, own, got[chunks:]), "elem", 2)
    y0 = arranged(at, own, got)
    both_near = flipped(both, "pts", 1)

    high, low = weights(at, {0: mine, 2: mine_near, 1: beside, 4: across, 3: beside_near, 6: across_near})
    high, low = late_weights(at, {5: both, 7: both_near}, high, low)

    y1 = first_rows(high, low, y0, above)
    below, y1, passed = lax.optimization_barrier((below, y1, passed))
    outer = added(outer, passed)
    high_outer, low_outer = outer_weights(at, outer, flipped(outer, "pts", 1), high, low)
    y1_ends, *ends = second_rows(chunks, high, low, high_outer, low_outer, y0, below, above, y1)
    belows = [shifted(value, "elem", 2) for value in ends[chunks:]]
    aboves = [shifted(value, "elem", -2) for value in ends[:chunks]]
    y3, y4, near = middle_rows(at, chunks, high, low, y0, y1, ends)
    near = flipped(near, "elem", 1)
    parts = []
    for c in range(chunks):
        given = (high, low, high_outer, low_outer, y1, y1_ends, y3, ends[c], ends[chunks + c], belows[c], aboves[c])
        far = flipped(last_rows(at, c * part, True, *given), "elem", 1)
        parts.append(far)
    shared = (high, low, high_outer, low_outer, y1, y1_ends, y3)
    ends_own = own_rows(at, shared, (ends[:chunks], ends[chunks:], belows, aboves))
    if part % 128:
        (far,) = parts
        mine = jnp.where(side == 0, jnp.concatenate([ends_own, y4[:2]]), jnp.concatenate([y4[2:], ends_own]))
        theirs = jnp.where(side == 0, jnp.concatenate([far, near]), jnp.concatenate([near, far]))
        swap = lambda first, second: jnp.concatenate([first, second], axis=2)
        result = jnp.where(side == 0, swap(mine, theirs), swap(theirs, mine))
    else:
        result = finished(at, parts, collected(at, y4, ends_own, near))
    return result.reshape(count * size, columns)


def solution(mesh):
    return jax.shard_map(
        body,
        mesh=mesh,
        in_specs=(
            P("elem", "pts", None),
            P("elem", "pts", None),
            P("elem", "pts"),
            P("elem", None, "pts"),
            P("elem", "pts"),
            P("elem", "pts"),
        ),
        out_specs=P("elem", "pts"),
        check_vma=False,
    )
```
